256 devices in a mesh: cx: 32 (over y, x, core), tp: 8 (over z).
Axes of the slice: x: 4, y: 4, z: 8, core: 2. Of those that a mesh axis runs over, the one named last changes fastest.
Arguments:
- layer_input: bfloat16 [4096, 3072], P('cx', 'tp'), may hold values from -40 to 40
- queries: bfloat16 [4096, 4096], P('cx', 'tp'), may hold values from -6 to 6
- keys: bfloat16 [4096, 4096], P('cx', 'tp'), may hold values from -6 to 6
- values: bfloat16 [4096, 4096], P('cx', 'tp'), may hold values from -6 to 6
- gate_input: bfloat16 [4096, 4096], P('cx', 'tp'), may hold values from -6 to 6
- log_decay: float32 [32, 4096], P('tp', 'cx'), may hold values from -1 to 0
- prior_state: float32 [32, 128, 128], P('tp'), may hold values from -192 to 192
- attn_gain: float32 [4096], P('tp'), may hold values from 0.5 to 1.5
- out_weight: bfloat16 [4096, 3072], P('tp'), may hold values from -0.09375 to 0.09375
- moe_gain: float32 [3072], replicated, may hold values from 0.5 to 1.5
- router: bfloat16 [3072, 16], replicated, may hold values from -0.109375 to 0.109375
- expert_ids: int32 [4096, 2], P('cx'), may hold values from 0 to 15, all different within a row; in each aligned block of 128 rows (0 to 127, 128 to 255, ...) at most 32 rows name the same one
- w_gate: bfloat16 [32, 3072, 3072], P('cx', None, 'tp'), may hold values from -0.109375 to 0.109375
- w_up: bfloat16 [32, 3072, 3072], P('cx', None, 'tp'), may hold values from -0.109375 to 0.109375
- w_down: bfloat16 [32, 3072, 3072], P('cx', 'tp'), may hold values from -0.078125 to 0.078125
Outputs:
- mixed: bfloat16 [4096, 3072], P('cx', 'tp')
The draws below stay inside these ranges and needn't reach their ends.
Inputs may be any that keep to these rules, and one draw needn't show every extreme that they name: `expert_ids`: each row names 2 different experts. Among the rows of one index of cx no expert is named by more than 32 rows, and in every draw some expert is named by exactly 32 of them.
All inputs are finite; a program needn't handle non-finite values.
Results may differ from the reference program's by a relative error of at most 0.0085.
Values may be sent and summed in bfloat16 or wider, within the bound.
No kernel may reach another device: no remote copies, remote signals or barrier semaphores. Data moves between devices by JAX's collectives and lax.ppermute only.
A program may use at most 128 MiB of HBM per device.

```python
import math
import jax
import jax.numpy as jnp
import numpy as np
from jax import lax

D = 3072
HEADS = 32
HEAD = 128
FF = 6144
TOPK = 2
TOK_DEV = 128
EXPERTS = 16
CAP = 32
SPAN_TOKENS = 4096


def draw_log_decay(key, part):
    key = jax.random.fold_in(key, 11)
    flow_lanes = jax.random.split(key, 7)
    fast_share = 0.5
    blocks = SPAN_TOKENS // TOK_DEV
    is_fast = jax.random.uniform(flow_lanes[0], (HEADS, 1)) < fast_share
    fast_rate = jax.random.uniform(flow_lanes[1], (HEADS, 1), minval=1.0 / 50.0, maxval=1.0 / 30.0)
    slow_rate = jax.random.uniform(flow_lanes[2], (HEADS, 1), minval=0.02, maxval=0.07) / SPAN_TOKENS
    rate = jnp.where(is_fast, fast_rate, slow_rate)
    block_factor = jnp.exp(jax.random.uniform(flow_lanes[3], (HEADS, blocks, 1), minval=-0.6931, maxval=0.6931))
    block_factor = jnp.broadcast_to(block_factor, (HEADS, blocks, TOK_DEV)).reshape(HEADS, SPAN_TOKENS)
    jitter = jax.random.uniform(flow_lanes[4], (HEADS, SPAN_TOKENS), minval=0.5, maxval=1.5)
    steady_portion = -rate * block_factor * jitter
    arrival_position = jax.random.randint(flow_lanes[5], (3,), 0, SPAN_TOKENS)
    match_count = (jnp.arange(SPAN_TOKENS)[None, :] == arrival_position[:, None]).astype(jnp.float32)
    kept_entries = jax.random.uniform(flow_lanes[6], (HEADS, 3), minval=0.5, maxval=0.8)
    arrival_groups = jnp.sum(jnp.log(kept_entries)[:, :, None] * match_count[None, :, :], axis=1)
    return steady_portion + arrival_groups


def draw_layer_input(key, part):
    key = jax.random.fold_in(key, 23)
    flow_lanes = jax.random.split(key, 4)
    spread = 0.6
    base = jnp.clip(jax.random.normal(flow_lanes[0], (SPAN_TOKENS, D)), -4.0, 4.0)
    row_scale = jnp.exp(jax.random.uniform(flow_lanes[2], (SPAN_TOKENS, 1), minval=-spread, maxval=spread))
    ramp = jnp.exp(1.0986 * (jnp.arange(D, dtype=jnp.float32)[None, :] / D - 0.5))
    column_scale = ramp * jnp.exp(jax.random.uniform(flow_lanes[3], (1, D), minval=-spread, maxval=spread))
    return (base * row_scale * column_scale).astype(jnp.bfloat16)


def block_scale(stream_key, dims, pieces, low, top_value):
    gain, own = 1.0, jax.random.fold_in(stream_key, 6)
    for dim, parts in pieces:
        heights = jnp.exp(jax.random.uniform(jax.random.fold_in(own, dim), (parts,), jnp.float32, low / len(pieces), top_value / len(pieces)))
        gain = gain * jnp.repeat(heights, dims[dim] // parts).reshape([-1 if axis == dim else 1 for axis in range(len(dims))])
    return gain


def deal_out(stream_key, own, number, rows, count, top, most, skew):
    sequence = jax.random.permutation(stream_key, count)
    packed, usual = shares(count, rows * top, most, skew, True), shares(count, rows * top, most, skew, False)
    places = jnp.arange(count)

    def named(sizes, turn):
        used = int((sizes > 0).sum())
        fixed = max(1, used // 4)
        passed = fixed + (places - fixed + turn * (used - fixed)) % max(1, count - fixed)
        return jnp.zeros((count,), jnp.int32).at[sequence[jnp.where(places < fixed, places, passed)]].set(jnp.asarray(sizes, jnp.int32))

    sizes = jnp.where(number % 4 == 0, named(packed, number // 4), named(usual, number - number // 4 - 1))
    mixed = jax.random.permutation(jax.random.fold_in(own, 3), count)
    giver, receiver = mixed[0:count // 2 * 2:2], mixed[1:count // 2 * 2:2]
    slack = jnp.minimum(sizes[giver] - 1, most - sizes[receiver]) // 2
    slack = jnp.where((giver == sequence[0]) | (receiver == sequence[0]) | (sizes[receiver] == 0), 0, jnp.maximum(slack, 0))
    passed = jax.random.randint(jax.random.fold_in(own, 4), (count // 2,), 0, 1 << 20) % (slack + 1)
    sizes = sizes.at[giver].add(-passed).at[receiver].add(passed)
    items = jnp.searchsorted(jnp.cumsum(sizes), jnp.arange(rows * top), side="right").astype(jnp.int32)
    table = items.reshape(top, rows).T
    table = table[jax.random.permutation(jax.random.fold_in(own, 1), rows)]
    turn = jax.random.randint(jax.random.fold_in(own, 2), (rows, 1), 0, top)
    return jnp.take_along_axis(table, (jnp.arange(top)[None, :] + turn) % top, axis=1)


def shares(number_of, total, limit, slope, full):
    portions = [(1 << 20) // math.isqrt(standing ** slope) + 1 for standing in range(1, number_of + 1)]
    largest = limit if full else min(limit, max(-(-total // number_of), total * portions[0] // sum(portions)))
    least = 1 if total - largest >= number_of - 1 else 0
    holding, spare = [largest] + [least] * (number_of - 1), total - largest - least * (number_of - 1)
    while spare > 0:
        free = [i for i in range(1, number_of) if holding[i] < largest] or [i for i in range(1, number_of) if holding[i] < limit]
        pool, budget = sum([portions[i] for i in free]), spare
        for i in free:
            extra = min(limit - holding[i], max(1, budget * portions[i] // pool), spare)
            holding[i] = holding[i] + extra
            spare = spare - extra
    return np.array(holding)


def gaussian(own_key, extent, deviation, reach, pieces=(), kind=jnp.bfloat16):
    factor_of = block_scale(own_key, extent, pieces, -0.22, 0.18) if pieces else 1.0
    entries = jax.random.normal(own_key, extent, jnp.float32) * deviation * factor_of
    return jnp.minimum(jnp.maximum(entries, -reach), reach).astype(kind)


def setup_inputs(seed: int = 0) -> dict:
    arg_keys = jax.random.split(jax.random.key(seed), 16)
    layer_input = draw_layer_input(jax.random.fold_in(arg_keys[15], 71), 0)
    queries = gaussian(arg_keys[1], (SPAN_TOKENS, HEADS * HEAD), 1.0, 6.0, ((0, 32), (1, 8)))
    keys = gaussian(arg_keys[2], (SPAN_TOKENS, HEADS * HEAD), 1.0, 6.0, ((0, 32), (1, 8)))
    values = gaussian(arg_keys[3], (SPAN_TOKENS, HEADS * HEAD), 1.0, 6.0, ((0, 32), (1, 8)))
    gate_input = gaussian(arg_keys[4], (SPAN_TOKENS, HEADS * HEAD), 1.0, 6.0, ((0, 32), (1, 8)))
    log_decay = draw_log_decay(jax.random.fold_in(arg_keys[15], 71), 0)
    prior_state = gaussian(arg_keys[6], (HEADS, HEAD, HEAD), 32.0, 192.0, ((0, 8),), jnp.float32)
    attn_gain = jnp.clip(1.0 + 0.1 * jax.random.normal(arg_keys[7], (HEADS * HEAD,), jnp.float32), 0.5, 1.5)
    out_weight = gaussian(arg_keys[8], (HEADS * HEAD, D), (HEADS * HEAD) ** -0.5, 0.09375, ((0, 8),))
    moe_gain = jnp.clip(1.0 + 0.1 * jax.random.normal(arg_keys[9], (D,), jnp.float32), 0.5, 1.5)
    router = gaussian(arg_keys[10], (D, EXPERTS), D ** -0.5, 0.109375)
    expert_ids_keys = jax.random.split(jax.random.fold_in(arg_keys[11], 1), SPAN_TOKENS // TOK_DEV)
    expert_ids_turns = jax.random.permutation(jax.random.fold_in(arg_keys[11], 3), SPAN_TOKENS // TOK_DEV)
    expert_ids = jax.vmap(lambda own, number: deal_out(jax.random.fold_in(arg_keys[11], 2), own, number, TOK_DEV, EXPERTS, TOPK, CAP, 2))(expert_ids_keys, expert_ids_turns).reshape((SPAN_TOKENS, TOPK))
    w_gate = gaussian(arg_keys[12], (2 * EXPERTS, D, FF // 2), D ** -0.5, 0.109375, ((0, 32), (2, 8)))
    w_up = gaussian(arg_keys[13], (2 * EXPERTS, D, FF // 2), D ** -0.5, 0.109375, ((0, 32), (2, 8)))
    w_down = gaussian(arg_keys[14], (2 * EXPERTS, FF // 2, D), FF ** -0.5, 0.078125, ((0, 32), (1, 8)))
    return {"layer_input": layer_input, "queries": queries, "keys": keys, "values": values, "gate_input": gate_input, "log_decay": log_decay, "prior_state": prior_state, "attn_gain": attn_gain, "out_weight": out_weight, "moe_gain": moe_gain, "router": router, "expert_ids": expert_ids, "w_gate": w_gate, "w_up": w_up, "w_down": w_down}


epsilon = 1e-06
highest_precision = lax.Precision.HIGHEST

def head_block(carried_state, inputs):
    query_tile, key_tile, value_tile, decay_block = inputs
    running_state = jnp.cumsum(decay_block, axis=1)
    length = running_state.shape[1]
    causal = (jnp.arange(length)[:, None] >= jnp.arange(length)[None, :])[None]
    spread = running_state[:, :, None] - running_state[:, None, :]
    weights = jnp.where(causal, jnp.exp(jnp.where(causal, spread, 0.0)), 0.0)
    scores = jnp.einsum('thk,shk->hts', query_tile, key_tile, precision=highest_precision) * weights
    inner = jnp.einsum('hts,shv->thv', scores, value_tile, precision=highest_precision)
    carried_contribution = jnp.exp(running_state).T[:, :, None] * jnp.einsum('rxg,xgd->rxd', query_tile, carried_state, precision=highest_precision)
    trailing_rows = jnp.exp(running_state[:, -1:] - running_state)
    state_update = jnp.einsum('gpc,gpw->pcw', key_tile * trailing_rows.T[:, :, None], value_tile, precision=highest_precision)
    renewed = jnp.exp(running_state[:, -1])[:, None, None] * carried_state + state_update
    return (renewed, inner + carried_contribution)

def reference(layer_input, queries, keys, values, gate_input, log_decay, prior_state, attn_gain, out_weight, moe_gain, router, expert_ids, w_gate, w_up, w_down):
    blocks = SPAN_TOKENS // TOK_DEV
    query_all = queries.astype(jnp.float32).reshape(blocks, TOK_DEV, HEADS, HEAD)
    key_all = keys.astype(jnp.float32).reshape(blocks, TOK_DEV, HEADS, HEAD)
    value_all = values.astype(jnp.float32).reshape(blocks, TOK_DEV, HEADS, HEAD)
    decay_all = log_decay.reshape(HEADS, blocks, TOK_DEV).transpose(1, 0, 2)
    ending, attended = lax.scan(head_block, prior_state, (query_all, key_all, value_all, decay_all))
    attended = attended.reshape(SPAN_TOKENS, HEADS, HEAD)
    squares = lax.optimization_barrier(jnp.mean(attended * attended, axis=-1, keepdims=True))
    gating = jax.nn.sigmoid(gate_input.astype(jnp.float32).reshape(SPAN_TOKENS, HEADS, HEAD))
    normed = attended * lax.rsqrt(squares + epsilon) * attn_gain.reshape(HEADS, HEAD) * gating
    normed = normed.astype(jnp.bfloat16).reshape(SPAN_TOKENS, HEADS * HEAD)
    hidden_state = layer_input.astype(jnp.float32) + jnp.dot(normed, out_weight, preferred_element_type=jnp.float32)
    row_mean = lax.optimization_barrier(jnp.mean(hidden_state * hidden_state, axis=-1, keepdims=True))
    expert_input = (hidden_state * lax.rsqrt(row_mean + epsilon) * moe_gain).astype(jnp.bfloat16)
    logits = jnp.dot(expert_input, router, preferred_element_type=jnp.float32)
    matched = expert_ids[:, :, None] == jnp.arange(EXPERTS, dtype=jnp.int32)[None, None, :]
    chosen = lax.optimization_barrier(jnp.sum(jnp.where(matched, logits[:, None, :], 0.0), axis=-1))
    margin = chosen[:, 0] - chosen[:, 1]
    mixing = jnp.stack([jax.nn.sigmoid(margin), jax.nn.sigmoid(-margin)], axis=1)
    onehot = matched.reshape(blocks, TOPK * TOK_DEV, EXPERTS).astype(jnp.int32)
    before = jnp.cumsum(onehot, axis=1) - onehot
    position = lax.optimization_barrier(jnp.sum(before * onehot, axis=2)).reshape(blocks, TOK_DEV, TOPK)
    at_slot = position[..., None] == jnp.arange(CAP, dtype=jnp.int32)
    chosen_ids = expert_ids.reshape(blocks, TOK_DEV, TOPK)
    mixing_blocks = mixing.reshape(blocks, TOK_DEV, TOPK)
    expert_float = expert_input.astype(jnp.float32).reshape(blocks, TOK_DEV, D)

    def one_expert(total, inputs):
        index, gate_pair, up_pair, down_pair = inputs
        picked = (chosen_ids == index)[..., None] & at_slot
        dispatch = lax.optimization_barrier(jnp.sum(picked, axis=2)).astype(jnp.float32)
        weighting = lax.optimization_barrier(jnp.sum(jnp.where(picked, mixing_blocks[..., None], 0.0), axis=2))
        routed = jnp.einsum('btc,btd->bcd', dispatch, expert_float, precision=highest_precision)
        routed = routed.astype(jnp.bfloat16).reshape(blocks * CAP, D)
        gate_full = jnp.concatenate([gate_pair[0], gate_pair[1]], axis=1)
        up_full = jnp.concatenate([up_pair[0], up_pair[1]], axis=1)
        down_full = jnp.concatenate([down_pair[0], down_pair[1]], axis=0)
        gated = jnp.dot(routed, gate_full, preferred_element_type=jnp.float32)
        lifted = jnp.dot(routed, up_full, preferred_element_type=jnp.float32)
        activated = (jax.nn.silu(gated) * lifted).astype(jnp.bfloat16)
        produced = jnp.dot(activated, down_full, preferred_element_type=jnp.float32).reshape(blocks, CAP, D)
        return (total + jnp.einsum('btc,bcd->btd', weighting, produced, precision=highest_precision), None)
    start_total = jnp.zeros((blocks, TOK_DEV, D), jnp.float32)
    expert_inputs = (jnp.arange(EXPERTS, dtype=jnp.int32), w_gate.reshape(EXPERTS, 2, D, FF // 2), w_up.reshape(EXPERTS, 2, D, FF // 2), w_down.reshape(EXPERTS, 2, FF // 2, D))
    moe_total, unused = lax.scan(one_expert, start_total, expert_inputs)
    return (hidden_state + moe_total.reshape(SPAN_TOKENS, D)).astype(jnp.bfloat16)
```

```python
import functools

import jax
import jax.numpy as jnp
from jax import lax
from jax.experimental import pallas as pl
from jax.experimental.pallas import tpu as pltpu
from jax.sharding import Mesh, PartitionSpec as P

epsilon = 1e-06
exact = lax.Precision.HIGHEST
bf16 = jnp.bfloat16
f32 = jnp.float32
MIB = 1 << 20


def mm(a, b, contract_a=1, contract_b=0, precision=None):
    return lax.dot_general(
        a, b, (((contract_a,), (contract_b,)), ((), ())),
        precision=precision, preferred_element_type=f32,
    )


def lower_triangle(n, strict=False):
    rows = lax.broadcasted_iota(jnp.int32, (n, n), 0)
    cols = lax.broadcasted_iota(jnp.int32, (n, n), 1)
    return (rows > cols) if strict else (rows >= cols)


def block_state_kernel(keys, values, log_decay, out):
    heads, positions = log_decay.shape
    size = keys.shape[1] // heads
    per_head = out.shape[1]
    rows = size // per_head
    until = mm(lower_triangle(positions).astype(f32), log_decay[...], 1, 1, exact)
    for h in range(heads):
        lanes = slice(h * size, (h + 1) * size)
        total = until[positions - 1:positions, h:h + 1]
        trailing = jnp.exp(total - until[:, h:h + 1])
        weighted = (keys[:, lanes].astype(f32) * trailing).astype(bf16)
        state = mm(weighted, values[:, lanes], 0, 0)
        out[h, :, :rows, :] = state.astype(bf16).reshape(per_head, rows, size)
        high = total.astype(bf16).astype(f32)
        middle = (total - high).astype(bf16).astype(f32)
        low = total - high - middle
        row = lax.broadcasted_iota(jnp.int32, (rows, size), 0)
        terms = jnp.where(row == 0, high, jnp.where(row == 1, middle, jnp.where(row == 2, low, 0.0)))
        out[h, :, rows:, :] = jnp.broadcast_to(terms.astype(bf16), (per_head, rows, size))


def state_scan_kernel(part, received, prior, out):
    blocks, rows, _ = out.shape
    state = prior[pl.ds(pl.multiple_of(part[0] * rows, rows), rows), :]
    for k in range(blocks):
        out[k] = state.astype(bf16)
        terms = received[k, rows:, :].astype(f32)
        total = terms[0:1] + terms[1:2] + terms[2:3]
        state = jnp.exp(total) * state + received[k, :rows, :].astype(f32)


def inner_kernel(queries, keys, values, log_decay, out, growth):
    heads, positions = log_decay.shape
    size = queries.shape[1] // heads
    causal = lower_triangle(positions)
    until = mm(causal.astype(f32), log_decay[...], 1, 1, exact)
    until_row = mm(log_decay[...], causal.astype(f32), 1, 1, exact)
    for h in range(heads):
        lanes = slice(h * size, (h + 1) * size)
        spread = until[:, h:h + 1] - until_row[h:h + 1, :]
        weights = jnp.where(causal, jnp.exp(jnp.where(causal, spread, 0.0)), 0.0)
        scores = mm(queries[:, lanes], keys[:, lanes], 1, 1) * weights
        out[:, lanes] = mm(scores.astype(bf16), values[:, lanes])
        growth[:, lanes] = jnp.broadcast_to(jnp.exp(until[:, h:h + 1]), (positions, size))


def project_kernel(queries, inner, growth, state, gate_input, gain, weight, out, normed, *, heads):
    size = queries.shape[1] // heads

    @pl.when(pl.program_id(0) == 0)
    def _():
        for h in range(heads):
            lanes = slice(h * size, (h + 1) * size)
            carried = mm(queries[:, lanes], state[lanes, :])
            attended = inner[:, lanes] + growth[:, lanes] * carried
            squares = jnp.mean(attended * attended, axis=1, keepdims=True)
            gating = jax.nn.sigmoid(gate_input[:, lanes].astype(f32))
            rows = attended * lax.rsqrt(squares + epsilon) * gain[:, lanes] * gating
            normed[:, lanes] = rows.astype(bf16)

    product = mm(normed[...], weight[...])
    for c in range(out.shape[0]):
        width = out.shape[2]
        out[c] = product[:, c * width:(c + 1) * width].astype(bf16)


def slots_of(ids, experts, capacity):
    positions = ids.shape[0]
    expert = lax.broadcasted_iota(jnp.int32, (positions, experts), 1)
    first = (ids[:, 0:1] == expert).astype(f32)
    second = (ids[:, 1:2] == expert).astype(f32)
    earlier = mm(lower_triangle(positions, True).astype(bf16), (first + second).astype(bf16))
    places = []
    for choice in (first, second):
        position = jnp.sum(choice * earlier, axis=1, keepdims=True).astype(jnp.int32)
        number = jnp.sum(choice * expert.astype(f32), axis=1, keepdims=True).astype(jnp.int32)
        places.append(number * capacity + position)
    return first, second, places


def dispatch_kernel(index, partial, layer_input, gain, router, ids, outgoing, hidden, sums, *, experts, capacity):
    del index
    positions, width = layer_input.shape
    total = layer_input[...].astype(f32)
    for k in range(partial.shape[0]):
        total += partial[k].astype(f32)
    hidden[...] = total
    scaled = (total * gain[0]).astype(bf16)
    logits = mm(scaled, router[...])
    squares = jnp.sum(total * total, axis=1, keepdims=True)
    sums[...] = jnp.concatenate(
        [logits, jnp.broadcast_to(squares, (positions, sums.shape[1] - experts))], axis=1
    )
    _, _, places = slots_of(ids[...], experts, capacity)
    slot = lax.broadcasted_iota(jnp.int32, (positions, experts * capacity), 1)
    chosen = ((slot == places[0]) | (slot == places[1])).astype(bf16)
    outgoing[...] = mm(chosen, scaled, 0, 0).astype(bf16)


def expert_kernel(rows, inverse, gate_up_hbm_gate, gate_up_hbm_up, down_hbm, out, gate_up, down, sems, *, width):
    chunks, _, share = rows.shape

    @pl.when(pl.program_id(0) == 0)
    def _():
        copies = [
            pltpu.make_async_copy(gate_up_hbm_gate, gate_up.at[:, pl.ds(0, share)], sems.at[0]),
            pltpu.make_async_copy(gate_up_hbm_up, gate_up.at[:, pl.ds(share, share)], sems.at[1]),
            pltpu.make_async_copy(down_hbm, down, sems.at[2]),
        ]
        for copy in copies:
            copy.start()
        for copy in copies:
            copy.wait()

    squares = jnp.zeros((rows.shape[1], 1), f32)
    total = jnp.zeros((rows.shape[1], 2 * share), f32)
    for c in range(0, chunks, 2):
        pair = jnp.concatenate([rows[c], rows[c + 1]], axis=1)
        lanes = slice(c * share, (c + 2) * share)
        wide = pair.astype(f32) * inverse[:, lanes]
        squares += jnp.sum(wide * wide, axis=1, keepdims=True)
        total += mm(pair, gate_up[lanes, :])
    total *= lax.rsqrt(squares / width + epsilon)
    gated = total[:, :share]
    activated = (gated * jax.nn.sigmoid(gated) * total[:, share:]).astype(bf16)
    for c in range(0, chunks, 2):
        product = mm(activated, down[:, c * share:(c + 2) * share])
        out[c] = product[:, :share].astype(bf16)
        out[c + 1] = product[:, share:].astype(bf16)


def combine_kernel(returned, hidden, sums, ids, out, *, experts, capacity, width):
    positions = hidden.shape[0]
    first, second, places = slots_of(ids[...], experts, capacity)
    scale = lax.rsqrt(sums[:, experts:experts + 1] / width + epsilon)
    logits = sums[:, :experts] * scale
    margin = jnp.sum((first - second) * logits, axis=1, keepdims=True)
    slot = lax.broadcasted_iota(jnp.int32, (positions, experts * capacity), 1)
    total = hidden[...]
    for place, mixing in zip(places, (jax.nn.sigmoid(margin), jax.nn.sigmoid(-margin))):
        total += mixing * mm((slot == place).astype(bf16), returned[...])
    out[...] = total.astype(out.dtype)


def call(kernel, shapes, *args, limit=48, **kwargs):
    return pl.pallas_call(
        kernel,
        out_shape=shapes,
        compiler_params=pltpu.CompilerParams(vmem_limit_bytes=limit * MIB),
        **kwargs,
    )(*args)


def whole(shape):
    return pl.BlockSpec(shape, lambda *_: (0,) * len(shape))


def shards(
    layer_input, queries, keys, values, gate_input, log_decay, prior_state, attn_gain,
    out_weight, moe_gain, router, expert_ids, w_gate, w_up, w_down,
):
    struct = jax.ShapeDtypeStruct
    positions, head_lanes = queries.shape
    heads, size, _ = prior_state.shape
    chips, cores, peers = lax.axis_size("chip"), lax.axis_size("core"), lax.axis_size("tp")
    blocks = chips * cores
    width = out_weight.shape[1]
    share = layer_input.shape[1]
    experts = router.shape[1]
    capacity = 8 * positions // blocks
    slots = experts * capacity
    core = lax.axis_index("core")
    cx = lax.axis_index("chip") * cores + core
    tp = lax.axis_index("tp")

    rows = heads * size // blocks
    parts = call(block_state_kernel, struct((heads, size // rows, 2 * rows, size), bf16), keys, values, log_decay)
    received = lax.all_to_all(parts.reshape(blocks, 2 * rows, size), ("chip", "core"), 0, 0, tiled=True)
    inner, growth = call(
        inner_kernel,
        (struct((positions, head_lanes), f32), struct((positions, head_lanes), f32)),
        queries, keys, values, log_decay,
    )
    befores = call(
        state_scan_kernel, struct((blocks, rows, size), bf16),
        cx.reshape(1), received, prior_state.reshape(heads * size, size),
        in_specs=[pl.BlockSpec(memory_space=pltpu.SMEM)] + [pl.BlockSpec(memory_space=pltpu.VMEM)] * 2,
    )
    state = lax.all_to_all(befores, ("chip", "core"), 0, 0, tiled=True).reshape(heads * size, size)

    steps = 4
    each = peers // steps
    partial = call(
        functools.partial(project_kernel, heads=heads),
        struct((peers, positions, share), bf16),
        queries, inner, growth, state, gate_input, attn_gain.reshape(1, head_lanes), out_weight,
        grid=(steps,),
        in_specs=[whole((positions, head_lanes))] * 3
        + [whole((heads * size, size)), whole((positions, head_lanes)), whole((1, head_lanes))]
        + [pl.BlockSpec((head_lanes, each * share), lambda i: (0, i))],
        out_specs=pl.BlockSpec((each, positions, share), lambda i: (i, 0, 0)),
        scratch_shapes=[pltpu.VMEM((positions, head_lanes), bf16)],
    )
    partial = lax.all_to_all(partial, "tp", 0, 0, tiled=True)
    outgoing, hidden, sums = pl.pallas_call(
        functools.partial(dispatch_kernel, experts=experts, capacity=capacity),
        out_shape=(struct((slots, share), bf16), struct((positions, share), f32), struct((positions, 128), f32)),
        grid_spec=pltpu.PrefetchScalarGridSpec(
            num_scalar_prefetch=1,
            grid=(1,),
            in_specs=[
                whole((peers, positions, share)),
                whole((positions, share)),
                pl.BlockSpec((1, 1, share), lambda i, index: (index[0], 0, 0)),
                pl.BlockSpec((share, experts), lambda i, index: (index[0], 0)),
                whole((positions, 2)),
            ],
            out_specs=[whole((slots, share)), whole((positions, share)), whole((positions, 128))],
        ),
        compiler_params=pltpu.CompilerParams(vmem_limit_bytes=48 * MIB),
    )(tp.reshape(1), partial, layer_input, moe_gain.reshape(peers, 1, share), router, expert_ids)

    arrived = lax.all_to_all(outgoing.reshape(chips, capacity, share), "chip", 0, 0, tiled=True)
    gathered = lax.all_gather(arrived.reshape(chips * capacity, share), ("core", "tp"))
    sums = lax.psum(sums, "tp")
    held = chips * capacity
    rows_step = 256
    per_half = held // rows_step
    produced = call(
        functools.partial(expert_kernel, width=width),
        struct((cores * peers, held, share), bf16),
        gathered.reshape(cores * peers, held, share), (1.0 / moe_gain).reshape(1, width),
        w_gate[0], w_up[0], w_down[0],
        grid=(cores * per_half,),
        in_specs=[
            pl.BlockSpec((peers, rows_step, share), lambda i: (i // per_half, i % per_half, 0)),
            whole((1, width)),
        ] + [pl.BlockSpec(memory_space=pl.ANY)] * 3,
        out_specs=pl.BlockSpec((peers, rows_step, share), lambda i: (i // per_half, i % per_half, 0)),
        scratch_shapes=[
            pltpu.VMEM((width, 2 * share), bf16),
            pltpu.VMEM((share, width), bf16),
            pltpu.SemaphoreType.DMA((3,)),
        ],
    ).reshape(cores, peers, held, share)

    other = lax.dynamic_index_in_dim(produced, 1 - core, 0, False)
    own = lax.dynamic_index_in_dim(produced, core, 0, False)
    other = lax.ppermute(other, "core", [(0, 1), (1, 0)])
    both = (own.astype(f32) + other.astype(f32)).astype(bf16)
    summed = lax.psum_scatter(both.reshape(peers * held, share), "tp", scatter_dimension=0, tiled=True)
    returned = lax.all_to_all(summed.reshape(chips, capacity, share), "chip", 0, 0, tiled=True)
    return call(
        functools.partial(combine_kernel, experts=experts, capacity=capacity, width=width),
        struct((positions, share), bf16),
        returned.reshape(slots, share), hidden, sums, expert_ids,
    )


def solution(mesh):
    cx, tp = mesh.devices.shape
    fine = Mesh(mesh.devices.reshape(cx // 2, 2, tp), ("chip", "core", "tp"))
    both = ("chip", "core")
    placed = (
        P(both, "tp"), P(both, "tp"), P(both, "tp"), P(both, "tp"), P(both, "tp"),
        P("tp", both), P("tp", None, None), P("tp"), P("tp", None), P(), P(),
        P(both, None), P(both, None, "tp"), P(both, None, "tp"), P(both, "tp", None),
    )
    return jax.shard_map(shards, mesh=fine, in_specs=placed, out_specs=P(both, "tp"), check_vma=False)
```

```python
import functools

import jax
import jax.numpy as jnp
from jax import lax
from jax.experimental import pallas as pl
from jax.experimental.pallas import tpu as pltpu
from jax.sharding import Mesh, PartitionSpec as P

epsilon = 1e-06
exact = lax.Precision.HIGHEST
bf16 = jnp.bfloat16
f32 = jnp.float32
LIMIT = 60 << 20


def mm(a, b, contract_a=1, contract_b=0, precision=None):
    return lax.dot_general(
        a, b, (((contract_a,), (contract_b,)), ((), ())),
        precision=precision, preferred_element_type=f32,
    )


def lower_triangle(n, strict=False):
    rows = lax.broadcasted_iota(jnp.int32, (n, n), 0)
    cols = lax.broadcasted_iota(jnp.int32, (n, n), 1)
    return (rows > cols) if strict else (rows >= cols)


def block_state_kernel(keys, values, log_decay, out):
    heads, positions = log_decay.shape
    size = keys.shape[1] // heads
    per_head = out.shape[1]
    rows = size // per_head
    until = mm(lower_triangle(positions).astype(f32), log_decay[...], 1, 1, exact)
    for h in range(heads):
        lanes = slice(h * size, (h + 1) * size)
        total = until[positions - 1:positions, h:h + 1]
        trailing = jnp.exp(total - until[:, h:h + 1])
        weighted = (keys[:, lanes].astype(f32) * trailing).astype(bf16)
        state = mm(weighted, values[:, lanes], 0, 0)
        out[h, :, :rows, :] = state.astype(bf16).reshape(per_head, rows, size)
        high = total.astype(bf16).astype(f32)
        middle = (total - high).astype(bf16).astype(f32)
        low = total - high - middle
        row = lax.broadcasted_iota(jnp.int32, (rows, size), 0)
        terms = jnp.where(row == 0, high, jnp.where(row == 1, middle, jnp.where(row == 2, low, 0.0)))
        out[h, :, rows:, :] = jnp.broadcast_to(terms.astype(bf16), (per_head, rows, size))


def state_scan_kernel(part, received, prior, out):
    blocks, rows, _ = out.shape
    state = prior[pl.ds(pl.multiple_of(part[0] * rows, rows), rows), :]
    for k in range(blocks):
        out[k] = state.astype(bf16)
        terms = received[k, rows:, :].astype(f32)
        total = terms[0:1] + terms[1:2] + terms[2:3]
        state = jnp.exp(total) * state + received[k, :rows, :].astype(f32)


def inner_kernel(queries, keys, values, log_decay, out, growth):
    heads, positions = log_decay.shape
    size = queries.shape[1] // heads
    causal = lower_triangle(positions)
    until = mm(causal.astype(f32), log_decay[...], 1, 1, exact)
    until_row = mm(log_decay[...], causal.astype(f32), 1, 1, exact)
    for h in range(heads):
        lanes = slice(h * size, (h + 1) * size)
        spread = until[:, h:h + 1] - until_row[h:h + 1, :]
        weights = jnp.where(causal, jnp.exp(jnp.where(causal, spread, 0.0)), 0.0)
        scores = mm(queries[:, lanes], keys[:, lanes], 1, 1) * weights
        out[:, lanes] = mm(scores.astype(bf16), values[:, lanes])
        growth[:, lanes] = jnp.broadcast_to(jnp.exp(until[:, h:h + 1]), (positions, size))


def project_kernel(queries, inner, growth, state, gate_input, gain, weight, out, normed, *, heads):
    size = queries.shape[1] // heads

    @pl.when(pl.program_id(0) == 0)
    def _():
        for h in range(heads):
            lanes = slice(h * size, (h + 1) * size)
            carried = mm(queries[:, lanes], state[lanes, :])
            attended = inner[:, lanes] + growth[:, lanes] * carried
            squares = jnp.mean(attended * attended, axis=1, keepdims=True)
            gating = jax.nn.sigmoid(gate_input[:, lanes].astype(f32))
            rows = attended * lax.rsqrt(squares + epsilon) * gain[:, lanes] * gating
            normed[:, lanes] = rows.astype(bf16)

    product = mm(normed[...], weight[...])
    for c in range(out.shape[0]):
        width = out.shape[2]
        out[c] = product[:, c * width:(c + 1) * width].astype(bf16)


def slots_of(ids, experts, capacity):
    positions = ids.shape[0]
    expert = lax.broadcasted_iota(jnp.int32, (positions, experts), 1)
    first = (ids[:, 0:1] == expert).astype(f32)
    second = (ids[:, 1:2] == expert).astype(f32)
    earlier = mm(lower_triangle(positions, True).astype(bf16), (first + second).astype(bf16))
    places = []
    for choice in (first, second):
        position = jnp.sum(choice * earlier, axis=1, keepdims=True).astype(jnp.int32)
        number = jnp.sum(choice * expert.astype(f32), axis=1, keepdims=True).astype(jnp.int32)
        places.append(number * capacity + position)
    return first, second, places


def dispatch_kernel(index, partial, layer_input, gain, router, ids, outgoing, hidden, sums, *, experts, capacity):
    del index
    positions, width = layer_input.shape
    total = layer_input[...].astype(f32)
    for k in range(partial.shape[0]):
        total += partial[k].astype(f32)
    hidden[...] = total
    scaled = (total * gain[0]).astype(bf16)
    logits = mm(scaled, router[...])
    squares = jnp.sum(total * total, axis=1, keepdims=True)
    sums[...] = jnp.concatenate(
        [logits, jnp.broadcast_to(squares, (positions, sums.shape[1] - experts))], axis=1
    )
    _, _, places = slots_of(ids[...], experts, capacity)
    slot = lax.broadcasted_iota(jnp.int32, (positions, experts * capacity), 1)
    chosen = ((slot == places[0]) | (slot == places[1])).astype(bf16)
    outgoing[...] = mm(chosen, scaled, 0, 0).astype(bf16)


def expert_kernel(core, rows, inverse, gate_hbm, up_hbm, down_hbm, other, own, gate_up, down, sems, *, width, per_half):
    del core
    chunks, _, share = rows.shape
    step = pl.program_id(0)
    copies = [
        pltpu.make_async_copy(gate_hbm, gate_up.at[:, pl.ds(0, share)], sems.at[0]),
        pltpu.make_async_copy(up_hbm, gate_up.at[:, pl.ds(share, share)], sems.at[1]),
        pltpu.make_async_copy(down_hbm, down, sems.at[2]),
    ]

    @pl.when(step == 0)
    def _():
        for copy in copies:
            copy.start()
        copies[0].wait()
        copies[1].wait()

    squares = jnp.zeros((rows.shape[1], 1), f32)
    total = jnp.zeros((rows.shape[1], 2 * share), f32)
    for c in range(0, chunks, 2):
        pair = jnp.concatenate([rows[c], rows[c + 1]], axis=1)
        lanes = slice(c * share, (c + 2) * share)
        wide = pair.astype(f32) * inverse[:, lanes]
        squares += jnp.sum(wide * wide, axis=1, keepdims=True)
        total += mm(pair, gate_up[lanes, :])
    total *= lax.rsqrt(squares / width + epsilon)
    gated = total[:, :share]
    activated = (gated * jax.nn.sigmoid(gated) * total[:, share:]).astype(bf16)

    @pl.when(step == 0)
    def _():
        copies[2].wait()

    def produce(out):
        for c in range(0, chunks, 2):
            product = mm(activated, down[:, c * share:(c + 2) * share])
            out[c] = product[:, :share].astype(bf16)
            out[c + 1] = product[:, share:].astype(bf16)

    pl.when(step < per_half)(lambda: produce(other))
    pl.when(step >= per_half)(lambda: produce(own))


def add_kernel(a, b, out):
    out[...] = (a[...].astype(f32) + b[...].astype(f32)).astype(bf16)


def combine_kernel(returned, hidden, sums, ids, out, *, experts, capacity, width):
    positions = hidden.shape[0]
    first, second, places = slots_of(ids[...], experts, capacity)
    scale = lax.rsqrt(sums[:, experts:experts + 1] / width + epsilon)
    logits = sums[:, :experts] * scale
    margin = jnp.sum((first - second) * logits, axis=1, keepdims=True)
    slot = lax.broadcasted_iota(jnp.int32, (positions, experts * capacity), 1)
    total = hidden[...]
    for place, mixing in zip(places, (jax.nn.sigmoid(margin), jax.nn.sigmoid(-margin))):
        total += mixing * mm((slot == place).astype(bf16), returned[...])
    out[...] = total.astype(out.dtype)


def call(kernel, shapes, *args, **kwargs):
    return pl.pallas_call(
        kernel,
        out_shape=shapes,
        compiler_params=pltpu.CompilerParams(vmem_limit_bytes=LIMIT),
        **kwargs,
    )(*args)


def whole(shape):
    return pl.BlockSpec(shape, lambda *_: (0,) * len(shape))


def shards(
    layer_input, queries, keys, values, gate_input, log_decay, prior_state, attn_gain,
    out_weight, moe_gain, router, expert_ids, w_gate, w_up, w_down,
):
    struct = jax.ShapeDtypeStruct
    positions, head_lanes = queries.shape
    heads, size, _ = prior_state.shape
    chips, cores, peers = lax.axis_size("chip"), lax.axis_size("core"), lax.axis_size("tp")
    blocks = chips * cores
    width = out_weight.shape[1]
    share = layer_input.shape[1]
    experts = router.shape[1]
    capacity = 8 * positions // blocks
    slots = experts * capacity
    core = lax.axis_index("core")
    cx = lax.axis_index("chip") * cores + core
    tp = lax.axis_index("tp")

    rows = heads * size // blocks
    parts = call(block_state_kernel, struct((heads, size // rows, 2 * rows, size), bf16), keys, values, log_decay)
    received = lax.all_to_all(parts.reshape(blocks, 2 * rows, size), ("chip", "core"), 0, 0, tiled=True)
    inner, growth = call(
        inner_kernel,
        (struct((positions, head_lanes), f32), struct((positions, head_lanes), f32)),
        queries, keys, values, log_decay,
    )
    befores = call(
        state_scan_kernel, struct((blocks, rows, size), bf16),
        cx.reshape(1), received, prior_state.reshape(heads * size, size),
        in_specs=[pl.BlockSpec(memory_space=pltpu.SMEM)] + [pl.BlockSpec(memory_space=pltpu.VMEM)] * 2,
    )
    state = lax.all_to_all(befores, ("chip", "core"), 0, 0, tiled=True).reshape(heads * size, size)

    steps = 4
    each = peers // steps
    partial = call(
        functools.partial(project_kernel, heads=heads),
        struct((peers, positions, share), bf16),
        queries, inner, growth, state, gate_input, attn_gain.reshape(1, head_lanes), out_weight,
        grid=(steps,),
        in_specs=[whole((positions, head_lanes))] * 3
        + [whole((heads * size, size)), whole((positions, head_lanes)), whole((1, head_lanes))]
        + [pl.BlockSpec((head_lanes, each * share), lambda i: (0, i))],
        out_specs=pl.BlockSpec((each, positions, share), lambda i: (i, 0, 0)),
        scratch_shapes=[pltpu.VMEM((positions, head_lanes), bf16)],
    )
    partial = lax.all_to_all(partial, "tp", 0, 0, tiled=True)
    outgoing, hidden, sums = pl.pallas_call(
        functools.partial(dispatch_kernel, experts=experts, capacity=capacity),
        out_shape=(struct((slots, share), bf16), struct((positions, share), f32), struct((positions, 128), f32)),
        grid_spec=pltpu.PrefetchScalarGridSpec(
            num_scalar_prefetch=1,
            grid=(1,),
            in_specs=[
                whole((peers, positions, share)),
                whole((positions, share)),
                pl.BlockSpec((1, 1, share), lambda i, index: (index[0], 0, 0)),
                pl.BlockSpec((share, experts), lambda i, index: (index[0], 0)),
                whole((positions, 2)),
            ],
            out_specs=[whole((slots, share)), whole((positions, share)), whole((positions, 128))],
        ),
        compiler_params=pltpu.CompilerParams(vmem_limit_bytes=LIMIT),
    )(tp.reshape(1), partial, layer_input, moe_gain.reshape(peers, 1, share), router, expert_ids)

    arrived = lax.all_to_all(outgoing.reshape(chips, capacity, share), "chip", 0, 0, tiled=True)
    gathered = lax.all_gather(arrived.reshape(chips * capacity, share), ("core", "tp"))
    for distance in (1, 2, 4):
        sums += lax.ppermute(sums, "tp", [(i, i ^ distance) for i in range(peers)])
    held = chips * capacity
    rows_step = 256
    per_half = held // rows_step
    block = (peers, rows_step, share)
    other, own = pl.pallas_call(
        functools.partial(expert_kernel, width=width, per_half=per_half),
        out_shape=(struct((peers, held, share), bf16),) * 2,
        grid_spec=pltpu.PrefetchScalarGridSpec(
            num_scalar_prefetch=1,
            grid=(cores * per_half,),
            in_specs=[
                pl.BlockSpec(block, lambda i, core: (jnp.where(i < per_half, 1 - core[0], core[0]), i % per_half, 0)),
                whole((1, width)),
            ] + [pl.BlockSpec(memory_space=pl.ANY)] * 3,
            out_specs=[
                pl.BlockSpec(block, lambda i, core: (0, jnp.minimum(i, per_half - 1), 0)),
                pl.BlockSpec(block, lambda i, core: (0, jnp.maximum(i - per_half, 0), 0)),
            ],
            scratch_shapes=[
                pltpu.VMEM((width, 2 * share), bf16),
                pltpu.VMEM((share, width), bf16),
                pltpu.SemaphoreType.DMA((3,)),
            ],
        ),
        compiler_params=pltpu.CompilerParams(vmem_limit_bytes=LIMIT),
    )(
        core.reshape(1), gathered.reshape(cores * peers, held, share), (1.0 / moe_gain).reshape(1, width),
        w_gate[0], w_up[0], w_down[0],
    )

    other = lax.ppermute(other, "core", [(0, 1), (1, 0)])
    part = pl.BlockSpec((1, held, share), lambda i: (i, 0, 0))
    both = call(
        add_kernel, struct((peers, held, share), bf16), own, other,
        grid=(peers,), in_specs=[part, part], out_specs=part,
    )
    summed = lax.psum_scatter(both.reshape(peers * held, share), "tp", scatter_dimension=0, tiled=True)
    returned = lax.all_to_all(summed.reshape(chips, capacity, share), "chip", 0, 0, tiled=True)
    return call(
        functools.partial(combine_kernel, experts=experts, capacity=capacity, width=width),
        struct((positions, share), bf16),
        returned.reshape(slots, share), hidden, sums, expert_ids,
    )


def solution(mesh):
    cx, tp = mesh.devices.shape
    fine = Mesh(mesh.devices.reshape(cx // 2, 2, tp), ("chip", "core", "tp"))
    both = ("chip", "core")
    placed = (
        P(both, "tp"), P(both, "tp"), P(both, "tp"), P(both, "tp"), P(both, "tp"),
        P("tp", both), P("tp", None, None), P("tp"), P("tp", None), P(), P(),
        P(both, None), P(both, None, "tp"), P(both, None, "tp"), P(both, "tp", None),
    )
    return jax.shard_map(shards, mesh=fine, in_specs=placed, out_specs=P(both, "tp"), check_vma=False)
```

```python
import functools

import jax
import jax.numpy as jnp
from jax import lax
from jax.experimental import pallas as pl
from jax.experimental.pallas import tpu as pltpu
from jax.sharding import Mesh, PartitionSpec as P

epsilon = 1e-06
exact = lax.Precision.HIGHEST
bf16 = jnp.bfloat16
f32 = jnp.float32
LIMIT = 60 << 20


def mm(a, b, contract_a=1, contract_b=0, precision=None):
    return lax.dot_general(
        a, b, (((contract_a,), (contract_b,)), ((), ())),
        precision=precision, preferred_element_type=f32,
    )


def lower_triangle(n, strict=False):
    rows = lax.broadcasted_iota(jnp.int32, (n, n), 0)
    cols = lax.broadcasted_iota(jnp.int32, (n, n), 1)
    return (rows > cols) if strict else (rows >= cols)


def block_state_kernel(keys, values, log_decay, out):
    heads, positions = log_decay.shape
    size = keys.shape[1] // heads
    per_head = out.shape[1]
    rows = size // per_head
    until = mm(lower_triangle(positions).astype(f32), log_decay[...], 1, 1, exact)
    for h in range(heads):
        lanes = slice(h * size, (h + 1) * size)
        total = until[positions - 1:positions, h:h + 1]
        trailing = jnp.exp(total - until[:, h:h + 1])
        weighted = (keys[:, lanes].astype(f32) * trailing).astype(bf16)
        state = mm(weighted, values[:, lanes], 0, 0)
        out[h, :, :rows, :] = state.astype(bf16).reshape(per_head, rows, size)
        high = total.astype(bf16).astype(f32)
        middle = (total - high).astype(bf16).astype(f32)
        low = total - high - middle
        row = lax.broadcasted_iota(jnp.int32, (rows, size), 0)
        terms = jnp.where(row == 0, high, jnp.where(row == 1, middle, jnp.where(row == 2, low, 0.0)))
        out[h, :, rows:, :] = jnp.broadcast_to(terms.astype(bf16), (per_head, rows, size))


def state_scan_kernel(part, received, prior, out):
    blocks, rows, _ = out.shape
    state = prior[pl.ds(pl.multiple_of(part[0] * rows, rows), rows), :]
    for k in range(blocks):
        out[k] = state.astype(bf16)
        terms = received[k, rows:, :].astype(f32)
        total = terms[0:1] + terms[1:2] + terms[2:3]
        state = jnp.exp(total) * state + received[k, :rows, :].astype(f32)


def inner_kernel(queries, keys, values, log_decay, out, growth):
    heads, positions = log_decay.shape
    size = queries.shape[1] // heads
    causal = lower_triangle(positions)
    until = mm(causal.astype(f32), log_decay[...], 1, 1, exact)
    until_row = mm(log_decay[...], causal.astype(f32), 1, 1, exact)
    for h in range(heads):
        lanes = slice(h * size, (h + 1) * size)
        spread = until[:, h:h + 1] - until_row[h:h + 1, :]
        weights = jnp.where(causal, jnp.exp(jnp.where(causal, spread, 0.0)), 0.0)
        scores = mm(queries[:, lanes], keys[:, lanes], 1, 1) * weights
        out[:, lanes] = mm(scores.astype(bf16), values[:, lanes])
        growth[:, lanes] = jnp.broadcast_to(jnp.exp(until[:, h:h + 1]), (positions, size))


def project_kernel(queries, inner, growth, state, gate_input, gain, weight, out, normed, *, heads):
    size = queries.shape[1] // heads

    @pl.when(pl.program_id(0) == 0)
    def _():
        for h in range(heads):
            lanes = slice(h * size, (h + 1) * size)
            carried = mm(queries[:, lanes], state[lanes, :])
            attended = inner[:, lanes] + growth[:, lanes] * carried
            squares = jnp.mean(attended * attended, axis=1, keepdims=True)
            gating = jax.nn.sigmoid(gate_input[:, lanes].astype(f32))
            rows = attended * lax.rsqrt(squares + epsilon) * gain[:, lanes] * gating
            normed[:, lanes] = rows.astype(bf16)

    product = mm(normed[...], weight[...])
    for c in range(out.shape[0]):
        width = out.shape[2]
        out[c] = product[:, c * width:(c + 1) * width].astype(bf16)


def slots_of(ids, experts, capacity):
    positions = ids.shape[0]
    expert = lax.broadcasted_iota(jnp.int32, (positions, experts), 1)
    first = (ids[:, 0:1] == expert).astype(f32)
    second = (ids[:, 1:2] == expert).astype(f32)
    earlier = mm(lower_triangle(positions, True).astype(bf16), (first + second).astype(bf16))
    places = []
    for choice in (first, second):
        position = jnp.sum(choice * earlier, axis=1, keepdims=True).astype(jnp.int32)
        number = jnp.sum(choice * expert.astype(f32), axis=1, keepdims=True).astype(jnp.int32)
        places.append(number * capacity + position)
    return first, second, places


def dispatch_kernel(index, partial, layer_input, gain, router, ids, outgoing, hidden, sums, *, experts, capacity):
    del index
    positions, width = layer_input.shape
    total = layer_input[...].astype(f32)
    for k in range(partial.shape[0]):
        total += partial[k].astype(f32)
    hidden[...] = total
    scaled = (total * gain[0]).astype(bf16)
    logits = mm(scaled, router[...])
    squares = jnp.sum(total * total, axis=1, keepdims=True)
    sums[...] = jnp.concatenate(
        [logits, jnp.broadcast_to(squares, (positions, sums.shape[1] - experts))], axis=1
    )
    _, _, places = slots_of(ids[...], experts, capacity)
    slot = lax.broadcasted_iota(jnp.int32, (positions, experts * capacity), 1)
    chosen = ((slot == places[0]) | (slot == places[1])).astype(bf16)
    outgoing[...] = mm(chosen, scaled, 0, 0).astype(bf16)


def fetch(pairs, sems):
    copies = [pltpu.make_async_copy(source, target, sems.at[k]) for k, (source, target) in enumerate(pairs)]
    for copy in copies:
        copy.start()
    return copies


def column_pairs(tp, hbm, scratch, distances, peers):
    share = hbm.shape[1] // peers
    pairs = []
    for k, distance in enumerate(distances):
        start = pl.multiple_of(lax.rem(tp + distance + peers, peers) * share, share)
        pairs.append((hbm.at[:, pl.ds(start, share)], scratch.at[:, pl.ds(k * share, share)]))
    return pairs


def activate(rows, inverse, gate_up, width):
    chunks, _, share = rows.shape
    squares = jnp.zeros((rows.shape[1], 1), f32)
    total = jnp.zeros((rows.shape[1], 2 * share), f32)
    for c in range(0, chunks, 2):
        pair = jnp.concatenate([rows[c], rows[c + 1]], axis=1)
        lanes = slice(c * share, (c + 2) * share)
        wide = pair.astype(f32) * inverse[:, lanes]
        squares += jnp.sum(wide * wide, axis=1, keepdims=True)
        total += mm(pair, gate_up[lanes, :])
    total *= lax.rsqrt(squares / width + epsilon)
    gated = total[:, :share]
    return (gated * jax.nn.sigmoid(gated) * total[:, share:]).astype(bf16)


def products(activated, down, chunks):
    share = down.shape[1] // chunks
    found = []
    for c in range(0, chunks, 2):
        both = min(2, chunks - c)
        product = mm(activated, down[:, c * share:(c + both) * share])
        found += [product[:, k * share:(k + 1) * share] for k in range(both)]
    return found


def other_half_kernel(
    place, rows, inverse, gate_hbm, up_hbm, down_hbm, first, rest, gate_up, down, sems, *, width, distances
):
    chunks, _, share = rows.shape
    near = len(distances) - rest.shape[0]
    pairs = [(gate_hbm, gate_up.at[:, pl.ds(0, share)]), (up_hbm, gate_up.at[:, pl.ds(share, share)])]
    pairs += column_pairs(place[1], down_hbm, down, distances, chunks)

    @pl.when(pl.program_id(0) == 0)
    def _():
        copies = fetch(pairs, sems)
        for copy in copies:
            copy.wait()

    for k, product in enumerate(products(activate(rows, inverse, gate_up, width), down, chunks)):
        if k < near:
            first[k] = product.astype(bf16)
        else:
            rest[k - near] = product.astype(bf16)


def own_half_kernel(place, rows, inverse, gate_hbm, up_hbm, out, gate_up, sems, *, width):
    del place
    share = rows.shape[2]

    @pl.when(pl.program_id(0) == 0)
    def _():
        copies = fetch([(gate_hbm, gate_up.at[:, pl.ds(0, share)]), (up_hbm, gate_up.at[:, pl.ds(share, share)])], sems)
        for copy in copies:
            copy.wait()

    out[...] = activate(rows, inverse, gate_up, width)


def own_products_kernel(place, activated, sibling, down_hbm, *rest, distances, peers, split):
    outs, (down, sems) = rest[:-2], rest[-2:]
    copies = fetch(column_pairs(place[1], down_hbm, down, distances, peers), sems)
    for copy in copies:
        copy.wait()
    half = activated.shape[0] // 2
    for h in range(2):
        rows = slice(h * half, (h + 1) * half)
        for k, product in enumerate(products(activated[rows, :], down, len(distances))):
            total = (product + sibling[k, rows, :].astype(f32)).astype(bf16)
            if split:
                outs[2 * k + h][...] = total
            elif k < len(distances) - 1:
                outs[2 * k + h][...] = total
            else:
                outs[-1][rows, :] = total


def combine_kernel(returned, hidden, sums, ids, out, *, experts, capacity, width):
    positions = hidden.shape[0]
    first, second, places = slots_of(ids[...], experts, capacity)
    scale = lax.rsqrt(sums[:, experts:experts + 1] / width + epsilon)
    logits = sums[:, :experts] * scale
    margin = jnp.sum((first - second) * logits, axis=1, keepdims=True)
    slot = lax.broadcasted_iota(jnp.int32, (positions, experts * capacity), 1)
    total = hidden[...]
    for place, mixing in zip(places, (jax.nn.sigmoid(margin), jax.nn.sigmoid(-margin))):
        total += mixing * mm((slot == place).astype(bf16), returned[...])
    out[...] = total.astype(out.dtype)


def call(kernel, shapes, *args, **kwargs):
    return pl.pallas_call(
        kernel,
        out_shape=shapes,
        compiler_params=pltpu.CompilerParams(vmem_limit_bytes=LIMIT),
        **kwargs,
    )(*args)


def whole(shape):
    return pl.BlockSpec(shape, lambda *_: (0,) * len(shape))


def shards(
    layer_input, queries, keys, values, gate_input, log_decay, prior_state, attn_gain,
    out_weight, moe_gain, router, expert_ids, w_gate, w_up, w_down,
):
    struct = jax.ShapeDtypeStruct
    positions, head_lanes = queries.shape
    heads, size, _ = prior_state.shape
    chips, cores, peers = lax.axis_size("chip"), lax.axis_size("core"), lax.axis_size("tp")
    blocks = chips * cores
    width = out_weight.shape[1]
    share = layer_input.shape[1]
    experts = router.shape[1]
    capacity = 8 * positions // blocks
    slots = experts * capacity
    core = lax.axis_index("core")
    cx = lax.axis_index("chip") * cores + core
    tp = lax.axis_index("tp")

    rows = heads * size // blocks
    parts = call(block_state_kernel, struct((heads, size // rows, 2 * rows, size), bf16), keys, values, log_decay)
    received = lax.all_to_all(parts.reshape(blocks, 2 * rows, size), ("chip", "core"), 0, 0, tiled=True)
    inner, growth = call(
        inner_kernel,
        (struct((positions, head_lanes), f32), struct((positions, head_lanes), f32)),
        queries, keys, values, log_decay,
    )
    befores = call(
        state_scan_kernel, struct((blocks, rows, size), bf16),
        cx.reshape(1), received, prior_state.reshape(heads * size, size),
        in_specs=[pl.BlockSpec(memory_space=pltpu.SMEM)] + [pl.BlockSpec(memory_space=pltpu.VMEM)] * 2,
    )
    state = lax.all_to_all(befores, ("chip", "core"), 0, 0, tiled=True).reshape(heads * size, size)

    steps = 4
    each = peers // steps
    partial = call(
        functools.partial(project_kernel, heads=heads),
        struct((peers, positions, share), bf16),
        queries, inner, growth, state, gate_input, attn_gain.reshape(1, head_lanes), out_weight,
        grid=(steps,),
        in_specs=[whole((positions, head_lanes))] * 3
        + [whole((heads * size, size)), whole((positions, head_lanes)), whole((1, head_lanes))]
        + [pl.BlockSpec((head_lanes, each * share), lambda i: (0, i))],
        out_specs=pl.BlockSpec((each, positions, share), lambda i: (i, 0, 0)),
        scratch_shapes=[pltpu.VMEM((positions, head_lanes), bf16)],
    )
    partial = lax.all_to_all(partial, "tp", 0, 0, tiled=True)
    outgoing, hidden, sums = pl.pallas_call(
        functools.partial(dispatch_kernel, experts=experts, capacity=capacity),
        out_shape=(struct((slots, share), bf16), struct((positions, share), f32), struct((positions, 128), f32)),
        grid_spec=pltpu.PrefetchScalarGridSpec(
            num_scalar_prefetch=1,
            grid=(1,),
            in_specs=[
                whole((peers, positions, share)),
                whole((positions, share)),
                pl.BlockSpec((1, 1, share), lambda i, index: (index[0], 0, 0)),
                pl.BlockSpec((share, experts), lambda i, index: (index[0], 0)),
                whole((positions, 2)),
            ],
            out_specs=[whole((slots, share)), whole((positions, share)), whole((positions, 128))],
        ),
        compiler_params=pltpu.CompilerParams(vmem_limit_bytes=LIMIT),
    )(tp.reshape(1), partial, layer_input, moe_gain.reshape(peers, 1, share), router, expert_ids)

    arrived = lax.all_to_all(outgoing.reshape(chips, capacity, share), "chip", 0, 0, tiled=True)
    gathered = lax.all_gather(arrived.reshape(chips * capacity, share), ("core", "tp"))
    for distance in (1, 2, 4):
        sums += lax.ppermute(sums, "tp", [(i, i ^ distance) for i in range(peers)])
    gathered, sums = lax.optimization_barrier((gathered, sums))
    gathered = gathered.reshape(cores * peers, chips * capacity, share)
    held = chips * capacity
    rows_step = 256
    per_half = held // rows_step
    half = held // 2
    far, near = (4, 3, -3), (2, -2, 1, -1, 0)
    place = jnp.stack([core, tp])
    inverse = (1.0 / moe_gain).reshape(1, width)
    params = pltpu.CompilerParams(vmem_limit_bytes=LIMIT)
    hbm = pl.BlockSpec(memory_space=pl.ANY)
    gate, up, down = w_gate[0], w_up[0], w_down[0]
    work = 2 * held * width * share
    block = (peers, rows_step, share)

    first, rest = pl.pallas_call(
        functools.partial(other_half_kernel, width=width, distances=far + near),
        out_shape=(struct((len(far), held, share), bf16), struct((len(near), held, share), bf16)),
        grid_spec=pltpu.PrefetchScalarGridSpec(
            num_scalar_prefetch=1,
            grid=(per_half,),
            in_specs=[pl.BlockSpec(block, lambda i, place: (1 - place[0], i, 0)), whole((1, width)), hbm, hbm, hbm],
            out_specs=[
                pl.BlockSpec((len(far), rows_step, share), lambda i, place: (0, i, 0)),
                pl.BlockSpec((len(near), rows_step, share), lambda i, place: (0, i, 0)),
            ],
            scratch_shapes=[
                pltpu.VMEM((width, 2 * share), bf16),
                pltpu.VMEM((share, width), bf16),
                pltpu.SemaphoreType.DMA((2 + peers,)),
            ],
        ),
        compiler_params=params,
        cost_estimate=pl.CostEstimate(flops=3 * work, bytes_accessed=14 << 20, transcendentals=held * share),
    )(place, gathered, inverse, gate, up, down)
    swap = [(0, 1), (1, 0)]
    first = lax.ppermute(first, "core", swap)
    rest = lax.ppermute(rest, "core", swap)
    activated = pl.pallas_call(
        functools.partial(own_half_kernel, width=width),
        out_shape=struct((held, share), bf16),
        grid_spec=pltpu.PrefetchScalarGridSpec(
            num_scalar_prefetch=1,
            grid=(per_half,),
            in_specs=[pl.BlockSpec(block, lambda i, place: (place[0], i, 0)), whole((1, width)), hbm, hbm],
            out_specs=pl.BlockSpec((rows_step, share), lambda i, place: (i, 0)),
            scratch_shapes=[pltpu.VMEM((width, 2 * share), bf16), pltpu.SemaphoreType.DMA((2,))],
        ),
        compiler_params=params,
        cost_estimate=pl.CostEstimate(flops=2 * work, bytes_accessed=8 << 20, transcendentals=held * share),
    )(place, gathered, inverse, gate, up)

    def own_products(sibling, distances, split):
        n = len(distances)
        piece = struct((half, share), bf16)
        shapes = (piece,) * (2 * n) if split else (piece,) * (2 * n - 2) + (struct((held, share), bf16),)
        return pl.pallas_call(
            functools.partial(own_products_kernel, distances=distances, peers=peers, split=split),
            out_shape=shapes,
            grid_spec=pltpu.PrefetchScalarGridSpec(
                num_scalar_prefetch=1,
                grid=(1,),
                in_specs=[whole((held, share)), whole((n, held, share)), hbm],
                out_specs=[whole(s.shape) for s in shapes],
                scratch_shapes=[pltpu.VMEM((share, n * share), bf16), pltpu.SemaphoreType.DMA((n,))],
            ),
            compiler_params=pltpu.CompilerParams(vmem_limit_bytes=24 << 20),
            cost_estimate=pl.CostEstimate(flops=n * work // peers, bytes_accessed=3 * n * held * share * 2, transcendentals=0),
        )(place, activated, sibling, down)

    def moved(piece, step):
        return lax.ppermute(piece, "tp", [(i, (i + step) % peers) for i in range(peers)])

    def plus(*pieces):
        return sum(piece.astype(f32) for piece in pieces).astype(bf16)

    a4, b4, a3, b3, a3m, b3m = own_products(first, far, True)
    a_up, b_down = moved(a4, 1), moved(b4, -1)
    a_down, b_up = moved(a3m, -1), moved(b3, 1)
    a2, b2, a2m, b2m, a1, b1, a1m, b1m, mine = own_products(rest, near, False)
    a_up, b_down = moved(plus(a_up, a3), 1), moved(plus(b_down, b3m), -1)
    a_down, b_up = moved(plus(a_down, a2m), -1), moved(plus(b_up, b2), 1)
    a_up, b_down = moved(plus(a_up, a2), 1), moved(plus(b_down, b2m), -1)
    a_down, b_up = moved(plus(a_down, a1m), -1), moved(plus(b_up, b1), 1)
    a_up, b_down = moved(plus(a_up, a1), 1), moved(plus(b_down, b1m), -1)
    summed = jnp.concatenate([plus(mine[:half], a_up, a_down), plus(mine[half:], b_up, b_down)])
    returned = lax.all_to_all(summed.reshape(chips, capacity, share), "chip", 0, 0, tiled=True)
    return call(
        functools.partial(combine_kernel, experts=experts, capacity=capacity, width=width),
        struct((positions, share), bf16),
        returned.reshape(slots, share), hidden, sums, expert_ids,
    )


def solution(mesh):
    cx, tp = mesh.devices.shape
    fine = Mesh(mesh.devices.reshape(cx // 2, 2, tp), ("chip", "core", "tp"))
    both = ("chip", "core")
    placed = (
        P(both, "tp"), P(both, "tp"), P(both, "tp"), P(both, "tp"), P(both, "tp"),
        P("tp", both), P("tp", None, None), P("tp"), P("tp", None), P(), P(),
        P(both, None), P(both, None, "tp"), P(both, None, "tp"), P(both, "tp", None),
    )
    return jax.shard_map(shards, mesh=fine, in_specs=placed, out_specs=P(both, "tp"), check_vma=False)
```

```python
import functools

import jax
import jax.numpy as jnp
from jax import lax
from jax.experimental import pallas as pl
from jax.experimental.pallas import tpu as pltpu
from jax.sharding import Mesh, PartitionSpec as P

epsilon = 1e-06
exact = lax.Precision.HIGHEST
bf16 = jnp.bfloat16
f32 = jnp.float32
LIMIT = 30 << 20


def mm(a, b, contract_a=1, contract_b=0, precision=None):
    return lax.dot_general(
        a, b, (((contract_a,), (contract_b,)), ((), ())),
        precision=precision, preferred_element_type=f32,
    )


def lower_triangle(n, strict=False):
    rows = lax.broadcasted_iota(jnp.int32, (n, n), 0)
    cols = lax.broadcasted_iota(jnp.int32, (n, n), 1)
    return (rows > cols) if strict else (rows >= cols)


def block_state_kernel(keys, values, log_decay, out):
    heads, positions = log_decay.shape
    size = keys.shape[1] // heads
    per_head = out.shape[1]
    rows = size // per_head
    until = mm(lower_triangle(positions).astype(f32), log_decay[...], 1, 1, exact)
    for h in range(heads):
        lanes = slice(h * size, (h + 1) * size)
        total = until[positions - 1:positions, h:h + 1]
        trailing = jnp.exp(total - until[:, h:h + 1])
        weighted = (keys[:, lanes].astype(f32) * trailing).astype(bf16)
        state = mm(weighted, values[:, lanes], 0, 0)
        out[h, :, :rows, :] = state.astype(bf16).reshape(per_head, rows, size)
        high = total.astype(bf16).astype(f32)
        middle = (total - high).astype(bf16).astype(f32)
        low = total - high - middle
        row = lax.broadcasted_iota(jnp.int32, (rows, size), 0)
        terms = jnp.where(row == 0, high, jnp.where(row == 1, middle, jnp.where(row == 2, low, 0.0)))
        out[h, :, rows:, :] = jnp.broadcast_to(terms.astype(bf16), (per_head, rows, size))


def state_scan_kernel(part, received, prior, out):
    blocks, rows, _ = out.shape
    state = prior[pl.ds(pl.multiple_of(part[0] * rows, rows), rows), :]
    for k in range(blocks):
        out[k] = state.astype(bf16)
        terms = received[k, rows:, :].astype(f32)
        total = terms[0:1] + terms[1:2] + terms[2:3]
        state = jnp.exp(total) * state + received[k, :rows, :].astype(f32)


def inner_kernel(queries, keys, values, log_decay, out, growth):
    heads, positions = log_decay.shape
    size = queries.shape[1] // heads
    causal = lower_triangle(positions)
    until = mm(causal.astype(f32), log_decay[...], 1, 1, exact)
    until_row = mm(log_decay[...], causal.astype(f32), 1, 1, exact)
    for h in range(heads):
        lanes = slice(h * size, (h + 1) * size)
        spread = until[:, h:h + 1] - until_row[h:h + 1, :]
        weights = jnp.where(causal, jnp.exp(jnp.where(causal, spread, 0.0)), 0.0)
        scores = mm(queries[:, lanes], keys[:, lanes], 1, 1) * weights
        out[:, lanes] = mm(scores.astype(bf16), values[:, lanes])
        growth[:, lanes] = jnp.broadcast_to(jnp.exp(until[:, h:h + 1]), (positions, size))


def project_kernel(queries, inner, growth, state, gate_input, gain, weight, out, *, heads):
    size = queries.shape[1] // heads
    normed = []
    for h in range(heads):
        lanes = slice(h * size, (h + 1) * size)
        carried = mm(queries[:, lanes], state[lanes, :])
        attended = inner[:, lanes] + growth[:, lanes] * carried
        squares = jnp.mean(attended * attended, axis=1, keepdims=True)
        gating = jax.nn.sigmoid(gate_input[:, lanes].astype(f32))
        normed.append((attended * lax.rsqrt(squares + epsilon) * gain[:, lanes] * gating).astype(bf16))
    normed = jnp.concatenate(normed, axis=1)
    width = out.shape[2]
    for c in range(0, out.shape[0], 2):
        product = mm(normed, weight[:, c * width:(c + 2) * width])
        out[c] = product[:, :width].astype(bf16)
        out[c + 1] = product[:, width:].astype(bf16)


def slots_of(ids, experts, capacity):
    positions = ids.shape[0]
    expert = lax.broadcasted_iota(jnp.int32, (positions, experts), 1)
    first = (ids[:, 0:1] == expert).astype(f32)
    second = (ids[:, 1:2] == expert).astype(f32)
    earlier = mm(lower_triangle(positions, True).astype(bf16), (first + second).astype(bf16))
    places = []
    for choice in (first, second):
        position = jnp.sum(choice * earlier, axis=1, keepdims=True).astype(jnp.int32)
        number = jnp.sum(choice * expert.astype(f32), axis=1, keepdims=True).astype(jnp.int32)
        places.append(number * capacity + position)
    return first, second, places


def dispatch_kernel(index, partial, layer_input, gain, router, ids, outgoing, hidden, sums, *, experts, capacity):
    del index
    positions, width = layer_input.shape
    total = layer_input[...].astype(f32)
    for k in range(partial.shape[0]):
        total += partial[k].astype(f32)
    hidden[...] = total
    scaled = (total * gain[0]).astype(bf16)
    logits = mm(scaled, router[...])
    squares = jnp.sum(total * total, axis=1, keepdims=True)
    sums[...] = jnp.concatenate(
        [logits, jnp.broadcast_to(squares, (positions, sums.shape[1] - experts))], axis=1
    )
    _, _, places = slots_of(ids[...], experts, capacity)
    slot = lax.broadcasted_iota(jnp.int32, (positions, experts * capacity), 1)
    chosen = ((slot == places[0]) | (slot == places[1])).astype(bf16)
    outgoing[...] = mm(chosen, scaled, 0, 0).astype(bf16)


def fetch(pairs, sems):
    copies = [pltpu.make_async_copy(source, target, sems.at[k]) for k, (source, target) in enumerate(pairs)]
    for copy in copies:
        copy.start()
    return copies


def load_kernel(source, target, sems):
    parts = sems.shape[0]
    rows = source.shape[0] // parts
    pairs = [(source.at[pl.ds(k * rows, rows)], target.at[pl.ds(k * rows, rows)]) for k in range(parts)]
    for copy in fetch(pairs, sems):
        copy.wait()


def load_experts_kernel(place, gate_hbm, up_hbm, down_hbm, gate_up, down, sems, *, distances, peers):
    share = down_hbm.shape[1] // peers
    rows = gate_hbm.shape[0] // 4
    pairs = []
    for k in range(4):
        part = pl.ds(k * rows, rows)
        pairs.append((gate_hbm.at[part], gate_up.at[part, pl.ds(0, share)]))
        pairs.append((up_hbm.at[part], gate_up.at[part, pl.ds(share, share)]))
    for k, distance in enumerate(distances):
        start = pl.multiple_of(lax.rem(place[1] + distance + peers, peers) * share, share)
        pairs.append((down_hbm.at[:, pl.ds(start, share)], down.at[:, pl.ds(k * share, share)]))
    for copy in fetch(pairs, sems):
        copy.wait()


def activate(rows, inverse, gate_up, width):
    chunks, _, share = rows.shape
    squares = jnp.zeros((rows.shape[1], 1), f32)
    total = jnp.zeros((rows.shape[1], 2 * share), f32)
    for c in range(0, chunks, 2):
        pair = jnp.concatenate([rows[c], rows[c + 1]], axis=1)
        lanes = slice(c * share, (c + 2) * share)
        wide = pair.astype(f32) * inverse[:, lanes]
        squares += jnp.sum(wide * wide, axis=1, keepdims=True)
        total += mm(pair, gate_up[lanes, :])
    total *= lax.rsqrt(squares / width + epsilon)
    gated = total[:, :share]
    return (gated * jax.nn.sigmoid(gated) * total[:, share:]).astype(bf16)


def products(activated, down, chunks, share):
    found = []
    chunks = list(chunks)
    while chunks:
        both = min(2, len(chunks))
        product = mm(activated, down[:, chunks[0] * share:(chunks[0] + both) * share])
        found += [product[:, k * share:(k + 1) * share] for k in range(both)]
        chunks = chunks[both:]
    return found


def other_half_kernel(place, rows, inverse, gate_up, down, first, rest, *, width):
    del place
    chunks, _, share = rows.shape
    far = chunks - rest.shape[0]
    activated = activate(rows, inverse, gate_up, width)
    for k, product in enumerate(products(activated, down, range(chunks), share)):
        if k < far:
            first[k] = product.astype(bf16)
        else:
            rest[k - far] = product.astype(bf16)


def own_half_kernel(place, rows, inverse, gate_up, out, *, width):
    del place
    out[...] = activate(rows, inverse, gate_up, width)


def own_products_kernel(activated, sibling, down, *outs, start, split):
    count, _, share = sibling.shape
    half = activated.shape[0] // 2
    for h in range(2):
        rows = slice(h * half, (h + 1) * half)
        for k, product in enumerate(products(activated[rows, :], down, range(start, start + count), share)):
            total = (product + sibling[k, rows, :].astype(f32)).astype(bf16)
            if split or k < count - 1:
                outs[2 * k + h][...] = total
            else:
                outs[-1][rows, :] = total


def combine_kernel(returned, hidden, sums, ids, out, *, experts, capacity, width):
    positions = hidden.shape[0]
    first, second, places = slots_of(ids[...], experts, capacity)
    scale = lax.rsqrt(sums[:, experts:experts + 1] / width + epsilon)
    logits = sums[:, :experts] * scale
    margin = jnp.sum((first - second) * logits, axis=1, keepdims=True)
    slot = lax.broadcasted_iota(jnp.int32, (positions, experts * capacity), 1)
    total = hidden[...]
    for place, mixing in zip(places, (jax.nn.sigmoid(margin), jax.nn.sigmoid(-margin))):
        total += mixing * mm((slot == place).astype(bf16), returned[...])
    out[...] = total.astype(out.dtype)


def call(kernel, shapes, *args, **kwargs):
    return pl.pallas_call(
        kernel,
        out_shape=shapes,
        compiler_params=pltpu.CompilerParams(vmem_limit_bytes=LIMIT),
        **kwargs,
    )(*args)


def stays(x):
    return pltpu.with_memory_space_constraint(x, pltpu.HBM)


def in_vmem(x):
    return pltpu.with_memory_space_constraint(x, pltpu.VMEM)


def whole(shape):
    return pl.BlockSpec(shape, lambda *_: (0,) * len(shape))


def shards(
    layer_input, queries, keys, values, gate_input, log_decay, prior_state, attn_gain,
    out_weight, moe_gain, router, expert_ids, w_gate, w_up, w_down,
):
    struct = jax.ShapeDtypeStruct
    positions, head_lanes = queries.shape
    heads, size, _ = prior_state.shape
    chips, cores, peers = lax.axis_size("chip"), lax.axis_size("core"), lax.axis_size("tp")
    blocks = chips * cores
    width = out_weight.shape[1]
    share = layer_input.shape[1]
    experts = router.shape[1]
    capacity = 8 * positions // blocks
    slots = experts * capacity
    core = lax.axis_index("core")
    cx = lax.axis_index("chip") * cores + core
    tp = lax.axis_index("tp")

    queries, keys, values, log_decay = stays(queries), stays(keys), stays(values), stays(log_decay)
    vmem = pl.BlockSpec(memory_space=pltpu.VMEM)
    hbm = pl.BlockSpec(memory_space=pl.ANY)

    rows = heads * size // blocks
    parts = call(block_state_kernel, struct((heads, size // rows, 2 * rows, size), bf16), keys, values, log_decay)
    parts, out_weight = lax.optimization_barrier((parts, out_weight))
    out_weight = pl.pallas_call(
        load_kernel,
        out_shape=pltpu.VMEM((head_lanes, width), bf16),
        in_specs=[hbm],
        out_specs=vmem,
        scratch_shapes=[pltpu.SemaphoreType.DMA((4,))],
        compiler_params=pltpu.CompilerParams(vmem_limit_bytes=4 << 20),
        cost_estimate=pl.CostEstimate(flops=0, bytes_accessed=2 * head_lanes * width, transcendentals=0),
    )(stays(out_weight))
    received = lax.all_to_all(parts.reshape(blocks, 2 * rows, size), ("chip", "core"), 0, 0, tiled=True)
    inner, growth = call(
        inner_kernel,
        (struct((positions, head_lanes), f32), struct((positions, head_lanes), f32)),
        queries, keys, values, log_decay,
    )
    befores = call(
        state_scan_kernel, struct((blocks, rows, size), bf16),
        cx.reshape(1), received, stays(prior_state.reshape(heads * size, size)),
        in_specs=[pl.BlockSpec(memory_space=pltpu.SMEM)] + [pl.BlockSpec(memory_space=pltpu.VMEM)] * 2,
    )
    state = lax.all_to_all(befores, ("chip", "core"), 0, 0, tiled=True).reshape(heads * size, size)

    partial = call(
        functools.partial(project_kernel, heads=heads),
        struct((peers, positions, share), bf16),
        queries, inner, growth, state, stays(gate_input), stays(attn_gain.reshape(1, head_lanes)), in_vmem(out_weight),
        in_specs=[vmem] * 7,
    )
    partial = lax.all_to_all(partial, "tp", 0, 0, tiled=True)
    outgoing, hidden, sums = pl.pallas_call(
        functools.partial(dispatch_kernel, experts=experts, capacity=capacity),
        out_shape=(struct((slots, share), bf16), struct((positions, share), f32), struct((positions, 128), f32)),
        grid_spec=pltpu.PrefetchScalarGridSpec(
            num_scalar_prefetch=1,
            grid=(1,),
            in_specs=[
                whole((peers, positions, share)),
                whole((positions, share)),
                pl.BlockSpec((1, 1, share), lambda i, index: (index[0], 0, 0)),
                pl.BlockSpec((share, experts), lambda i, index: (index[0], 0)),
                whole((positions, 2)),
            ],
            out_specs=[whole((slots, share)), whole((positions, share)), whole((positions, 128))],
        ),
        compiler_params=pltpu.CompilerParams(vmem_limit_bytes=LIMIT),
    )(tp.reshape(1), partial, stays(layer_input), stays(moe_gain.reshape(peers, 1, share)), router, expert_ids)

    arrived = lax.all_to_all(outgoing.reshape(chips, capacity, share), "chip", 0, 0, tiled=True)
    arrived, gate, up, down = lax.optimization_barrier((arrived, w_gate[0], w_up[0], w_down[0]))
    gathered = lax.all_gather(arrived.reshape(chips * capacity, share), ("core", "tp"))
    far, near = (4, 3, -3), (2, -2, 1, -1, 0)
    place = jnp.stack([core, tp])
    gate_up, down = pl.pallas_call(
        functools.partial(load_experts_kernel, distances=far + near, peers=peers),
        out_shape=(pltpu.VMEM((width, 2 * share), bf16), pltpu.VMEM((share, width), bf16)),
        in_specs=[pl.BlockSpec(memory_space=pltpu.SMEM), hbm, hbm, hbm],
        out_specs=(vmem, vmem),
        scratch_shapes=[pltpu.SemaphoreType.DMA((8 + peers,))],
        compiler_params=pltpu.CompilerParams(vmem_limit_bytes=4 << 20),
        cost_estimate=pl.CostEstimate(flops=0, bytes_accessed=6 * width * share, transcendentals=0),
    )(place, stays(gate), stays(up), stays(down))
    gate_up, down = in_vmem(gate_up), in_vmem(down)
    for distance in (1, 2, 4):
        sums += lax.ppermute(sums, "tp", [(i, i ^ distance) for i in range(peers)])
    gathered, sums = lax.optimization_barrier((gathered, sums))
    gathered = stays(gathered.reshape(cores * peers, chips * capacity, share))
    held = chips * capacity
    rows_step = 256
    per_half = held // rows_step
    half = held // 2
    inverse = (1.0 / moe_gain).reshape(1, width)
    params = pltpu.CompilerParams(vmem_limit_bytes=LIMIT)
    work = 2 * held * width * share
    block = (peers, rows_step, share)

    first, rest = pl.pallas_call(
        functools.partial(other_half_kernel, width=width),
        out_shape=(struct((len(far), held, share), bf16), struct((len(near), held, share), bf16)),
        grid_spec=pltpu.PrefetchScalarGridSpec(
            num_scalar_prefetch=1,
            grid=(per_half,),
            in_specs=[pl.BlockSpec(block, lambda i, place: (1 - place[0], i, 0)), whole((1, width)), vmem, vmem],
            out_specs=[
                pl.BlockSpec((len(far), rows_step, share), lambda i, place: (0, i, 0)),
                pl.BlockSpec((len(near), rows_step, share), lambda i, place: (0, i, 0)),
            ],
        ),
        compiler_params=params,
        cost_estimate=pl.CostEstimate(flops=3 * work, bytes_accessed=7 << 20, transcendentals=held * share),
    )(place, gathered, inverse, gate_up, down)
    swap = [(0, 1), (1, 0)]
    first = lax.ppermute(first, "core", swap)
    rest = lax.ppermute(rest, "core", swap)
    activated = pl.pallas_call(
        functools.partial(own_half_kernel, width=width),
        out_shape=struct((held, share), bf16),
        grid_spec=pltpu.PrefetchScalarGridSpec(
            num_scalar_prefetch=1,
            grid=(per_half,),
            in_specs=[pl.BlockSpec(block, lambda i, place: (place[0], i, 0)), whole((1, width)), vmem],
            out_specs=pl.BlockSpec((rows_step, share), lambda i, place: (i, 0)),
        ),
        compiler_params=params,
        cost_estimate=pl.CostEstimate(flops=2 * work, bytes_accessed=4 << 20, transcendentals=held * share),
    )(place, gathered, inverse, gate_up)

    def own_products(sibling, start, split):
        n = sibling.shape[0]
        piece = struct((half, share), bf16)
        shapes = (piece,) * (2 * n) if split else (piece,) * (2 * n - 2) + (struct((held, share), bf16),)
        return pl.pallas_call(
            functools.partial(own_products_kernel, start=start, split=split),
            out_shape=shapes,
            in_specs=[vmem] * 3,
            compiler_params=params,
            cost_estimate=pl.CostEstimate(flops=n * work // peers, bytes_accessed=2 * n * held * share * 2, transcendentals=0),
        )(activated, sibling, down)

    def moved(piece, step):
        return lax.ppermute(piece, "tp", [(i, (i + step) % peers) for i in range(peers)])

    def plus(*pieces):
        return sum(piece.astype(f32) for piece in pieces).astype(bf16)

    a4, b4, a3, b3, a3m, b3m = own_products(first, 0, True)
    a_up, b_down = moved(a4, 1), moved(b4, -1)
    a_down, b_up = moved(a3m, -1), moved(b3, 1)
    a2, b2, a2m, b2m, a1, b1, a1m, b1m, mine = own_products(rest, len(far), False)
    a_up, b_down = moved(plus(a_up, a3), 1), moved(plus(b_down, b3m), -1)
    a_down, b_up = moved(plus(a_down, a2m), -1), moved(plus(b_up, b2), 1)
    a_up, b_down = moved(plus(a_up, a2), 1), moved(plus(b_down, b2m), -1)
    a_down, b_up = moved(plus(a_down, a1m), -1), moved(plus(b_up, b1), 1)
    a_up, b_down = moved(plus(a_up, a1), 1), moved(plus(b_down, b1m), -1)
    summed = jnp.concatenate([plus(mine[:half], a_up, a_down), plus(mine[half:], b_up, b_down)])
    returned = lax.all_to_all(summed.reshape(chips, capacity, share), "chip", 0, 0, tiled=True)
    return call(
        functools.partial(combine_kernel, experts=experts, capacity=capacity, width=width),
        struct((positions, share), bf16),
        returned.reshape(slots, share), hidden, sums, expert_ids,
    )


def solution(mesh):
    cx, tp = mesh.devices.shape
    fine = Mesh(mesh.devices.reshape(cx // 2, 2, tp), ("chip", "core", "tp"))
    both = ("chip", "core")
    placed = (
        P(both, "tp"), P(both, "tp"), P(both, "tp"), P(both, "tp"), P(both, "tp"),
        P("tp", both), P("tp", None, None), P("tp"), P("tp", None), P(), P(),
        P(both, None), P(both, None, "tp"), P(both, None, "tp"), P(both, "tp", None),
    )
    return jax.shard_map(shards, mesh=fine, in_specs=placed, out_specs=P(both, "tp"), check_vma=False)
```

```python
import functools

import jax
import jax.numpy as jnp
from jax import lax
from jax.experimental import pallas as pl
from jax.experimental.pallas import tpu as pltpu
from jax.sharding import Mesh, PartitionSpec as P

epsilon = 1e-06
exact = lax.Precision.HIGHEST
bf16 = jnp.bfloat16
f32 = jnp.float32
LIMIT = 30 << 20


def mm(a, b, contract_a=1, contract_b=0, precision=None):
    return lax.dot_general(
        a, b, (((contract_a,), (contract_b,)), ((), ())),
        precision=precision, preferred_element_type=f32,
    )


def lower_triangle(n, strict=False):
    rows = lax.broadcasted_iota(jnp.int32, (n, n), 0)
    cols = lax.broadcasted_iota(jnp.int32, (n, n), 1)
    return (rows > cols) if strict else (rows >= cols)


def block_state_kernel(keys, values, log_decay, ids, out, *, experts, capacity):
    heads, positions = log_decay.shape
    size = keys.shape[1] // heads
    per_head = out.shape[1]
    rows = size // per_head
    until = mm(lower_triangle(positions).astype(f32), log_decay[...], 1, 1, exact)
    first, second = slots_of(ids[...], experts, capacity)
    chosen = [jnp.broadcast_to(ids[k:k + 1, :].astype(f32), (8, positions)).astype(bf16) for k in range(2)]
    others = mm(chosen[1], first.astype(bf16), 1, 1) + mm(chosen[0], second.astype(bf16), 1, 1)
    for h in range(heads):
        lanes = slice(h * size, (h + 1) * size)
        total = until[positions - 1:positions, h:h + 1]
        trailing = jnp.exp(total - until[:, h:h + 1])
        weighted = (keys[:, lanes].astype(f32) * trailing).astype(bf16)
        state = mm(weighted, values[:, lanes], 0, 0)
        out[h, :, :rows, :] = state.astype(bf16).reshape(per_head, rows, size)
        high = total.astype(bf16).astype(f32)
        middle = (total - high).astype(bf16).astype(f32)
        low = total - high - middle
        row = lax.broadcasted_iota(jnp.int32, (rows, size), 0)
        terms = jnp.where(row == 0, high, jnp.where(row == 1, middle, jnp.where(row == 2, low, 0.0)))
        terms = jnp.where(row == 3, others[0:1, lanes], terms)
        out[h, :, rows:, :] = jnp.broadcast_to(terms.astype(bf16), (per_head, rows, size))


def state_scan_kernel(part, received, prior, out, others):
    blocks, rows, _ = out.shape
    state = prior[pl.ds(pl.multiple_of(part[0] * rows, rows), rows), :]
    for k in range(blocks):
        out[k] = state.astype(bf16)
        terms = received[k, rows:, :].astype(f32)
        total = terms[0:1] + terms[1:2] + terms[2:3]
        state = jnp.exp(total) * state + received[k, :rows, :].astype(f32)
        others[k:k + 1, :] = terms[3:4]


def inner_kernel(queries, keys, values, log_decay, out, growth):
    heads, positions = log_decay.shape
    size = queries.shape[1] // heads
    causal = lower_triangle(positions)
    until = mm(causal.astype(f32), log_decay[...], 1, 1, exact)
    until_row = mm(log_decay[...], causal.astype(f32), 1, 1, exact)
    for h in range(heads):
        lanes = slice(h * size, (h + 1) * size)
        spread = until[:, h:h + 1] - until_row[h:h + 1, :]
        weights = jnp.where(causal, jnp.exp(jnp.where(causal, spread, 0.0)), 0.0)
        scores = mm(queries[:, lanes], keys[:, lanes], 1, 1) * weights
        out[:, lanes] = mm(scores.astype(bf16), values[:, lanes])
    growth[...] = jnp.exp(until)


def project_kernel(queries, inner, growth, state, gate_input, gain, weight, out, normed, *, heads):
    size = queries.shape[1] // heads
    step = pl.program_id(0)

    @pl.when(step == 0)
    def _():
        for h in range(heads):
            lanes = slice(h * size, (h + 1) * size)
            carried = mm(queries[:, lanes], state[lanes, :])
            attended = inner[:, lanes] + growth[:, h:h + 1] * carried
            squares = jnp.mean(attended * attended, axis=1, keepdims=True)
            gating = jax.nn.sigmoid(gate_input[:, lanes].astype(f32))
            normed[:, lanes] = (attended * lax.rsqrt(squares + epsilon) * gain[:, lanes] * gating).astype(bf16)

    each, _, width = out.shape
    product = mm(normed[...], weight[:, pl.ds(pl.multiple_of(step * each * width, each * width), each * width)])
    for c in range(each):
        out[c] = product[:, c * width:(c + 1) * width].astype(bf16)


def slots_of(ids, experts, capacity):
    positions = ids.shape[1]
    expert = lax.broadcasted_iota(jnp.int32, (experts, positions), 0)
    choices = [(ids[k:k + 1, :] == expert).astype(f32) for k in range(2)]
    earlier = mm((choices[0] + choices[1]).astype(bf16), lower_triangle(positions, True).astype(bf16), 1, 1)
    slot = lax.broadcasted_iota(jnp.int32, (experts * capacity, positions), 0)
    found = []
    for k, choice in enumerate(choices):
        position = jnp.sum(choice * earlier, axis=0, keepdims=True).astype(jnp.int32)
        found.append((slot == ids[k:k + 1, :] * capacity + position).astype(f32))
    return found


def dispatch_kernel(index, partial, layer_input, gain, ids, outgoing, hidden, *, experts, capacity):
    del index
    total = layer_input[...].astype(f32)
    for k in range(partial.shape[0]):
        total += partial[k].astype(f32)
    hidden[...] = total
    first, second = slots_of(ids[...], experts, capacity)
    outgoing[...] = mm((first + second).astype(bf16), (total * gain[0]).astype(bf16)).astype(bf16)


def fetch(pairs, sems):
    copies = [pltpu.make_async_copy(source, target, sems.at[k]) for k, (source, target) in enumerate(pairs)]
    for copy in copies:
        copy.start()
    return copies


def load_kernel(source, target, sems):
    parts = sems.shape[0]
    rows = source.shape[0] // parts
    pairs = [(source.at[pl.ds(k * rows, rows)], target.at[pl.ds(k * rows, rows)]) for k in range(parts)]
    for copy in fetch(pairs, sems):
        copy.wait()


def load_experts_kernel(place, *refs, order, distances, peers):
    weights, (gate_up, down, sems) = refs[:6], refs[6:]
    depth, share = weights[0].shape
    rows = depth // peers
    pairs = []
    for c, distance in enumerate(order):
        start = pl.multiple_of(lax.rem(place[0] + distance + peers, peers) * rows, rows)
        for k, weight in enumerate(weights[:4]):
            pairs.append((weight.at[pl.ds(start, rows)], gate_up.at[pl.ds(c * rows, rows), pl.ds(k * share, share)]))
    for c, distance in enumerate(distances):
        start = pl.multiple_of(lax.rem(place[0] + distance + peers, peers) * rows, rows)
        for k, weight in enumerate(weights[4:]):
            pairs.append((weight.at[:, pl.ds(start, rows)], down.at[pl.ds(k * share, share), pl.ds(c * rows, rows)]))
    for copy in fetch(pairs, sems):
        copy.wait()


def gate_up_sums(place, chunks, gain, router, gate_up, order, first, h):
    peers, _, width = gain.shape
    experts = router.shape[0]
    total, squares, logits = 0.0, 0.0, 0.0
    for c in range(0, len(chunks), 2):
        pair = [chunk[h][...] for chunk in chunks[c:c + 2]]
        for k, piece in enumerate(pair):
            group = lax.rem(place[0] + order[first + c + k] + peers, peers)
            wide = piece.astype(f32) / gain[group]
            squares += jnp.sum(wide * wide, axis=1, keepdims=True)
            logits += mm(piece, router[:, pl.ds(pl.multiple_of(group * width, width), width)], 1, 1)
        lanes = slice((first + c) * width, (first + c + 2) * width)
        total += mm(jnp.concatenate(pair, axis=1), gate_up[lanes, :])
    beside = jnp.concatenate([logits, jnp.broadcast_to(squares, (logits.shape[0], 128 - experts))], axis=1)
    return total, beside


def near_chunks_kernel(place, gain, router, gate_up, *refs, order, count):
    chunks, (total, beside) = refs[:2 * count], refs[2 * count:]
    chunks = [chunks[2 * k:2 * k + 2] for k in range(count)]
    half = chunks[0][0].shape[0]
    for h in range(2):
        rows = slice(h * half, (h + 1) * half)
        total[rows, :], beside[rows, :] = gate_up_sums(place, chunks, gain, router, gate_up, order, 0, h)


def mixing_of(place, others, logits, h, capacity):
    rows, experts = logits.shape
    blocks, lanes = others.shape
    row = lax.broadcasted_iota(jnp.int32, (rows, blocks), 0)
    block = lax.broadcasted_iota(jnp.int32, (rows, blocks), 1)
    sender = 2 * (lax.div(row, capacity) + h * (rows // capacity)) + place[1]
    from_sender = mm((sender == block).astype(bf16), others[...].astype(bf16))
    row = lax.broadcasted_iota(jnp.int32, (rows, lanes), 0)
    lane = lax.broadcasted_iota(jnp.int32, (rows, lanes), 1)
    own_lane = lax.rem(place[2], lanes // capacity) * capacity + lax.rem(row, capacity)
    other = jnp.sum(jnp.where(lane == own_lane, from_sender, 0.0), axis=1, keepdims=True).astype(jnp.int32)
    expert = lax.broadcasted_iota(jnp.int32, (rows, experts), 1)
    sign = (expert == place[2]).astype(f32) - (expert == other).astype(f32)
    return jax.nn.sigmoid(jnp.sum(sign * logits, axis=1, keepdims=True))


def products(activated, down, start, count, share):
    found = []
    for c in range(start, start + count, 2):
        both = min(2, start + count - c)
        product = mm(activated, down[:, c * share:(c + both) * share])
        found += [product[:, k * share:(k + 1) * share].astype(bf16) for k in range(both)]
    return found


def far_chunks_kernel(
    place, gain, router, gate_up, down, others, total, beside, *refs, order, count, far, width, capacity
):
    chunks, outs, activated = refs[:2 * count], refs[2 * count:-1], refs[-1]
    chunks = [chunks[2 * k:2 * k + 2] for k in range(count)]
    half = chunks[0][0].shape[0]
    units = activated.shape[1]
    for h in range(2):
        rows = slice(h * half, (h + 1) * half)
        product, sums = gate_up_sums(place, chunks, gain, router, gate_up, order, len(order) - count, h)
        sums += beside[rows, :]
        experts = router.shape[0]
        scale = lax.rsqrt(sums[:, experts:experts + 1] / width + epsilon)
        mixing = mixing_of(place, others, sums[:, :experts] * scale, h, capacity)
        both = (total[rows, :] + product) * scale
        gated = both[:, :units]
        active = (gated * jax.nn.sigmoid(gated) * both[:, units:] * mixing).astype(bf16)
        activated[rows, :] = active
        for k, piece in enumerate(products(active, down, 0, far, outs[0].shape[1])):
            outs[2 * k + h][...] = piece


def near_products_kernel(activated, down, *outs, far, near):
    half = activated.shape[0] // 2
    for h in range(2):
        rows = slice(h * half, (h + 1) * half)
        for k, piece in enumerate(products(activated[rows, :], down, far, near, outs[0].shape[1])):
            outs[2 * k + h][...] = piece


def combine_kernel(returned, hidden, ids, out, *, experts, capacity):
    first, second = slots_of(ids[...], experts, capacity)
    out[...] = (hidden[...] + mm((first + second).astype(bf16), returned[...], 0, 0)).astype(out.dtype)


def call(kernel, shapes, *args, **kwargs):
    return pl.pallas_call(
        kernel,
        out_shape=shapes,
        compiler_params=pltpu.CompilerParams(vmem_limit_bytes=LIMIT),
        **kwargs,
    )(*args)


def stays(x):
    return pltpu.with_memory_space_constraint(x, pltpu.HBM)


def in_vmem(x):
    return pltpu.with_memory_space_constraint(x, pltpu.VMEM)


def whole(shape):
    return pl.BlockSpec(shape, lambda *_: (0,) * len(shape))


def shards(
    layer_input, queries, keys, values, gate_input, log_decay, prior_state, attn_gain,
    out_weight, moe_gain, router, expert_ids, w_gate, w_up, w_down,
):
    struct = jax.ShapeDtypeStruct
    positions, head_lanes = queries.shape
    heads, size, _ = prior_state.shape
    chips, cores, peers = lax.axis_size("chip"), lax.axis_size("core"), lax.axis_size("tp")
    blocks = chips * cores
    width = out_weight.shape[1]
    share = layer_input.shape[1]
    experts = router.shape[1]
    capacity = 8 * positions // blocks
    slots = experts * capacity
    core = lax.axis_index("core")
    cx = lax.axis_index("chip") * cores + core
    tp = lax.axis_index("tp")

    ids = stays(expert_ids.T)
    queries, keys, values, log_decay = stays(queries), stays(keys), stays(values), stays(log_decay)
    vmem = pl.BlockSpec(memory_space=pltpu.VMEM)
    hbm = pl.BlockSpec(memory_space=pl.ANY)

    swap = [(0, 1), (1, 0)]
    weights = []
    for weight in (w_gate[0], w_up[0], w_down[0]):
        weights += [weight, lax.ppermute(weight, "core", swap)]

    rows = heads * size // blocks
    parts = call(
        functools.partial(block_state_kernel, experts=experts, capacity=capacity),
        struct((heads, size // rows, 2 * rows, size), bf16), keys, values, log_decay, ids,
    )
    parts, out_weight = lax.optimization_barrier((parts, out_weight))
    out_weight = pl.pallas_call(
        load_kernel,
        out_shape=pltpu.VMEM((head_lanes, width), bf16),
        in_specs=[hbm],
        out_specs=vmem,
        scratch_shapes=[pltpu.SemaphoreType.DMA((4,))],
        compiler_params=pltpu.CompilerParams(vmem_limit_bytes=4 << 20),
        cost_estimate=pl.CostEstimate(flops=0, bytes_accessed=2 * head_lanes * width, transcendentals=0),
    )(stays(out_weight))
    received = lax.all_to_all(parts.reshape(blocks, 2 * rows, size), ("chip", "core"), 0, 0, tiled=True)
    inner, growth = call(
        inner_kernel,
        (struct((positions, head_lanes), f32), struct((positions, heads), f32)),
        queries, keys, values, log_decay,
    )
    befores, others = call(
        state_scan_kernel, (struct((blocks, rows, size), bf16), struct((blocks, size), f32)),
        cx.reshape(1), received, stays(prior_state.reshape(heads * size, size)),
        in_specs=[pl.BlockSpec(memory_space=pltpu.SMEM)] + [pl.BlockSpec(memory_space=pltpu.VMEM)] * 2,
    )
    state = lax.all_to_all(befores, ("chip", "core"), 0, 0, tiled=True).reshape(heads * size, size)

    each = 2
    partial = call(
        functools.partial(project_kernel, heads=heads),
        struct((peers, positions, share), bf16),
        queries, stays(inner), stays(growth), state, stays(gate_input), stays(attn_gain.reshape(1, head_lanes)),
        in_vmem(out_weight),
        grid=(peers // each,),
        in_specs=[whole((positions, head_lanes))] * 2 + [whole((positions, heads)), whole((heads * size, size))]
        + [whole((positions, head_lanes)), whole((1, head_lanes)), vmem],
        out_specs=pl.BlockSpec((each, positions, share), lambda i: (i, 0, 0)),
        scratch_shapes=[pltpu.VMEM((positions, head_lanes), bf16)],
    )
    partial = lax.all_to_all(partial, "tp", 0, 0, tiled=True)
    outgoing, hidden = pl.pallas_call(
        functools.partial(dispatch_kernel, experts=experts, capacity=capacity),
        out_shape=(struct((slots, share), bf16), struct((positions, share), f32)),
        grid_spec=pltpu.PrefetchScalarGridSpec(
            num_scalar_prefetch=1,
            grid=(1,),
            in_specs=[
                whole((peers, positions, share)),
                whole((positions, share)),
                pl.BlockSpec((1, 1, share), lambda i, index: (index[0], 0, 0)),
                whole(ids.shape),
            ],
            out_specs=[whole((slots, share)), whole((positions, share))],
        ),
        compiler_params=pltpu.CompilerParams(vmem_limit_bytes=LIMIT),
    )(tp.reshape(1), partial, stays(layer_input), stays(moe_gain.reshape(peers, 1, share)), ids)

    arrived = lax.all_to_all(outgoing.reshape(chips, capacity, share), "chip", 0, 0, tiled=True)
    held = chips * capacity
    half = held // 2
    arrived = arrived.reshape(held, share)
    here = (arrived[:half], arrived[half:])
    here, weights = lax.optimization_barrier((here, weights))

    def moved(piece, step):
        return lax.ppermute(piece, "tp", [(i, (i + step) % peers) for i in range(peers)])

    order = (0, 1, -1, 2, -2, 3, -3, 4)
    far, near = (4, 3, -3), (2, -2, 1, -1, 0)
    units = cores * share
    work = 2 * held * width * units
    place = jnp.stack([tp, core, lax.axis_index("chip")])
    params = pltpu.CompilerParams(vmem_limit_bytes=LIMIT)
    smem = pl.BlockSpec(memory_space=pltpu.SMEM)
    gate_up, down = pl.pallas_call(
        functools.partial(load_experts_kernel, order=order, distances=far + near, peers=peers),
        out_shape=(pltpu.VMEM((width, 2 * units), bf16), pltpu.VMEM((units, width), bf16)),
        in_specs=[smem] + [hbm] * 6,
        out_specs=(vmem, vmem),
        scratch_shapes=[pltpu.SemaphoreType.DMA((6 * peers,))],
        compiler_params=pltpu.CompilerParams(vmem_limit_bytes=4 << 20),
        cost_estimate=pl.CostEstimate(flops=0, bytes_accessed=6 * width * units, transcendentals=0),
    )(place, *[stays(weight) for weight in weights])
    gain, router = stays(moe_gain.reshape(peers, 1, share)), stays(router.T)
    others = stays(others)
    chunks = {0: here}
    up, down_way = here, here
    for distance in (1, 2, 3):
        up = (moved(up[0], 1), moved(up[1], 1))
        down_way = (moved(down_way[0], -1), moved(down_way[1], -1))
        if distance == 1:
            up, down_way, gate_up, down = lax.optimization_barrier((up, down_way, gate_up, down))
        chunks[-distance], chunks[distance] = up, down_way
    chunks[4] = (moved(up[0], 1), moved(down_way[1], -1))
    gate_up, down = in_vmem(gate_up), in_vmem(down)
    last = 2
    first_chunks = [piece for distance in order[:-last] for piece in chunks[distance]]
    total, beside = pl.pallas_call(
        functools.partial(near_chunks_kernel, order=order, count=len(order) - last),
        out_shape=(struct((held, 2 * units), f32), struct((held, 128), f32)),
        in_specs=[smem] + [vmem] * (3 + len(first_chunks)),
        compiler_params=params,
        cost_estimate=pl.CostEstimate(
            flops=2 * work * (peers - last) // peers, bytes_accessed=4 << 20, transcendentals=0),
    )(place, gain, router, gate_up, *first_chunks)
    last_chunks = [piece for distance in order[-last:] for piece in chunks[distance]]
    piece = struct((half, share), bf16)
    *ready, activated = pl.pallas_call(
        functools.partial(far_chunks_kernel, order=order, count=last, far=len(far), width=width, capacity=capacity),
        out_shape=(piece,) * (2 * len(far)) + (struct((held, units), bf16),),
        in_specs=[smem] + [vmem] * (7 + len(last_chunks)),
        compiler_params=params,
        cost_estimate=pl.CostEstimate(
            flops=2 * work * last // peers + work * len(far) // peers, bytes_accessed=4 << 20,
            transcendentals=held * units),
    )(place, gain, router, gate_up, down, others, total, beside, *last_chunks)
    a4, b4, a3, b3, a3m, b3m = ready

    def plus(*pieces):
        return sum(piece.astype(f32) for piece in pieces).astype(bf16)

    a_up, b_down = moved(a4, 1), moved(b4, -1)
    a_down, b_up = moved(a3m, -1), moved(b3, 1)
    a2, b2, a2m, b2m, a1, b1, a1m, b1m, a0, b0 = pl.pallas_call(
        functools.partial(near_products_kernel, far=len(far), near=len(near)),
        out_shape=(piece,) * (2 * len(near)),
        in_specs=[vmem] * 2,
        compiler_params=params,
        cost_estimate=pl.CostEstimate(flops=work * len(near) // peers, bytes_accessed=4 << 20, transcendentals=0),
    )(activated, down)
    a_up, b_down = moved(plus(a_up, a3), 1), moved(plus(b_down, b3m), -1)
    a_down, b_up = moved(plus(a_down, a2m), -1), moved(plus(b_up, b2), 1)
    a_up, b_down = moved(plus(a_up, a2), 1), moved(plus(b_down, b2m), -1)
    a_down, b_up = moved(plus(a_down, a1m), -1), moved(plus(b_up, b1), 1)
    a_up, b_down = moved(plus(a_up, a1), 1), moved(plus(b_down, b1m), -1)
    summed = jnp.concatenate([plus(a0, a_up, a_down), plus(b0, b_up, b_down)])
    returned = lax.all_to_all(summed.reshape(chips, capacity, share), "chip", 0, 0, tiled=True)
    return call(
        functools.partial(combine_kernel, experts=experts, capacity=capacity),
        struct((positions, share), bf16),
        returned.reshape(slots, share), hidden, ids,
    )


def solution(mesh):
    cx, tp = mesh.devices.shape
    fine = Mesh(mesh.devices.reshape(cx // 2, 2, tp), ("chip", "core", "tp"))
    both = ("chip", "core")
    placed = (
        P(both, "tp"), P(both, "tp"), P(both, "tp"), P(both, "tp"), P(both, "tp"),
        P("tp", both), P("tp", None, None), P("tp"), P("tp", None), P(), P(),
        P(both, None), P(both, None, "tp"), P(both, None, "tp"), P(both, "tp", None),
    )
    return jax.shard_map(shards, mesh=fine, in_specs=placed, out_specs=P(both, "tp"), check_vma=False)
```

```python
import functools

import jax
import jax.numpy as jnp
from jax import lax
from jax.experimental import pallas as pl
from jax.experimental.pallas import tpu as pltpu
from jax.sharding import Mesh, PartitionSpec as P

epsilon = 1e-06
exact = lax.Precision.HIGHEST
bf16 = jnp.bfloat16
f32 = jnp.float32
LIMIT = 30 << 20


def mm(a, b, contract_a=1, contract_b=0, precision=None):
    return lax.dot_general(
        a, b, (((contract_a,), (contract_b,)), ((), ())),
        precision=precision, preferred_element_type=f32,
    )


def lower_triangle(n, strict=False):
    rows = lax.broadcasted_iota(jnp.int32, (n, n), 0)
    cols = lax.broadcasted_iota(jnp.int32, (n, n), 1)
    return (rows > cols) if strict else (rows >= cols)


def block_state_kernel(keys, values, log_decay, ids, out, *, experts, capacity):
    heads, positions = log_decay.shape
    size = keys.shape[1] // heads
    per_head = out.shape[1]
    rows = size // per_head
    until = mm(lower_triangle(positions).astype(f32), log_decay[...], 1, 1, exact)
    first, second = slots_of(ids[...], experts, capacity)
    chosen = [jnp.broadcast_to(ids[k:k + 1, :].astype(f32), (8, positions)).astype(bf16) for k in range(2)]
    others = mm(chosen[1], first.astype(bf16), 1, 1) + mm(chosen[0], second.astype(bf16), 1, 1)
    for h in range(heads):
        lanes = slice(h * size, (h + 1) * size)
        total = until[positions - 1:positions, h:h + 1]
        trailing = jnp.exp(total - until[:, h:h + 1])
        weighted = (keys[:, lanes].astype(f32) * trailing).astype(bf16)
        state = mm(weighted, values[:, lanes], 0, 0)
        out[h, :, :rows, :] = state.astype(bf16).reshape(per_head, rows, size)
        high = total.astype(bf16).astype(f32)
        middle = (total - high).astype(bf16).astype(f32)
        low = total - high - middle
        row = lax.broadcasted_iota(jnp.int32, (rows, size), 0)
        terms = jnp.where(row == 0, high, jnp.where(row == 1, middle, jnp.where(row == 2, low, 0.0)))
        terms = jnp.where(row == 3, others[0:1, lanes], terms)
        out[h, :, rows:, :] = jnp.broadcast_to(terms.astype(bf16), (per_head, rows, size))


def state_scan_kernel(part, received, prior, out, others):
    blocks, rows, _ = out.shape
    state = prior[pl.ds(pl.multiple_of(part[0] * rows, rows), rows), :]
    for k in range(blocks):
        out[k] = state.astype(bf16)
        terms = received[k, rows:, :].astype(f32)
        total = terms[0:1] + terms[1:2] + terms[2:3]
        state = jnp.exp(total) * state + received[k, :rows, :].astype(f32)
        others[k:k + 1, :] = terms[3:4]


def inner_kernel(queries, keys, values, log_decay, out, growth):
    heads, positions = log_decay.shape
    size = queries.shape[1] // heads
    causal = lower_triangle(positions)
    until = mm(causal.astype(f32), log_decay[...], 1, 1, exact)
    until_row = mm(log_decay[...], causal.astype(f32), 1, 1, exact)
    for h in range(heads):
        lanes = slice(h * size, (h + 1) * size)
        spread = until[:, h:h + 1] - until_row[h:h + 1, :]
        weights = jnp.where(causal, jnp.exp(jnp.where(causal, spread, 0.0)), 0.0)
        scores = mm(queries[:, lanes], keys[:, lanes], 1, 1) * weights
        out[:, lanes] = mm(scores.astype(bf16), values[:, lanes])
    growth[...] = jnp.exp(until)


def project_kernel(place, queries, inner, growth, state, gate_input, gain, weight, *outs, heads, order):
    size = queries.shape[1] // heads
    normed = []
    for h in range(heads):
        lanes = slice(h * size, (h + 1) * size)
        carried = mm(queries[:, lanes], state[lanes, :])
        attended = inner[:, lanes] + growth[:, h:h + 1] * carried
        squares = jnp.mean(attended * attended, axis=1, keepdims=True)
        gating = jax.nn.sigmoid(gate_input[:, lanes].astype(f32))
        normed.append((attended * lax.rsqrt(squares + epsilon) * gain[:, lanes] * gating).astype(bf16))
    normed = jnp.concatenate(normed, axis=1)
    peers = len(order)
    width = weight.shape[1] // peers
    for k, distance in enumerate(order):
        start = pl.multiple_of(lax.rem(place[0] + place[3] * distance + peers, peers) * width, width)
        product = mm(normed, weight[:, pl.ds(start, width)])
        if k:
            outs[k + 1][...] = product.astype(outs[k + 1].dtype)
        else:
            half = product.shape[0] // 2
            outs[0][...] = product[:half].astype(bf16)
            outs[1][...] = product[half:].astype(bf16)


def slots_of(ids, experts, capacity):
    positions = ids.shape[1]
    expert = lax.broadcasted_iota(jnp.int32, (experts, positions), 0)
    choices = [(ids[k:k + 1, :] == expert).astype(f32) for k in range(2)]
    earlier = mm((choices[0] + choices[1]).astype(bf16), lower_triangle(positions, True).astype(bf16), 1, 1)
    slot = lax.broadcasted_iota(jnp.int32, (experts * capacity, positions), 0)
    found = []
    for k, choice in enumerate(choices):
        position = jnp.sum(choice * earlier, axis=0, keepdims=True).astype(jnp.int32)
        found.append((slot == ids[k:k + 1, :] * capacity + position).astype(f32))
    return found


def dispatch_kernel(index, up, down, own, layer_input, gain, ids, outgoing, hidden, *, experts, capacity):
    del index
    total = layer_input[...].astype(f32) + own[...] + up[...].astype(f32) + down[...].astype(f32)
    hidden[...] = total
    first, second = slots_of(ids[...], experts, capacity)
    outgoing[...] = mm((first + second).astype(bf16), (total * gain[0]).astype(bf16)).astype(bf16)


def fetch(pairs, sems):
    copies = [pltpu.make_async_copy(source, target, sems.at[k]) for k, (source, target) in enumerate(pairs)]
    for copy in copies:
        copy.start()
    return copies


def load_kernel(source, target, sems):
    parts = sems.shape[0]
    rows = source.shape[0] // parts
    pairs = [(source.at[pl.ds(k * rows, rows)], target.at[pl.ds(k * rows, rows)]) for k in range(parts)]
    for copy in fetch(pairs, sems):
        copy.wait()


def load_rows_kernel(place, *refs, order, peers):
    weights, (gate_up, sems) = refs[:-2], refs[-2:]
    depth, share = weights[0].shape
    rows = depth // peers
    pairs = []
    for c, distance in enumerate(order):
        start = pl.multiple_of(lax.rem(place[0] + place[3] * distance + peers, peers) * rows, rows)
        for k, weight in enumerate(weights):
            pairs.append((weight.at[pl.ds(start, rows)], gate_up.at[pl.ds(c * rows, rows), pl.ds(k * share, share)]))
    for copy in fetch(pairs, sems):
        copy.wait()


def load_columns_kernel(place, *refs, order, peers):
    weights, (down, sems) = refs[:-2], refs[-2:]
    share, depth = weights[0].shape
    width = depth // peers
    pairs = []
    for c, distance in enumerate(order):
        start = pl.multiple_of(lax.rem(place[0] + place[3] * distance + peers, peers) * width, width)
        for k, weight in enumerate(weights):
            pairs.append((weight.at[:, pl.ds(start, width)], down.at[pl.ds(k * share, share), pl.ds(c * width, width)]))
    for copy in fetch(pairs, sems):
        copy.wait()


def gate_up_sums(place, pieces, gain, router, gate_up, order, first):
    peers, _, width = gain.shape
    experts = router.shape[0]
    total, squares, logits = 0.0, 0.0, 0.0
    for c in range(0, len(pieces), 2):
        pair = [piece[...] for piece in pieces[c:c + 2]]
        for k, piece in enumerate(pair):
            group = lax.rem(place[0] + place[3] * order[c + k] + peers, peers)
            wide = piece.astype(f32) / gain[group]
            squares += jnp.sum(wide * wide, axis=1, keepdims=True)
            logits += mm(piece, router[:, pl.ds(pl.multiple_of(group * width, width), width)], 1, 1)
        lanes = slice((first + c) * width, (first + c + 2) * width)
        total += mm(jnp.concatenate(pair, axis=1), gate_up[lanes, :])
    beside = jnp.concatenate([logits, jnp.broadcast_to(squares, (logits.shape[0], 128 - experts))], axis=1)
    return total, beside


def start_sums_kernel(place, gain, router, gate_up, *refs, order):
    count = len(order)
    for h in range(2):
        total, beside = refs[2 * count + 2 * h:2 * count + 2 * h + 2]
        total[...], beside[...] = gate_up_sums(place, refs[h * count:(h + 1) * count], gain, router, gate_up, order, 0)


def more_sums_kernel(place, gain, router, gate_up, *refs, order):
    count = len(order)
    befores, refs = refs[:4], refs[4:]
    for h in range(2):
        total, beside = refs[2 * count + 2 * h:2 * count + 2 * h + 2]
        product, sums = gate_up_sums(place, refs[h * count:(h + 1) * count], gain, router, gate_up, order, 0)
        total[...] = befores[2 * h][...] + product
        beside[...] = befores[2 * h + 1][...] + sums


def mixing_of(place, others, logits, h, capacity):
    rows, experts = logits.shape
    blocks, lanes = others.shape
    row = lax.broadcasted_iota(jnp.int32, (rows, blocks), 0)
    block = lax.broadcasted_iota(jnp.int32, (rows, blocks), 1)
    sender = 2 * (lax.div(row, capacity) + h * (rows // capacity)) + place[1]
    from_sender = mm((sender == block).astype(bf16), others[...].astype(bf16))
    row = lax.broadcasted_iota(jnp.int32, (rows, lanes), 0)
    lane = lax.broadcasted_iota(jnp.int32, (rows, lanes), 1)
    own_lane = lax.rem(place[2], lanes // capacity) * capacity + lax.rem(row, capacity)
    other = jnp.sum(jnp.where(lane == own_lane, from_sender, 0.0), axis=1, keepdims=True).astype(jnp.int32)
    expert = lax.broadcasted_iota(jnp.int32, (rows, experts), 1)
    sign = (expert == place[2]).astype(f32) - (expert == other).astype(f32)
    return jax.nn.sigmoid(jnp.sum(sign * logits, axis=1, keepdims=True))


def products(activated, down, start, count, share):
    found = []
    for c in range(start, start + count, 2):
        both = min(2, start + count - c)
        product = mm(activated, down[:, c * share:(c + both) * share])
        found += [product[:, k * share:(k + 1) * share].astype(bf16) for k in range(both)]
    return found


def far_products_kernel(
    place, gain, router, gate_up, down, others, total, beside, *refs, order, first, h, far, width, capacity
):
    count = len(order)
    outs, activated = refs[count:-1], refs[-1]
    units = activated.shape[1]
    product, sums = gate_up_sums(place, refs[:count], gain, router, gate_up, order, first)
    sums += beside[...]
    experts = router.shape[0]
    scale = lax.rsqrt(sums[:, experts:experts + 1] / width + epsilon)
    mixing = mixing_of(place, others, sums[:, :experts] * scale, h, capacity)
    both = (total[...] + product) * scale
    gated = both[:, :units]
    active = (gated * jax.nn.sigmoid(gated) * both[:, units:] * mixing).astype(bf16)
    activated[...] = active
    for k, piece in enumerate(products(active, down, 0, far, outs[0].shape[1])):
        outs[k][...] = piece


def near_products_kernel(active_a, active_b, down, *outs, far, near):
    for h, active in enumerate((active_a, active_b)):
        for k, piece in enumerate(products(active[...], down, far, near, outs[0].shape[1])):
            outs[2 * k + h][...] = piece


def combine_kernel(returned, hidden, ids, out, *, experts, capacity):
    first, second = slots_of(ids[...], experts, capacity)
    out[...] = (hidden[...] + mm((first + second).astype(bf16), returned[...], 0, 0)).astype(out.dtype)


def call(kernel, shapes, *args, **kwargs):
    return pl.pallas_call(
        kernel,
        out_shape=shapes,
        compiler_params=pltpu.CompilerParams(vmem_limit_bytes=LIMIT),
        **kwargs,
    )(*args)


def stays(x):
    return pltpu.with_memory_space_constraint(x, pltpu.HBM)


def in_vmem(x):
    return pltpu.with_memory_space_constraint(x, pltpu.VMEM)


def whole(shape):
    return pl.BlockSpec(shape, lambda *_: (0,) * len(shape))


def shards(
    layer_input, queries, keys, values, gate_input, log_decay, prior_state, attn_gain,
    out_weight, moe_gain, router, expert_ids, w_gate, w_up, w_down,
):
    struct = jax.ShapeDtypeStruct
    positions, head_lanes = queries.shape
    heads, size, _ = prior_state.shape
    chips, cores, peers = lax.axis_size("chip"), lax.axis_size("core"), lax.axis_size("tp")
    blocks = chips * cores
    width = out_weight.shape[1]
    share = layer_input.shape[1]
    experts = router.shape[1]
    capacity = 8 * positions // blocks
    slots = experts * capacity
    core, chip, tp = lax.axis_index("core"), lax.axis_index("chip"), lax.axis_index("tp")
    cx = chip * cores + core
    place = jnp.stack([tp, core, chip, 1 - 2 * core])
    place, cx, tp, keys = lax.optimization_barrier((place, cx, tp, keys))

    ids = stays(expert_ids.T)
    queries, keys, values, log_decay = stays(queries), stays(keys), stays(values), stays(log_decay)
    vmem = pl.BlockSpec(memory_space=pltpu.VMEM)
    smem = pl.BlockSpec(memory_space=pltpu.SMEM)
    tied = lax.optimization_barrier

    def moved(piece, step):
        pairs = [
            (c * peers + i, c * peers + (i + (step if c == 0 else -step)) % peers)
            for c in range(cores) for i in range(peers)
        ]
        return lax.ppermute(piece, ("core", "tp"), pairs)

    def plus(*pieces):
        return sum(piece.astype(f32) for piece in pieces).astype(bf16)
    hbm = pl.BlockSpec(memory_space=pl.ANY)

    swap = [(0, 1), (1, 0)]
    weights = []
    for weight in (w_gate[0], w_up[0], w_down[0]):
        weights += [weight, lax.ppermute(weight, "core", swap)]

    rows = heads * size // blocks
    parts = call(
        functools.partial(block_state_kernel, experts=experts, capacity=capacity),
        struct((heads, size // rows, 2 * rows, size), bf16), keys, values, log_decay, ids,
    )
    parts, out_weight = lax.optimization_barrier((parts, out_weight))
    out_weight = pl.pallas_call(
        load_kernel,
        out_shape=pltpu.VMEM((head_lanes, width), bf16),
        in_specs=[hbm],
        out_specs=vmem,
        scratch_shapes=[pltpu.SemaphoreType.DMA((4,))],
        compiler_params=pltpu.CompilerParams(vmem_limit_bytes=4 << 20),
        cost_estimate=pl.CostEstimate(flops=0, bytes_accessed=2 * head_lanes * width, transcendentals=0),
    )(stays(out_weight))
    received = lax.all_to_all(parts.reshape(blocks, 2 * rows, size), ("chip", "core"), 0, 0, tiled=True)
    inner, growth = call(
        inner_kernel,
        (struct((positions, head_lanes), f32), struct((positions, heads), f32)),
        queries, keys, values, log_decay,
    )
    befores, others = call(
        state_scan_kernel, (struct((blocks, rows, size), bf16), struct((blocks, size), f32)),
        cx.reshape(1), received, stays(prior_state.reshape(heads * size, size)),
        in_specs=[pl.BlockSpec(memory_space=pltpu.SMEM)] + [pl.BlockSpec(memory_space=pltpu.VMEM)] * 2,
    )
    state = lax.all_to_all(befores, ("chip", "core"), 0, 0, tiled=True).reshape(heads * size, size)

    row = struct((positions, share), bf16)
    top, bottom, r3, r3m, r2, r2m, r1, r1m, r0 = call(
        functools.partial(project_kernel, heads=heads, order=(4, 3, -3, 2, -2, 1, -1, 0)),
        (struct((positions // 2, share), bf16),) * 2 + (row,) * 6 + (struct((positions, share), f32),),
        place, queries, stays(inner), stays(growth), state, stays(gate_input), stays(attn_gain.reshape(1, head_lanes)),
        in_vmem(out_weight),
        in_specs=[smem] + [vmem] * 7,
    )
    middle = positions // 2
    up, down = tied((moved(top, 1), moved(bottom, -1)))
    up = jnp.concatenate([plus(up, r3[:middle]), r3[middle:]])
    down = jnp.concatenate([r3m[:middle], plus(down, r3m[middle:])])
    up, down = tied((moved(up, 1), moved(down, -1)))
    up, down = tied((moved(plus(up, r2), 1), moved(plus(down, r2m), -1)))
    up, down = tied((moved(plus(up, r1), 1), moved(plus(down, r1m), -1)))
    outgoing, hidden = pl.pallas_call(
        functools.partial(dispatch_kernel, experts=experts, capacity=capacity),
        out_shape=(struct((slots, share), bf16), struct((positions, share), f32)),
        grid_spec=pltpu.PrefetchScalarGridSpec(
            num_scalar_prefetch=1,
            grid=(1,),
            in_specs=[
                whole((positions, share)),
                whole((positions, share)),
                whole((positions, share)),
                whole((positions, share)),
                pl.BlockSpec((1, 1, share), lambda i, index: (index[0], 0, 0)),
                whole(ids.shape),
            ],
            out_specs=[whole((slots, share)), whole((positions, share))],
        ),
        compiler_params=pltpu.CompilerParams(vmem_limit_bytes=LIMIT),
    )(tp.reshape(1), up, down, r0, stays(layer_input), stays(moe_gain.reshape(peers, 1, share)), ids)

    arrived = lax.all_to_all(outgoing.reshape(chips, capacity, share), "chip", 0, 0, tiled=True)
    held = chips * capacity
    half = held // 2
    arrived = arrived.reshape(held, share)
    here = (arrived[:half], arrived[half:])
    here, weights = lax.optimization_barrier((here, weights))

    order = (0, 1, -1, 2, -2, 3, -3, 4)
    parts = order[:4], order[4:6], order[6:]
    far, near = (4, 3, -3), (2, -2, 1, -1, 0)
    units = cores * share
    work = held * width * units
    params = pltpu.CompilerParams(vmem_limit_bytes=LIMIT)
    gain, router = stays(moe_gain.reshape(peers, 1, share)), stays(router.T)
    others = stays(others)
    sides, downs = [stays(weight) for weight in weights[:4]], [stays(weight) for weight in weights[4:]]

    def cost(flops, size):
        return pl.CostEstimate(flops=flops, bytes_accessed=size, transcendentals=0)

    def load(kernel, shape, order, sources):
        return pl.pallas_call(
            functools.partial(kernel, order=order, peers=peers),
            out_shape=pltpu.VMEM(shape, bf16),
            in_specs=[smem] + [hbm] * len(sources),
            out_specs=vmem,
            scratch_shapes=[pltpu.SemaphoreType.DMA((len(order) * len(sources),))],
            compiler_params=pltpu.CompilerParams(vmem_limit_bytes=4 << 20),
            cost_estimate=cost(0, 4 * shape[0] * shape[1]),
        )(place, *sources)

    def kept(kernel, shapes, flops, *args, **options):
        return pl.pallas_call(
            functools.partial(kernel, **options),
            out_shape=shapes,
            in_specs=[smem] + [vmem] * (len(args) - 1) if args[0] is place else [vmem] * len(args),
            compiler_params=params,
            cost_estimate=cost(flops, 4 << 20),
        )(*args)

    sums = (struct((half, 2 * units), f32), struct((half, 128), f32)) * 2
    got = ({0: here[0]}, {0: here[1]})
    for distance in (1, 2, 3):
        moving = [(moved(mine[1 - distance], 1), moved(mine[distance - 1], -1)) for mine in got]
        if distance == 1:
            gate_up = load(load_rows_kernel, (width // 2, 2 * units), order[:4], sides)
            moving[0], gate_up = lax.optimization_barrier((moving[0], gate_up))
        elif distance == 2:
            gate_up_rest = load(load_rows_kernel, (width // 2, 2 * units), order[4:], sides)
            moving[0], gate_up_rest = lax.optimization_barrier((moving[0], gate_up_rest))
        else:
            down = load(load_columns_kernel, (units, width), far + near, downs)
            totals = kept(
                start_sums_kernel, sums, 2 * work, place, gain, router, in_vmem(gate_up),
                *[mine[k] for mine in got for k in parts[0]], order=parts[0],
            )
            moving[0], totals, down = lax.optimization_barrier((moving[0], totals, down))
        for mine, (up, down_way) in zip(got, moving):
            mine[-distance], mine[distance] = lax.optimization_barrier((up, down_way))
    got[0][4], got[1][4] = moved(got[0][-3], 1), moved(got[1][3], -1)
    gate_up_rest, down = in_vmem(gate_up_rest), in_vmem(down)
    totals = kept(
        more_sums_kernel, sums, work, place, gain, router, gate_up_rest, *totals,
        *[mine[k] for mine in got for k in parts[1]], order=parts[1],
    )
    piece = struct((half, share), bf16)
    ready = [
        kept(
            far_products_kernel, (piece,) * len(far) + (struct((half, units), bf16),), work,
            place, gain, router, gate_up_rest, down, others, *totals[2 * h:2 * h + 2], *[got[h][k] for k in parts[2]],
            order=parts[2], first=2, h=h, far=len(far), width=width, capacity=capacity,
        )
        for h in range(2)
    ]
    (a4, a3, a3m, active_a), (b4, b3, b3m, active_b) = ready

    a_up, a_down = tied((moved(a4, 1), moved(a3m, -1)))
    b_up, b_down = tied((moved(b3, 1), moved(b4, -1)))
    a2, b2, a2m, b2m, a1, b1, a1m, b1m, a0, b0 = kept(
        near_products_kernel, (piece,) * (2 * len(near)), work, active_a, active_b, down, far=len(far), near=len(near))
    a_up, a_down = tied((moved(plus(a_up, a3), 1), moved(plus(a_down, a2m), -1)))
    b_up, b_down = tied((moved(plus(b_up, b2), 1), moved(plus(b_down, b3m), -1)))
    a_up, a_down = tied((moved(plus(a_up, a2), 1), moved(plus(a_down, a1m), -1)))
    b_up, b_down = tied((moved(plus(b_up, b1), 1), moved(plus(b_down, b2m), -1)))
    a_up, b_down = moved(plus(a_up, a1), 1), moved(plus(b_down, b1m), -1)
    summed = jnp.concatenate([plus(a0, a_up, a_down), plus(b0, b_up, b_down)])
    returned = lax.all_to_all(summed.reshape(chips, capacity, share), "chip", 0, 0, tiled=True)
    return call(
        functools.partial(combine_kernel, experts=experts, capacity=capacity),
        struct((positions, share), bf16),
        returned.reshape(slots, share), hidden, ids,
    )


def solution(mesh):
    cx, tp = mesh.devices.shape
    fine = Mesh(mesh.devices.reshape(cx // 2, 2, tp), ("chip", "core", "tp"))
    both = ("chip", "core")
    placed = (
        P(both, "tp"), P(both, "tp"), P(both, "tp"), P(both, "tp"), P(both, "tp"),
        P("tp", both), P("tp", None, None), P("tp"), P("tp", None), P(), P(),
        P(both, None), P(both, None, "tp"), P(both, None, "tp"), P(both, "tp", None),
    )
    return jax.shard_map(shards, mesh=fine, in_specs=placed, out_specs=P(both, "tp"), check_vma=False)
```

```python
import functools

import jax
import jax.numpy as jnp
from jax import lax
from jax.experimental import pallas as pl
from jax.experimental.pallas import tpu as pltpu
from jax.sharding import Mesh, PartitionSpec as P

epsilon = 1e-06
exact = lax.Precision.HIGHEST
bf16 = jnp.bfloat16
f32 = jnp.float32
LIMIT = 30 << 20


def mm(a, b, contract_a=1, contract_b=0, precision=None):
    return lax.dot_general(
        a, b, (((contract_a,), (contract_b,)), ((), ())),
        precision=precision, preferred_element_type=f32,
    )


def lower_triangle(n, strict=False):
    rows = lax.broadcasted_iota(jnp.int32, (n, n), 0)
    cols = lax.broadcasted_iota(jnp.int32, (n, n), 1)
    return (rows > cols) if strict else (rows >= cols)


def block_state_kernel(keys, values, log_decay, ids, out, *, experts, capacity):
    heads, positions = log_decay.shape
    size = keys.shape[1] // heads
    per_head = out.shape[1]
    rows = size // per_head
    until = mm(lower_triangle(positions).astype(f32), log_decay[...], 1, 1, exact)
    first, second = slots_of(ids[...], experts, capacity)
    chosen = [jnp.broadcast_to(ids[k:k + 1, :].astype(f32), (8, positions)).astype(bf16) for k in range(2)]
    others = mm(chosen[1], first.astype(bf16), 1, 1) + mm(chosen[0], second.astype(bf16), 1, 1)
    for h in range(heads):
        lanes = slice(h * size, (h + 1) * size)
        total = until[positions - 1:positions, h:h + 1]
        trailing = jnp.exp(total - until[:, h:h + 1])
        weighted = (keys[:, lanes].astype(f32) * trailing).astype(bf16)
        state = mm(weighted, values[:, lanes], 0, 0)
        out[h, :, :rows, :] = state.astype(bf16).reshape(per_head, rows, size)
        high = total.astype(bf16).astype(f32)
        middle = (total - high).astype(bf16).astype(f32)
        low = total - high - middle
        row = lax.broadcasted_iota(jnp.int32, (rows, size), 0)
        terms = jnp.where(row == 0, high, jnp.where(row == 1, middle, jnp.where(row == 2, low, 0.0)))
        terms = jnp.where(row == 3, others[0:1, lanes], terms)
        out[h, :, rows:, :] = jnp.broadcast_to(terms.astype(bf16), (per_head, rows, size))


def load_part_kernel(part, source, target, sem):
    rows = target.shape[0]
    copy = pltpu.make_async_copy(source.at[pl.ds(pl.multiple_of(part[0] * rows, rows), rows)], target, sem)
    copy.start()
    copy.wait()


def state_scan_kernel(received, prior, out, others):
    blocks, rows, _ = out.shape
    state = prior[...]
    for k in range(blocks):
        out[k] = state.astype(bf16)
        terms = received[k, rows:, :].astype(f32)
        total = terms[0:1] + terms[1:2] + terms[2:3]
        state = jnp.exp(total) * state + received[k, :rows, :].astype(f32)
        others[k:k + 1, :] = terms[3:4]


def inner_kernel(queries, keys, values, log_decay, out, growth):
    heads, positions = log_decay.shape
    size = queries.shape[1] // heads
    causal = lower_triangle(positions)
    until = mm(causal.astype(f32), log_decay[...], 1, 1, exact)
    until_row = mm(log_decay[...], causal.astype(f32), 1, 1, exact)
    for h in range(heads):
        lanes = slice(h * size, (h + 1) * size)
        spread = until[:, h:h + 1] - until_row[h:h + 1, :]
        weights = jnp.where(causal, jnp.exp(jnp.where(causal, spread, 0.0)), 0.0)
        scores = mm(queries[:, lanes], keys[:, lanes], 1, 1) * weights
        out[:, lanes] = mm(scores.astype(bf16), values[:, lanes])
    growth[...] = jnp.exp(until)


def project_kernel(place, queries, inner, growth, state, gate_input, gain, weight, *outs, heads, order):
    size = queries.shape[1] // heads
    normed = []
    for h in range(heads):
        lanes = slice(h * size, (h + 1) * size)
        carried = mm(queries[:, lanes], state[lanes, :])
        attended = inner[:, lanes] + growth[:, h:h + 1] * carried
        squares = jnp.mean(attended * attended, axis=1, keepdims=True)
        gating = jax.nn.sigmoid(gate_input[:, lanes].astype(f32))
        normed.append((attended * lax.rsqrt(squares + epsilon) * gain[:, lanes] * gating).astype(bf16))
    normed = jnp.concatenate(normed, axis=1)
    peers = len(order)
    width = weight.shape[1] // peers
    for k, distance in enumerate(order):
        start = pl.multiple_of(lax.rem(place[0] + place[3] * distance + peers, peers) * width, width)
        product = mm(normed, weight[:, pl.ds(start, width)])
        if k:
            outs[k + 1][...] = product.astype(outs[k + 1].dtype)
        else:
            half = product.shape[0] // 2
            outs[0][...] = product[:half].astype(bf16)
            outs[1][...] = product[half:].astype(bf16)


def slots_of(ids, experts, capacity):
    positions = ids.shape[1]
    expert = lax.broadcasted_iota(jnp.int32, (experts, positions), 0)
    choices = [(ids[k:k + 1, :] == expert).astype(f32) for k in range(2)]
    earlier = mm((choices[0] + choices[1]).astype(bf16), lower_triangle(positions, True).astype(bf16), 1, 1)
    slot = lax.broadcasted_iota(jnp.int32, (experts * capacity, positions), 0)
    found = []
    for k, choice in enumerate(choices):
        position = jnp.sum(choice * earlier, axis=0, keepdims=True).astype(jnp.int32)
        found.append((slot == ids[k:k + 1, :] * capacity + position).astype(f32))
    return found


def prepare_kernel(place, gain, layer_input, ids, scale, layer, chosen, *, experts, capacity):
    scale[...] = gain[place[0]]
    layer[...] = layer_input[...]
    first, second = slots_of(ids[...], experts, capacity)
    chosen[...] = (first + second).astype(bf16)


def dispatch_kernel(up, down, own, scale, layer, chosen, outgoing, hidden):
    total = layer[...].astype(f32) + own[...] + up[...].astype(f32) + down[...].astype(f32)
    hidden[...] = total
    outgoing[...] = mm(chosen[...], (total * scale[...]).astype(bf16)).astype(bf16)


def fetch(pairs, sems):
    copies = [pltpu.make_async_copy(source, target, sems.at[k]) for k, (source, target) in enumerate(pairs)]
    for copy in copies:
        copy.start()
    return copies


def load_kernel(source, target, sems):
    parts = sems.shape[0]
    rows = source.shape[0] // parts
    pairs = [(source.at[pl.ds(k * rows, rows)], target.at[pl.ds(k * rows, rows)]) for k in range(parts)]
    for copy in fetch(pairs, sems):
        copy.wait()


def row_copies(place, weights, gate_up, sems, order, peers):
    depth, share = weights[0].shape
    rows = depth // peers
    copies = []
    for c, distance in enumerate(order):
        start = pl.multiple_of(lax.rem(place[0] + place[3] * distance + peers, peers) * rows, rows)
        for k, weight in enumerate(weights):
            target = gate_up.at[pl.ds(c * rows, rows), pl.ds(k * share, share)]
            copies.append(pltpu.make_async_copy(weight.at[pl.ds(start, rows)], target, sems.at[c * len(weights) + k]))
    return copies


def column_copies(place, weights, down, sems, order, peers):
    share, depth = weights[0].shape
    width = depth // peers
    copies = []
    for c, distance in enumerate(order):
        start = pl.multiple_of(lax.rem(place[0] + place[3] * distance + peers, peers) * width, width)
        for k, weight in enumerate(weights):
            target = down.at[pl.ds(k * share, share), pl.ds(c * width, width)]
            copies.append(pltpu.make_async_copy(weight.at[:, pl.ds(start, width)], target, sems.at[c * len(weights) + k]))
    return copies


def gate_up_sums(place, pieces, inverse, router, gate_up, order):
    peers, _, width = inverse.shape
    experts = router.shape[0]
    squares, logits = 0.0, 0.0
    for k, piece in enumerate(pieces):
        group = lax.rem(place[0] + place[3] * order[k] + peers, peers)
        wide = piece.astype(f32) * inverse[group]
        squares += jnp.sum(wide * wide, axis=1, keepdims=True)
        logits += mm(piece, router[:, pl.ds(pl.multiple_of(group * width, width), width)], 1, 1)
    total = mm(jnp.concatenate(pieces, axis=1), gate_up[...])
    beside = jnp.concatenate([logits, jnp.broadcast_to(squares, (logits.shape[0], 128 - experts))], axis=1)
    return total, beside


def pair_sums_kernel(place, inverse, router, gate_up, *refs, order, rows, columns, fresh):
    weights, downs, chunks = refs[:4], refs[4:6], refs[6:10]
    befores, outs = ((), refs[10:]) if fresh else (refs[10:14], refs[14:])
    peers = inverse.shape[0]
    totals, loaded, sems = outs[:4], outs[4:-2], outs[-2:]
    copies = row_copies(place, weights, loaded[0], sems[0], rows, peers)
    if columns:
        copies += column_copies(place, downs, loaded[1], sems[1], columns, peers)
    for copy in copies:
        copy.start()
    for h in range(2):
        found = gate_up_sums(place, [ref[...] for ref in chunks[2 * h:2 * h + 2]], inverse, router, gate_up, order)
        for k in range(2):
            totals[2 * h + k][...] = found[k] if fresh else befores[2 * h + k][...] + found[k]
    for copy in copies:
        copy.wait()


def first_load_kernel(place, gain, router, others, *refs, rows, columns):
    weights, downs, (gate_up, down, inverse, router_out, others_out, *sems) = refs[:4], refs[4:6], refs[6:]
    peers = gain.shape[0]
    copies = row_copies(place, weights, gate_up, sems[0], rows, peers)
    copies += column_copies(place, downs, down, sems[1], columns, peers)
    for copy in copies:
        copy.start()
    inverse[...] = 1.0 / gain[...]
    router_out[...] = router[...]
    others_out[...] = others[...]
    for copy in copies:
        copy.wait()


def mixing_of(place, others, logits, h, capacity):
    rows, experts = logits.shape
    blocks, lanes = others.shape
    row = lax.broadcasted_iota(jnp.int32, (rows, blocks), 0)
    block = lax.broadcasted_iota(jnp.int32, (rows, blocks), 1)
    sender = 2 * (lax.div(row, capacity) + h * (rows // capacity)) + place[1]
    from_sender = mm((sender == block).astype(bf16), others[...].astype(bf16))
    row = lax.broadcasted_iota(jnp.int32, (rows, lanes), 0)
    lane = lax.broadcasted_iota(jnp.int32, (rows, lanes), 1)
    own_lane = lax.rem(place[2], lanes // capacity) * capacity + lax.rem(row, capacity)
    other = jnp.sum(jnp.where(lane == own_lane, from_sender, 0.0), axis=1, keepdims=True).astype(jnp.int32)
    expert = lax.broadcasted_iota(jnp.int32, (rows, experts), 1)
    sign = (expert == place[2]).astype(f32) - (expert == other).astype(f32)
    return jax.nn.sigmoid(jnp.sum(sign * logits, axis=1, keepdims=True))


def products(activated, down, start, count, share):
    found = []
    for c in range(start, start + count, 2):
        both = min(2, start + count - c)
        product = mm(activated, down[:, c * share:(c + both) * share])
        found += [product[:, k * share:(k + 1) * share].astype(bf16) for k in range(both)]
    return found


def far_products_kernel(
    place, inverse, router, gate_up, down, others, total, beside, *refs, order, h, far, width, capacity
):
    count = len(order)
    outs, activated = refs[count:-1], refs[-1]
    units = activated.shape[1]
    product, sums = gate_up_sums(place, [ref[...] for ref in refs[:count]], inverse, router, gate_up, order)
    sums += beside[...]
    experts = router.shape[0]
    scale = lax.rsqrt(sums[:, experts:experts + 1] / width + epsilon)
    mixing = mixing_of(place, others, sums[:, :experts] * scale, h, capacity)
    both = (total[...] + product) * scale
    gated = both[:, :units]
    active = (gated * jax.nn.sigmoid(gated) * both[:, units:] * mixing).astype(bf16)
    activated[...] = active
    for k, piece in enumerate(products(active, down, 0, far, outs[0].shape[1])):
        outs[k][...] = piece


def near_products_kernel(active_a, active_b, down, *outs, near):
    for h, active in enumerate((active_a, active_b)):
        for k, piece in enumerate(products(active[...], down, 0, near, outs[0].shape[1])):
            outs[2 * k + h][...] = piece


def combine_kernel(returned, hidden, chosen, out):
    out[...] = (hidden[...] + mm(chosen[...], returned[...], 0, 0)).astype(out.dtype)


def call(kernel, shapes, *args, **kwargs):
    return pl.pallas_call(
        kernel,
        out_shape=shapes,
        compiler_params=pltpu.CompilerParams(vmem_limit_bytes=LIMIT),
        **kwargs,
    )(*args)


def stays(x):
    return pltpu.with_memory_space_constraint(x, pltpu.HBM)


def in_vmem(x):
    return pltpu.with_memory_space_constraint(x, pltpu.VMEM)


def whole(shape):
    return pl.BlockSpec(shape, lambda *_: (0,) * len(shape))


def shards(
    layer_input, queries, keys, values, gate_input, log_decay, prior_state, attn_gain,
    out_weight, moe_gain, router, expert_ids, w_gate, w_up, w_down,
):
    struct = jax.ShapeDtypeStruct
    positions, head_lanes = queries.shape
    heads, size, _ = prior_state.shape
    chips, cores, peers = lax.axis_size("chip"), lax.axis_size("core"), lax.axis_size("tp")
    blocks = chips * cores
    width = out_weight.shape[1]
    share = layer_input.shape[1]
    experts = router.shape[1]
    capacity = 8 * positions // blocks
    slots = experts * capacity
    core, chip, tp = lax.axis_index("core"), lax.axis_index("chip"), lax.axis_index("tp")
    cx = chip * cores + core
    place = jnp.stack([tp, core, chip, 1 - 2 * core])
    place, cx, tp, keys = lax.optimization_barrier((place, cx, tp, keys))

    ids = stays(expert_ids.T)
    queries, keys, values, log_decay = stays(queries), stays(keys), stays(values), stays(log_decay)
    vmem = pl.BlockSpec(memory_space=pltpu.VMEM)
    smem = pl.BlockSpec(memory_space=pltpu.SMEM)
    tied = lax.optimization_barrier

    def moved(piece, step):
        pairs = [
            (c * peers + i, c * peers + (i + (step if c == 0 else -step)) % peers)
            for c in range(cores) for i in range(peers)
        ]
        return lax.ppermute(piece, ("core", "tp"), pairs)

    def plus(*pieces):
        return sum(piece.astype(f32) for piece in pieces).astype(bf16)
    hbm = pl.BlockSpec(memory_space=pl.ANY)

    swap = [(0, 1), (1, 0)]
    weights = []
    for weight in (w_gate[0], w_up[0], w_down[0]):
        weights += [weight, lax.ppermute(weight, "core", swap)]

    rows = heads * size // blocks
    parts = call(
        functools.partial(block_state_kernel, experts=experts, capacity=capacity),
        struct((heads, size // rows, 2 * rows, size), bf16), keys, values, log_decay, ids,
    )
    parts, out_weight, prior_state = lax.optimization_barrier((parts, out_weight, prior_state))
    prior = pl.pallas_call(
        load_part_kernel,
        out_shape=pltpu.VMEM((rows, size), f32),
        in_specs=[smem, hbm],
        out_specs=vmem,
        scratch_shapes=[pltpu.SemaphoreType.DMA],
        compiler_params=pltpu.CompilerParams(vmem_limit_bytes=4 << 20),
        cost_estimate=pl.CostEstimate(flops=0, bytes_accessed=1 << 20, transcendentals=0),
    )(cx.reshape(1), stays(prior_state.reshape(heads * size, size)))
    out_weight = pl.pallas_call(
        load_kernel,
        out_shape=pltpu.VMEM((head_lanes, width), bf16),
        in_specs=[hbm],
        out_specs=vmem,
        scratch_shapes=[pltpu.SemaphoreType.DMA((4,))],
        compiler_params=pltpu.CompilerParams(vmem_limit_bytes=4 << 20),
        cost_estimate=pl.CostEstimate(flops=0, bytes_accessed=2 * head_lanes * width, transcendentals=0),
    )(stays(out_weight))
    received = lax.all_to_all(parts.reshape(blocks, 2 * rows, size), ("chip", "core"), 0, 0, tiled=True)
    inner, growth = call(
        inner_kernel,
        (struct((positions, head_lanes), f32), struct((positions, heads), f32)),
        queries, keys, values, log_decay,
    )
    befores, others = call(
        state_scan_kernel, (struct((blocks, rows, size), bf16), pltpu.HBM((blocks, size), f32)),
        received, in_vmem(prior), in_specs=[vmem] * 2,
    )
    state = lax.all_to_all(befores, ("chip", "core"), 0, 0, tiled=True).reshape(heads * size, size)

    row = struct((positions, share), bf16)
    top, bottom, r3, r3m, r2, r2m, r1, r1m, r0 = call(
        functools.partial(project_kernel, heads=heads, order=(4, 3, -3, 2, -2, 1, -1, 0)),
        (struct((positions // 2, share), bf16),) * 2 + (row,) * 6 + (struct((positions, share), f32),),
        place, queries, stays(inner), stays(growth), state, stays(gate_input), stays(attn_gain.reshape(1, head_lanes)),
        in_vmem(out_weight),
        in_specs=[smem] + [vmem] * 7,
    )
    middle = positions // 2
    gain_rows = moe_gain.reshape(peers, 1, share)
    up, down, layer_input, ids, gain_rows = tied((moved(top, 1), moved(bottom, -1), layer_input, ids, gain_rows))
    up = jnp.concatenate([plus(up, r3[:middle]), r3[middle:]])
    down = jnp.concatenate([r3m[:middle], plus(down, r3m[middle:])])
    up, down = tied((moved(up, 1), moved(down, -1)))
    up, down = tied((moved(plus(up, r2), 1), moved(plus(down, r2m), -1)))
    up, down = tied((moved(plus(up, r1), 1), moved(plus(down, r1m), -1)))
    small = pltpu.CompilerParams(vmem_limit_bytes=8 << 20)
    scale, layer, chosen = pl.pallas_call(
        functools.partial(prepare_kernel, experts=experts, capacity=capacity),
        out_shape=(pltpu.VMEM((1, share), f32), pltpu.VMEM((positions, share), bf16), pltpu.VMEM((slots, positions), bf16)),
        in_specs=[smem] + [vmem] * 3,
        out_specs=(vmem,) * 3,
        compiler_params=small,
    )(place, stays(gain_rows), stays(layer_input), stays(ids))
    chosen = in_vmem(chosen)
    outgoing, hidden = pl.pallas_call(
        dispatch_kernel,
        out_shape=(struct((slots, share), bf16), pltpu.VMEM((positions, share), f32)),
        in_specs=[vmem] * 6,
        out_specs=(vmem,) * 2,
        compiler_params=small,
    )(up, down, r0, in_vmem(scale), in_vmem(layer), chosen)

    arrived = lax.all_to_all(outgoing.reshape(chips, capacity, share), "chip", 0, 0, tiled=True)
    held = chips * capacity
    half = held // 2
    arrived = arrived.reshape(held, share)
    here = (arrived[:half], arrived[half:])
    here, weights = lax.optimization_barrier((here, weights))

    order = (0, 1, -1, 2, -2, 3, -3, 4)
    parts = order[:2], order[2:4], order[4:6], order[6:]
    far, near = (4, 3, -3), (2, -2, 1, -1, 0)
    units = cores * share
    work = held * width * units
    params = pltpu.CompilerParams(vmem_limit_bytes=LIMIT)
    gain, router = stays(moe_gain.reshape(peers, 1, share)), stays(router.T)
    others = stays(others)
    sides, downs = [stays(weight) for weight in weights[:4]], [stays(weight) for weight in weights[4:]]

    def cost(flops, size):
        return pl.CostEstimate(flops=flops, bytes_accessed=size, transcendentals=0)

    def kept(kernel, shapes, flops, specs, args, scratch=(), **options):
        return pl.pallas_call(
            functools.partial(kernel, **options),
            out_shape=shapes,
            in_specs=specs + [vmem] * (len(args) - len(specs)),
            out_specs=(vmem,) * len(shapes),
            scratch_shapes=scratch,
            compiler_params=params,
            cost_estimate=cost(flops, 4 << 20),
        )(*args)

    sums = (struct((half, 2 * units), f32), struct((half, 128), f32)) * 2
    wide = pltpu.VMEM((width // 4, 2 * units), bf16)
    semaphores = [pltpu.SemaphoreType.DMA((8,)), pltpu.SemaphoreType.DMA((2 * peers,))]
    got = ({0: here[0]}, {0: here[1]})
    for distance in (1, 2, 3):
        moving = [(moved(mine[1 - distance], 1), moved(mine[distance - 1], -1)) for mine in got]
        chunks = [mine[k] for mine in got for k in parts[distance - 2]] if distance > 1 else []
        if distance == 1:
            loaded = kept(
                first_load_kernel,
                (wide, pltpu.VMEM((units, len(far) * share), bf16), pltpu.VMEM(gain.shape, f32),
                 pltpu.VMEM(router.shape, bf16), pltpu.VMEM(others.shape, f32)),
                0, [smem] + [vmem] * 3 + [hbm] * 6, [place, gain, router, others, *sides, *downs], semaphores,
                rows=parts[0], columns=far,
            )
        elif distance == 2:
            *totals, gate_up, down_near = loaded = kept(
                pair_sums_kernel, sums + (wide, pltpu.VMEM((units, len(near) * share), bf16)), work,
                [smem] + [vmem] * 3 + [hbm] * 6, [place, inverse, router, in_vmem(gate_up), *sides, *downs, *chunks], semaphores,
                order=parts[0], rows=parts[1], columns=near, fresh=True,
            )
        else:
            *totals, gate_up = loaded = kept(
                pair_sums_kernel, sums + (wide,), work,
                [smem] + [vmem] * 3 + [hbm] * 6, [place, inverse, router, in_vmem(gate_up), *sides, *downs, *chunks, *totals],
                semaphores, order=parts[1], rows=parts[2], columns=(), fresh=False,
            )
        moving[0], loaded = tied((moving[0], loaded))
        if distance == 1:
            gate_up, down_far, *small = loaded
            inverse, router, others = [in_vmem(x) for x in small]
        elif distance == 2:
            *totals, gate_up, down_near = loaded
        else:
            *totals, gate_up = loaded
        for mine, (up, down_way) in zip(got, moving):
            mine[-distance], mine[distance] = lax.optimization_barrier((up, down_way))
    got[0][4], got[1][4] = moved(got[0][-3], 1), moved(got[1][3], -1)
    *totals, gate_up_last = kept(
        pair_sums_kernel, sums + (wide,), work, [smem] + [vmem] * 3 + [hbm] * 6,
        [place, inverse, router, in_vmem(gate_up), *sides, *downs, *[mine[k] for mine in got for k in parts[2]], *totals],
        semaphores, order=parts[2], rows=parts[3], columns=(), fresh=False,
    )
    gate_up_last, down_far, down_near = in_vmem(gate_up_last), in_vmem(down_far), in_vmem(down_near)
    piece = struct((half, share), bf16)
    ready = [
        kept(
            far_products_kernel, (piece,) * len(far) + (struct((half, units), bf16),), work, [smem],
            [place, inverse, router, gate_up_last, down_far, others, *totals[2 * h:2 * h + 2], *[got[h][k] for k in parts[3]]],
            order=parts[3], h=h, far=len(far), width=width, capacity=capacity,
        )
        for h in range(2)
    ]
    (a4, a3, a3m, active_a), (b4, b3, b3m, active_b) = ready

    a_up, a_down = tied((moved(a4, 1), moved(a3m, -1)))
    b_up, b_down = tied((moved(b3, 1), moved(b4, -1)))
    a2, b2, a2m, b2m, a1, b1, a1m, b1m, a0, b0 = kept(
        near_products_kernel, (piece,) * (2 * len(near)), work, [], [active_a, active_b, down_near], near=len(near))
    a_up, a_down = tied((moved(plus(a_up, a3), 1), moved(plus(a_down, a2m), -1)))
    b_up, b_down = tied((moved(plus(b_up, b2), 1), moved(plus(b_down, b3m), -1)))
    a_up, a_down = tied((moved(plus(a_up, a2), 1), moved(plus(a_down, a1m), -1)))
    b_up, b_down = tied((moved(plus(b_up, b1), 1), moved(plus(b_down, b2m), -1)))
    a_up, b_down = moved(plus(a_up, a1), 1), moved(plus(b_down, b1m), -1)
    summed = jnp.concatenate([plus(a0, a_up, a_down), plus(b0, b_up, b_down)])
    returned = lax.all_to_all(summed.reshape(chips, capacity, share), "chip", 0, 0, tiled=True)
    return call(
        combine_kernel, struct((positions, share), bf16),
        returned.reshape(slots, share), in_vmem(hidden), chosen, in_specs=[vmem] * 3,
    )


def solution(mesh):
    cx, tp = mesh.devices.shape
    fine = Mesh(mesh.devices.reshape(cx // 2, 2, tp), ("chip", "core", "tp"))
    both = ("chip", "core")
    placed = (
        P(both, "tp"), P(both, "tp"), P(both, "tp"), P(both, "tp"), P(both, "tp"),
        P("tp", both), P("tp", None, None), P("tp"), P("tp", None), P(), P(),
        P(both, None), P(both, None, "tp"), P(both, None, "tp"), P(both, "tp", None),
    )
    return jax.shard_map(shards, mesh=fine, in_specs=placed, out_specs=P(both, "tp"), check_vma=False)
```

```python
import functools

import jax
import jax.numpy as jnp
from jax import lax
from jax.experimental import pallas as pl
from jax.experimental.pallas import tpu as pltpu
from jax.sharding import Mesh, PartitionSpec as P

epsilon = 1e-06
exact = lax.Precision.HIGHEST
bf16 = jnp.bfloat16
f32 = jnp.float32
LIMIT = 30 << 20


def mm(a, b, contract_a=1, contract_b=0, precision=None):
    return lax.dot_general(
        a, b, (((contract_a,), (contract_b,)), ((), ())),
        precision=precision, preferred_element_type=f32,
    )


def lower_triangle(n, strict=False):
    rows = lax.broadcasted_iota(jnp.int32, (n, n), 0)
    cols = lax.broadcasted_iota(jnp.int32, (n, n), 1)
    return (rows > cols) if strict else (rows >= cols)


def block_state_kernel(keys, values, log_decay, ids, out, *, experts, capacity):
    heads, positions = log_decay.shape
    size = keys.shape[1] // heads
    per_head = out.shape[1]
    rows = size // per_head
    until = mm(lower_triangle(positions).astype(f32), log_decay[...], 1, 1, exact)
    first, second = slots_of(ids[...], experts, capacity)
    chosen = [jnp.broadcast_to(ids[k:k + 1, :].astype(f32), (8, positions)).astype(bf16) for k in range(2)]
    others = mm(chosen[1], first.astype(bf16), 1, 1) + mm(chosen[0], second.astype(bf16), 1, 1)
    for h in range(heads):
        lanes = slice(h * size, (h + 1) * size)
        total = until[positions - 1:positions, h:h + 1]
        trailing = jnp.exp(total - until[:, h:h + 1])
        weighted = (keys[:, lanes].astype(f32) * trailing).astype(bf16)
        state = mm(weighted, values[:, lanes], 0, 0)
        out[h, :, :rows, :] = state.astype(bf16).reshape(per_head, rows, size)
        high = total.astype(bf16).astype(f32)
        middle = (total - high).astype(bf16).astype(f32)
        low = total - high - middle
        row = lax.broadcasted_iota(jnp.int32, (rows, size), 0)
        terms = jnp.where(row == 0, high, jnp.where(row == 1, middle, jnp.where(row == 2, low, 0.0)))
        terms = jnp.where(row == 3, others[0:1, lanes], terms)
        out[h, :, rows:, :] = jnp.broadcast_to(terms.astype(bf16), (per_head, rows, size))


def load_part_kernel(part, source, target, sem):
    rows = target.shape[0]
    copy = pltpu.make_async_copy(source.at[pl.ds(pl.multiple_of(part[0] * rows, rows), rows)], target, sem)
    copy.start()
    copy.wait()


def state_scan_kernel(received, prior, out, others):
    blocks, rows, _ = out.shape
    state = prior[...]
    for k in range(blocks):
        out[k] = state.astype(bf16)
        terms = received[k, rows:, :].astype(f32)
        total = terms[0:1] + terms[1:2] + terms[2:3]
        state = jnp.exp(total) * state + received[k, :rows, :].astype(f32)
        others[k:k + 1, :] = terms[3:4]


def inner_kernel(queries, keys, values, log_decay, out, growth):
    heads, positions = log_decay.shape
    size = queries.shape[1] // heads
    causal = lower_triangle(positions)
    until = mm(causal.astype(f32), log_decay[...], 1, 1, exact)
    until_row = mm(log_decay[...], causal.astype(f32), 1, 1, exact)
    for h in range(heads):
        lanes = slice(h * size, (h + 1) * size)
        spread = until[:, h:h + 1] - until_row[h:h + 1, :]
        weights = jnp.where(causal, jnp.exp(jnp.where(causal, spread, 0.0)), 0.0)
        scores = mm(queries[:, lanes], keys[:, lanes], 1, 1) * weights
        out[:, lanes] = mm(scores.astype(bf16), values[:, lanes])
    growth[...] = jnp.exp(until)


def project_kernel(queries, inner, growth, state, gate_input, gain, weight, out, *, heads):
    size = queries.shape[1] // heads
    normed = []
    for h in range(heads):
        lanes = slice(h * size, (h + 1) * size)
        carried = mm(queries[:, lanes], state[lanes, :])
        attended = inner[:, lanes] + growth[:, h:h + 1] * carried
        squares = jnp.mean(attended * attended, axis=1, keepdims=True)
        gating = jax.nn.sigmoid(gate_input[:, lanes].astype(f32))
        normed.append((attended * lax.rsqrt(squares + epsilon) * gain[:, lanes] * gating).astype(bf16))
    normed = jnp.concatenate(normed, axis=1)
    peers, _, width = out.shape
    for c in range(0, peers, 2):
        product = mm(normed, weight[:, c * width:(c + 2) * width])
        out[c] = product[:, :width].astype(bf16)
        out[c + 1] = product[:, width:].astype(bf16)


def slots_of(ids, experts, capacity):
    positions = ids.shape[1]
    expert = lax.broadcasted_iota(jnp.int32, (experts, positions), 0)
    choices = [(ids[k:k + 1, :] == expert).astype(f32) for k in range(2)]
    earlier = mm((choices[0] + choices[1]).astype(bf16), lower_triangle(positions, True).astype(bf16), 1, 1)
    slot = lax.broadcasted_iota(jnp.int32, (experts * capacity, positions), 0)
    found = []
    for k, choice in enumerate(choices):
        position = jnp.sum(choice * earlier, axis=0, keepdims=True).astype(jnp.int32)
        found.append((slot == ids[k:k + 1, :] * capacity + position).astype(f32))
    return found


def prepare_kernel(place, gain, layer_input, ids, scale, layer, chosen, *, experts, capacity):
    scale[...] = gain[place[0]]
    layer[...] = layer_input[...]
    first, second = slots_of(ids[...], experts, capacity)
    chosen[...] = (first + second).astype(bf16)


def dispatch_kernel(partial, scale, layer, chosen, outgoing, hidden):
    total = layer[...].astype(f32)
    for k in range(partial.shape[0]):
        total += partial[k].astype(f32)
    hidden[...] = total
    outgoing[...] = mm(chosen[...], (total * scale[...]).astype(bf16)).astype(bf16)


def fetch(pairs, sems):
    copies = [pltpu.make_async_copy(source, target, sems.at[k]) for k, (source, target) in enumerate(pairs)]
    for copy in copies:
        copy.start()
    return copies


def load_kernel(source, target, sems):
    parts = sems.shape[0]
    rows = source.shape[0] // parts
    pairs = [(source.at[pl.ds(k * rows, rows)], target.at[pl.ds(k * rows, rows)]) for k in range(parts)]
    for copy in fetch(pairs, sems):
        copy.wait()


def row_copies(place, weights, gate_up, sems, order, peers):
    depth, share = weights[0].shape
    rows = depth // peers
    copies = []
    for c, distance in enumerate(order):
        start = pl.multiple_of(lax.rem(place[0] + distance + peers, peers) * rows, rows)
        for k, weight in enumerate(weights):
            target = gate_up.at[pl.ds(c * rows, rows), pl.ds(k * share, share)]
            copies.append(pltpu.make_async_copy(weight.at[pl.ds(start, rows)], target, sems.at[c * len(weights) + k]))
    return copies


def column_copies(place, weights, down, sems, order, peers):
    share, depth = weights[0].shape
    width = depth // peers
    copies = []
    for c, distance in enumerate(order):
        start = pl.multiple_of(lax.rem(place[0] + distance + peers, peers) * width, width)
        for k, weight in enumerate(weights):
            target = down.at[pl.ds(k * share, share), pl.ds(c * width, width)]
            copies.append(pltpu.make_async_copy(weight.at[:, pl.ds(start, width)], target, sems.at[c * len(weights) + k]))
    return copies


def gate_up_sums(place, pieces, inverse, router, gate_up, order):
    peers, _, width = inverse.shape
    experts = router.shape[0]
    squares, logits = 0.0, 0.0
    for k, piece in enumerate(pieces):
        group = lax.rem(place[0] + order[k] + peers, peers)
        wide = piece.astype(f32) * inverse[group]
        squares += jnp.sum(wide * wide, axis=1, keepdims=True)
        logits += mm(piece, router[:, pl.ds(pl.multiple_of(group * width, width), width)], 1, 1)
    total = mm(jnp.concatenate(pieces, axis=1), gate_up[...])
    beside = jnp.concatenate([logits, jnp.broadcast_to(squares, (logits.shape[0], 128 - experts))], axis=1)
    return total, beside


def pair_sums_kernel(place, inverse, router, gate_up, *refs, order, rows, columns, fresh):
    weights, downs, chunks = refs[:4], refs[4:6], refs[6:10]
    befores, outs = ((), refs[10:]) if fresh else (refs[10:14], refs[14:])
    peers = inverse.shape[0]
    totals, loaded, sems = outs[:4], outs[4:-2], outs[-2:]
    copies = row_copies(place, weights, loaded[0], sems[0], rows, peers)
    if columns:
        copies += column_copies(place, downs, loaded[1], sems[1], columns, peers)
    for copy in copies:
        copy.start()
    for h in range(2):
        found = gate_up_sums(place, [ref[...] for ref in chunks[2 * h:2 * h + 2]], inverse, router, gate_up, order)
        for k in range(2):
            totals[2 * h + k][...] = found[k] if fresh else befores[2 * h + k][...] + found[k]
    for copy in copies:
        copy.wait()


def first_load_kernel(place, gain, router, others, *refs, rows, columns):
    weights, downs, (gate_up, down, inverse, router_out, others_out, *sems) = refs[:4], refs[4:6], refs[6:]
    peers = gain.shape[0]
    copies = row_copies(place, weights, gate_up, sems[0], rows, peers)
    copies += column_copies(place, downs, down, sems[1], columns, peers)
    for copy in copies:
        copy.start()
    inverse[...] = 1.0 / gain[...]
    router_out[...] = router[...]
    others_out[...] = others[...]
    for copy in copies:
        copy.wait()


def mixing_of(place, others, logits, h, capacity):
    rows, experts = logits.shape
    blocks, lanes = others.shape
    row = lax.broadcasted_iota(jnp.int32, (rows, blocks), 0)
    block = lax.broadcasted_iota(jnp.int32, (rows, blocks), 1)
    sender = 2 * (lax.div(row, capacity) + h * (rows // capacity)) + place[1]
    from_sender = mm((sender == block).astype(bf16), others[...].astype(bf16))
    row = lax.broadcasted_iota(jnp.int32, (rows, lanes), 0)
    lane = lax.broadcasted_iota(jnp.int32, (rows, lanes), 1)
    own_lane = lax.rem(place[2], lanes // capacity) * capacity + lax.rem(row, capacity)
    other = jnp.sum(jnp.where(lane == own_lane, from_sender, 0.0), axis=1, keepdims=True).astype(jnp.int32)
    expert = lax.broadcasted_iota(jnp.int32, (rows, experts), 1)
    sign = (expert == place[2]).astype(f32) - (expert == other).astype(f32)
    return jax.nn.sigmoid(jnp.sum(sign * logits, axis=1, keepdims=True))


def products(activated, down, start, count, share):
    found = []
    for c in range(start, start + count, 2):
        both = min(2, start + count - c)
        product = mm(activated, down[:, c * share:(c + both) * share])
        found += [product[:, k * share:(k + 1) * share].astype(bf16) for k in range(both)]
    return found


def far_products_kernel(
    place, inverse, router, gate_up, down, others, total, beside, *refs, order, h, far, width, capacity
):
    count = len(order)
    outs, activated = refs[count:-1], refs[-1]
    units = activated.shape[1]
    product, sums = gate_up_sums(place, [ref[...] for ref in refs[:count]], inverse, router, gate_up, order)
    sums += beside[...]
    experts = router.shape[0]
    scale = lax.rsqrt(sums[:, experts:experts + 1] / width + epsilon)
    mixing = mixing_of(place, others, sums[:, :experts] * scale, h, capacity)
    both = (total[...] + product) * scale
    gated = both[:, :units]
    active = (gated * jax.nn.sigmoid(gated) * both[:, units:] * mixing).astype(bf16)
    activated[...] = active
    for k, piece in enumerate(products(active, down, 0, far, outs[0].shape[1])):
        outs[k][...] = piece


def near_products_kernel(active_a, active_b, down, *outs, near):
    for h, active in enumerate((active_a, active_b)):
        for k, piece in enumerate(products(active[...], down, 0, near, outs[0].shape[1])):
            outs[2 * k + h][...] = piece


def combine_kernel(returned, hidden, chosen, out):
    out[...] = (hidden[...] + mm(chosen[...], returned[...], 0, 0)).astype(out.dtype)


def call(kernel, shapes, *args, **kwargs):
    return pl.pallas_call(
        kernel,
        out_shape=shapes,
        compiler_params=pltpu.CompilerParams(vmem_limit_bytes=LIMIT),
        **kwargs,
    )(*args)


def stays(x):
    return pltpu.with_memory_space_constraint(x, pltpu.HBM)


def in_vmem(x):
    return pltpu.with_memory_space_constraint(x, pltpu.VMEM)


def whole(shape):
    return pl.BlockSpec(shape, lambda *_: (0,) * len(shape))


def shards(
    layer_input, queries, keys, values, gate_input, log_decay, prior_state, attn_gain,
    out_weight, moe_gain, router, expert_ids, w_gate, w_up, w_down,
):
    struct = jax.ShapeDtypeStruct
    positions, head_lanes = queries.shape
    heads, size, _ = prior_state.shape
    chips, cores, peers = lax.axis_size("chip"), lax.axis_size("core"), lax.axis_size("tp")
    blocks = chips * cores
    width = out_weight.shape[1]
    share = layer_input.shape[1]
    experts = router.shape[1]
    capacity = 8 * positions // blocks
    slots = experts * capacity
    core, chip, tp = lax.axis_index("core"), lax.axis_index("chip"), lax.axis_index("tp")
    cx = chip * cores + core
    place = jnp.stack([tp, core, chip])
    place, cx, tp, keys = lax.optimization_barrier((place, cx, tp, keys))

    ids = stays(expert_ids.T)
    queries, keys, values, log_decay = stays(queries), stays(keys), stays(values), stays(log_decay)
    vmem = pl.BlockSpec(memory_space=pltpu.VMEM)
    smem = pl.BlockSpec(memory_space=pltpu.SMEM)
    tied = lax.optimization_barrier

    def moved(piece, step):
        return lax.ppermute(piece, "tp", [(i, (i + step) % peers) for i in range(peers)])

    def plus(*pieces):
        return sum(piece.astype(f32) for piece in pieces).astype(bf16)
    hbm = pl.BlockSpec(memory_space=pl.ANY)

    swap = [(0, 1), (1, 0)]
    weights = []
    for weight in (w_gate[0], w_up[0], w_down[0]):
        weights += [weight, lax.ppermute(weight, "core", swap)]

    rows = heads * size // blocks
    parts = call(
        functools.partial(block_state_kernel, experts=experts, capacity=capacity),
        struct((heads, size // rows, 2 * rows, size), bf16), keys, values, log_decay, ids,
    )
    parts, out_weight, prior_state = lax.optimization_barrier((parts, out_weight, prior_state))
    prior = pl.pallas_call(
        load_part_kernel,
        out_shape=pltpu.VMEM((rows, size), f32),
        in_specs=[smem, hbm],
        out_specs=vmem,
        scratch_shapes=[pltpu.SemaphoreType.DMA],
        compiler_params=pltpu.CompilerParams(vmem_limit_bytes=4 << 20),
        cost_estimate=pl.CostEstimate(flops=0, bytes_accessed=1 << 20, transcendentals=0),
    )(cx.reshape(1), stays(prior_state.reshape(heads * size, size)))
    out_weight = pl.pallas_call(
        load_kernel,
        out_shape=pltpu.VMEM((head_lanes, width), bf16),
        in_specs=[hbm],
        out_specs=vmem,
        scratch_shapes=[pltpu.SemaphoreType.DMA((4,))],
        compiler_params=pltpu.CompilerParams(vmem_limit_bytes=4 << 20),
        cost_estimate=pl.CostEstimate(flops=0, bytes_accessed=2 * head_lanes * width, transcendentals=0),
    )(stays(out_weight))
    received = lax.all_to_all(parts.reshape(blocks, 2 * rows, size), ("chip", "core"), 0, 0, tiled=True)
    inner, growth = call(
        inner_kernel,
        (struct((positions, head_lanes), f32), struct((positions, heads), f32)),
        queries, keys, values, log_decay,
    )
    befores, others = call(
        state_scan_kernel, (struct((blocks, rows, size), bf16), pltpu.HBM((blocks, size), f32)),
        received, in_vmem(prior), in_specs=[vmem] * 2,
    )
    state = lax.all_to_all(befores, ("chip", "core"), 0, 0, tiled=True).reshape(heads * size, size)

    partial = call(
        functools.partial(project_kernel, heads=heads), struct((peers, positions, share), bf16),
        queries, stays(inner), stays(growth), state, stays(gate_input), stays(attn_gain.reshape(1, head_lanes)),
        in_vmem(out_weight), in_specs=[vmem] * 7,
    )
    gain_rows = moe_gain.reshape(peers, 1, share)
    partial, layer_input, ids, gain_rows = tied((partial, layer_input, ids, gain_rows))
    partial = lax.all_to_all(partial, "tp", 0, 0, tiled=True)
    small = pltpu.CompilerParams(vmem_limit_bytes=8 << 20)
    scale, layer, chosen = pl.pallas_call(
        functools.partial(prepare_kernel, experts=experts, capacity=capacity),
        out_shape=(pltpu.VMEM((1, share), f32), pltpu.VMEM((positions, share), bf16), pltpu.VMEM((slots, positions), bf16)),
        in_specs=[smem] + [vmem] * 3,
        out_specs=(vmem,) * 3,
        compiler_params=small,
    )(place, stays(gain_rows), stays(layer_input), stays(ids))
    chosen = in_vmem(chosen)
    outgoing, hidden = pl.pallas_call(
        dispatch_kernel,
        out_shape=(struct((slots, share), bf16), pltpu.VMEM((positions, share), f32)),
        in_specs=[vmem] * 4,
        out_specs=(vmem,) * 2,
        compiler_params=small,
    )(partial, in_vmem(scale), in_vmem(layer), chosen)

    arrived = lax.all_to_all(outgoing.reshape(chips, capacity, share), "chip", 0, 0, tiled=True)
    held = chips * capacity
    half = held // 2
    arrived = arrived.reshape(held, share)
    here = (arrived[:half], arrived[half:])
    here, weights = lax.optimization_barrier((here, weights))

    order = (0, 1, -1, 2, -2, 3, -3, 4)
    parts = order[:2], order[2:4], order[4:6], order[6:]
    far, near = (4, 3, -3), (2, -2, 1, -1, 0)
    units = cores * share
    work = held * width * units
    params = pltpu.CompilerParams(vmem_limit_bytes=LIMIT)
    gain, router = stays(moe_gain.reshape(peers, 1, share)), stays(router.T)
    others = stays(others)
    sides, downs = [stays(weight) for weight in weights[:4]], [stays(weight) for weight in weights[4:]]

    def cost(flops, size):
        return pl.CostEstimate(flops=flops, bytes_accessed=size, transcendentals=0)

    def kept(kernel, shapes, flops, specs, args, scratch=(), **options):
        return pl.pallas_call(
            functools.partial(kernel, **options),
            out_shape=shapes,
            in_specs=specs + [vmem] * (len(args) - len(specs)),
            out_specs=(vmem,) * len(shapes),
            scratch_shapes=scratch,
            compiler_params=params,
            cost_estimate=cost(flops, 4 << 20),
        )(*args)

    sums = (struct((half, 2 * units), f32), struct((half, 128), f32)) * 2
    wide = pltpu.VMEM((width // 4, 2 * units), bf16)
    semaphores = [pltpu.SemaphoreType.DMA((8,)), pltpu.SemaphoreType.DMA((2 * peers,))]
    got = ({0: here[0]}, {0: here[1]})
    for distance in (1, 2, 3):
        moving = [(moved(mine[1 - distance], 1), moved(mine[distance - 1], -1)) for mine in got]
        chunks = [mine[k] for mine in got for k in parts[distance - 2]] if distance > 1 else []
        if distance == 1:
            loaded = kept(
                first_load_kernel,
                (wide, pltpu.VMEM((units, len(far) * share), bf16), pltpu.VMEM(gain.shape, f32),
                 pltpu.VMEM(router.shape, bf16), pltpu.VMEM(others.shape, f32)),
                0, [smem] + [vmem] * 3 + [hbm] * 6, [place, gain, router, others, *sides, *downs], semaphores,
                rows=parts[0], columns=far,
            )
        elif distance == 2:
            *totals, gate_up, down_near = loaded = kept(
                pair_sums_kernel, sums + (wide, pltpu.VMEM((units, len(near) * share), bf16)), work,
                [smem] + [vmem] * 3 + [hbm] * 6, [place, inverse, router, in_vmem(gate_up), *sides, *downs, *chunks], semaphores,
                order=parts[0], rows=parts[1], columns=near, fresh=True,
            )
        else:
            *totals, gate_up = loaded = kept(
                pair_sums_kernel, sums + (wide,), work,
                [smem] + [vmem] * 3 + [hbm] * 6, [place, inverse, router, in_vmem(gate_up), *sides, *downs, *chunks, *totals],
                semaphores, order=parts[1], rows=parts[2], columns=(), fresh=False,
            )
        moving[0], loaded = tied((moving[0], loaded))
        if distance == 1:
            gate_up, down_far, *small = loaded
            inverse, router, others = [in_vmem(x) for x in small]
        elif distance == 2:
            *totals, gate_up, down_near = loaded
        else:
            *totals, gate_up = loaded
        for mine, (up, down_way) in zip(got, moving):
            mine[-distance], mine[distance] = lax.optimization_barrier((up, down_way))
    got[0][4], got[1][4] = moved(got[0][-3], 1), moved(got[1][3], -1)
    *totals, gate_up_last = kept(
        pair_sums_kernel, sums + (wide,), work, [smem] + [vmem] * 3 + [hbm] * 6,
        [place, inverse, router, in_vmem(gate_up), *sides, *downs, *[mine[k] for mine in got for k in parts[2]], *totals],
        semaphores, order=parts[2], rows=parts[3], columns=(), fresh=False,
    )
    gate_up_last, down_far, down_near = in_vmem(gate_up_last), in_vmem(down_far), in_vmem(down_near)
    piece = struct((half, share), bf16)
    ready = [
        kept(
            far_products_kernel, (piece,) * len(far) + (struct((half, units), bf16),), work, [smem],
            [place, inverse, router, gate_up_last, down_far, others, *totals[2 * h:2 * h + 2], *[got[h][k] for k in parts[3]]],
            order=parts[3], h=h, far=len(far), width=width, capacity=capacity,
        )
        for h in range(2)
    ]
    (a4, a3, a3m, active_a), (b4, b3, b3m, active_b) = ready

    a_up, a_down = tied((moved(a4, 1), moved(a3m, -1)))
    b_up, b_down = tied((moved(b3, 1), moved(b4, -1)))
    a2, b2, a2m, b2m, a1, b1, a1m, b1m, a0, b0 = kept(
        near_products_kernel, (piece,) * (2 * len(near)), work, [], [active_a, active_b, down_near], near=len(near))
    a_up, a_down = tied((moved(plus(a_up, a3), 1), moved(plus(a_down, a2m), -1)))
    b_up, b_down = tied((moved(plus(b_up, b2), 1), moved(plus(b_down, b3m), -1)))
    a_up, a_down = tied((moved(plus(a_up, a2), 1), moved(plus(a_down, a1m), -1)))
    b_up, b_down = tied((moved(plus(b_up, b1), 1), moved(plus(b_down, b2m), -1)))
    a_up, b_down = moved(plus(a_up, a1), 1), moved(plus(b_down, b1m), -1)
    summed = jnp.concatenate([plus(a0, a_up, a_down), plus(b0, b_up, b_down)])
    returned = lax.all_to_all(summed.reshape(chips, capacity, share), "chip", 0, 0, tiled=True)
    return call(
        combine_kernel, struct((positions, share), bf16),
        returned.reshape(slots, share), in_vmem(hidden), chosen, in_specs=[vmem] * 3,
    )


def solution(mesh):
    cx, tp = mesh.devices.shape
    fine = Mesh(mesh.devices.reshape(cx // 2, 2, tp), ("chip", "core", "tp"))
    both = ("chip", "core")
    placed = (
        P(both, "tp"), P(both, "tp"), P(both, "tp"), P(both, "tp"), P(both, "tp"),
        P("tp", both), P("tp", None, None), P("tp"), P("tp", None), P(), P(),
        P(both, None), P(both, None, "tp"), P(both, None, "tp"), P(both, "tp", None),
    )
    return jax.shard_map(shards, mesh=fine, in_specs=placed, out_specs=P(both, "tp"), check_vma=False)
```

```python
import functools

import jax
import jax.numpy as jnp
from jax import lax
from jax.experimental import pallas as pl
from jax.experimental.pallas import tpu as pltpu
from jax.sharding import Mesh, PartitionSpec as P

epsilon = 1e-06
exact = lax.Precision.HIGHEST
bf16 = jnp.bfloat16
f32 = jnp.float32
LIMIT = 30 << 20


def mm(a, b, contract_a=1, contract_b=0, precision=None):
    return lax.dot_general(
        a, b, (((contract_a,), (contract_b,)), ((), ())),
        precision=precision, preferred_element_type=f32,
    )


def lower_triangle(n, strict=False):
    rows = lax.broadcasted_iota(jnp.int32, (n, n), 0)
    cols = lax.broadcasted_iota(jnp.int32, (n, n), 1)
    return (rows > cols) if strict else (rows >= cols)


def block_state_kernel(keys, values, log_decay, ids, out, *, experts, capacity):
    heads, positions = log_decay.shape
    size = keys.shape[1] // heads
    per_head = out.shape[1]
    rows = size // per_head
    until = mm(lower_triangle(positions).astype(f32), log_decay[...], 1, 1, exact)
    first, second = slots_of(ids[...], experts, capacity)
    chosen = [jnp.broadcast_to(ids[k:k + 1, :].astype(f32), (8, positions)).astype(bf16) for k in range(2)]
    others = mm(chosen[1], first.astype(bf16), 1, 1) + mm(chosen[0], second.astype(bf16), 1, 1)
    for h in range(heads):
        lanes = slice(h * size, (h + 1) * size)
        total = until[positions - 1:positions, h:h + 1]
        trailing = jnp.exp(total - until[:, h:h + 1])
        weighted = (keys[:, lanes].astype(f32) * trailing).astype(bf16)
        state = mm(weighted, values[:, lanes], 0, 0)
        out[h, :, :rows, :] = state.astype(bf16).reshape(per_head, rows, size)
        high = total.astype(bf16).astype(f32)
        middle = (total - high).astype(bf16).astype(f32)
        low = total - high - middle
        row = lax.broadcasted_iota(jnp.int32, (rows, size), 0)
        terms = jnp.where(row == 0, high, jnp.where(row == 1, middle, jnp.where(row == 2, low, 0.0)))
        terms = jnp.where(row == 3, others[0:1, lanes], terms)
        out[h, :, rows:, :] = jnp.broadcast_to(terms.astype(bf16), (per_head, rows, size))


def load_part_kernel(part, source, target, sem):
    rows = target.shape[0]
    copy = pltpu.make_async_copy(source.at[pl.ds(pl.multiple_of(part[0] * rows, rows), rows)], target, sem)
    copy.start()
    copy.wait()


def state_scan_kernel(received, prior, out, others):
    blocks, rows, _ = out.shape
    state = prior[...]
    for k in range(blocks):
        out[k] = state.astype(bf16)
        terms = received[k, rows:, :].astype(f32)
        total = terms[0:1] + terms[1:2] + terms[2:3]
        state = jnp.exp(total) * state + received[k, :rows, :].astype(f32)
        others[k:k + 1, :] = terms[3:4]


def inner_kernel(queries, keys, values, log_decay, out, growth):
    heads, positions = log_decay.shape
    size = queries.shape[1] // heads
    causal = lower_triangle(positions)
    until = mm(causal.astype(f32), log_decay[...], 1, 1, exact)
    until_row = mm(log_decay[...], causal.astype(f32), 1, 1, exact)
    for h in range(heads):
        lanes = slice(h * size, (h + 1) * size)
        spread = until[:, h:h + 1] - until_row[h:h + 1, :]
        weights = jnp.where(causal, jnp.exp(jnp.where(causal, spread, 0.0)), 0.0)
        scores = mm(queries[:, lanes], keys[:, lanes], 1, 1) * weights
        out[:, lanes] = mm(scores.astype(bf16), values[:, lanes])
    growth[...] = jnp.exp(until)


def project_kernel(queries, inner, growth, state, gate_input, gain, weight, out, *, heads):
    size = queries.shape[1] // heads
    normed = []
    for h in range(heads):
        lanes = slice(h * size, (h + 1) * size)
        carried = mm(queries[:, lanes], state[lanes, :])
        attended = inner[:, lanes] + growth[:, h:h + 1] * carried
        squares = jnp.mean(attended * attended, axis=1, keepdims=True)
        gating = jax.nn.sigmoid(gate_input[:, lanes].astype(f32))
        normed.append((attended * lax.rsqrt(squares + epsilon) * gain[:, lanes] * gating).astype(bf16))
    normed = jnp.concatenate(normed, axis=1)
    peers, _, width = out.shape
    for c in range(0, peers, 2):
        product = mm(normed, weight[:, c * width:(c + 2) * width])
        out[c] = product[:, :width].astype(bf16)
        out[c + 1] = product[:, width:].astype(bf16)


def slots_of(ids, experts, capacity):
    positions = ids.shape[1]
    expert = lax.broadcasted_iota(jnp.int32, (experts, positions), 0)
    choices = [(ids[k:k + 1, :] == expert).astype(f32) for k in range(2)]
    earlier = mm((choices[0] + choices[1]).astype(bf16), lower_triangle(positions, True).astype(bf16), 1, 1)
    slot = lax.broadcasted_iota(jnp.int32, (experts * capacity, positions), 0)
    found = []
    for k, choice in enumerate(choices):
        position = jnp.sum(choice * earlier, axis=0, keepdims=True).astype(jnp.int32)
        found.append((slot == ids[k:k + 1, :] * capacity + position).astype(f32))
    return found


def prepare_kernel(place, gain, layer_input, ids, scale, layer, chosen, *, experts, capacity):
    scale[...] = gain[place[0]]
    layer[...] = layer_input[...]
    first, second = slots_of(ids[...], experts, capacity)
    chosen[...] = (first + second).astype(bf16)


def dispatch_kernel(partial, scale, layer, chosen, outgoing, hidden):
    total = layer[...].astype(f32)
    for k in range(partial.shape[0]):
        total += partial[k].astype(f32)
    hidden[...] = total
    outgoing[...] = mm(chosen[...], (total * scale[...]).astype(bf16)).astype(bf16)


def fetch(pairs, sems):
    copies = [pltpu.make_async_copy(source, target, sems.at[k]) for k, (source, target) in enumerate(pairs)]
    for copy in copies:
        copy.start()
    return copies


def load_kernel(source, target, sems):
    parts = sems.shape[0]
    rows = source.shape[0] // parts
    pairs = [(source.at[pl.ds(k * rows, rows)], target.at[pl.ds(k * rows, rows)]) for k in range(parts)]
    for copy in fetch(pairs, sems):
        copy.wait()


def row_copies(place, weights, gate_up, sems, order, peers):
    depth, share = weights[0].shape
    rows = depth // peers
    copies = []
    for c, distance in enumerate(order):
        start = pl.multiple_of(lax.rem(place[0] + distance + peers, peers) * rows, rows)
        for k, weight in enumerate(weights):
            target = gate_up.at[pl.ds(c * rows, rows), pl.ds(k * share, share)]
            copies.append(pltpu.make_async_copy(weight.at[pl.ds(start, rows)], target, sems.at[c * len(weights) + k]))
    return copies


def column_copies(place, weights, down, sems, order, peers):
    share, depth = weights[0].shape
    width = depth // peers
    copies = []
    for c, distance in enumerate(order):
        start = pl.multiple_of(lax.rem(place[0] + distance + peers, peers) * width, width)
        for k, weight in enumerate(weights):
            target = down.at[pl.ds(k * share, share), pl.ds(c * width, width)]
            copies.append(pltpu.make_async_copy(weight.at[:, pl.ds(start, width)], target, sems.at[c * len(weights) + k]))
    return copies


def gate_up_sums(place, pieces, inverse, router, gate_up, order):
    peers, _, width = inverse.shape
    experts = router.shape[0]
    squares, logits = 0.0, 0.0
    for k, piece in enumerate(pieces):
        group = lax.rem(place[0] + order[k] + peers, peers)
        wide = piece.astype(f32) * inverse[group]
        squares += jnp.sum(wide * wide, axis=1, keepdims=True)
        logits += mm(piece, router[:, pl.ds(pl.multiple_of(group * width, width), width)], 1, 1)
    total = mm(jnp.concatenate(pieces, axis=1), gate_up[...])
    beside = jnp.concatenate([logits, jnp.broadcast_to(squares, (logits.shape[0], 128 - experts))], axis=1)
    return total, beside


def pair_sums_kernel(place, inverse, router, gate_up, *refs, order, rows, columns, fresh):
    weights, downs, chunks = refs[:4], refs[4:6], refs[6:10]
    befores, outs = ((), refs[10:]) if fresh else (refs[10:14], refs[14:])
    peers = inverse.shape[0]
    totals, loaded, sems = outs[:4], outs[4:-2], outs[-2:]
    copies = row_copies(place, weights, loaded[0], sems[0], rows, peers)
    if columns:
        copies += column_copies(place, downs, loaded[1], sems[1], columns, peers)
    for copy in copies:
        copy.start()
    for h in range(2):
        found = gate_up_sums(place, [ref[...] for ref in chunks[2 * h:2 * h + 2]], inverse, router, gate_up, order)
        for k in range(2):
            totals[2 * h + k][...] = found[k] if fresh else befores[2 * h + k][...] + found[k]
    for copy in copies:
        copy.wait()


def first_load_kernel(place, gain, router, others, *refs, rows, columns):
    weights, downs, (gate_up, down, inverse, router_out, others_out, *sems) = refs[:4], refs[4:6], refs[6:]
    peers = gain.shape[0]
    copies = row_copies(place, weights, gate_up, sems[0], rows, peers)
    copies += column_copies(place, downs, down, sems[1], columns, peers)
    for copy in copies:
        copy.start()
    inverse[...] = 1.0 / gain[...]
    router_out[...] = router[...]
    others_out[...] = others[...]
    for copy in copies:
        copy.wait()


def mixing_of(place, others, logits, h, capacity):
    rows, experts = logits.shape
    blocks, lanes = others.shape
    row = lax.broadcasted_iota(jnp.int32, (rows, blocks), 0)
    block = lax.broadcasted_iota(jnp.int32, (rows, blocks), 1)
    sender = 2 * (lax.div(row, capacity) + h * (rows // capacity)) + place[1]
    from_sender = mm((sender == block).astype(bf16), others[...].astype(bf16))
    row = lax.broadcasted_iota(jnp.int32, (rows, lanes), 0)
    lane = lax.broadcasted_iota(jnp.int32, (rows, lanes), 1)
    own_lane = lax.rem(place[2], lanes // capacity) * capacity + lax.rem(row, capacity)
    other = jnp.sum(jnp.where(lane == own_lane, from_sender, 0.0), axis=1, keepdims=True).astype(jnp.int32)
    expert = lax.broadcasted_iota(jnp.int32, (rows, experts), 1)
    sign = (expert == place[2]).astype(f32) - (expert == other).astype(f32)
    return jax.nn.sigmoid(jnp.sum(sign * logits, axis=1, keepdims=True))


def products(activated, down, start, count, share):
    found = []
    for c in range(start, start + count, 2):
        both = min(2, start + count - c)
        product = mm(activated, down[:, c * share:(c + both) * share])
        found += [product[:, k * share:(k + 1) * share].astype(bf16) for k in range(both)]
    return found


def far_products_kernel(
    place, inverse, router, gate_up, down, others, total, beside, *refs, order, h, far, width, capacity
):
    count = len(order)
    outs, activated = refs[count:-1], refs[-1]
    units = activated.shape[1]
    product, sums = gate_up_sums(place, [ref[...] for ref in refs[:count]], inverse, router, gate_up, order)
    sums += beside[...]
    experts = router.shape[0]
    scale = lax.rsqrt(sums[:, experts:experts + 1] / width + epsilon)
    mixing = mixing_of(place, others, sums[:, :experts] * scale, h, capacity)
    both = (total[...] + product) * scale
    gated = both[:, :units]
    active = (gated * jax.nn.sigmoid(gated) * both[:, units:] * mixing).astype(bf16)
    activated[...] = active
    for k, piece in enumerate(products(active, down, 0, far, outs[0].shape[1])):
        outs[k][...] = piece


def near_products_kernel(active_a, active_b, down, *outs, near):
    for h, active in enumerate((active_a, active_b)):
        for k, piece in enumerate(products(active[...], down, 0, near, outs[0].shape[1])):
            outs[2 * k + h][...] = piece


def combine_kernel(returned, hidden, chosen, out):
    out[...] = (hidden[...] + mm(chosen[...], returned[...], 0, 0)).astype(out.dtype)


def call(kernel, shapes, *args, **kwargs):
    return pl.pallas_call(
        kernel,
        out_shape=shapes,
        compiler_params=pltpu.CompilerParams(vmem_limit_bytes=LIMIT),
        **kwargs,
    )(*args)


def stays(x):
    return pltpu.with_memory_space_constraint(x, pltpu.HBM)


def in_vmem(x):
    return pltpu.with_memory_space_constraint(x, pltpu.VMEM)


def whole(shape):
    return pl.BlockSpec(shape, lambda *_: (0,) * len(shape))


def shards(
    layer_input, queries, keys, values, gate_input, log_decay, prior_state, attn_gain,
    out_weight, moe_gain, router, expert_ids, w_gate, w_up, w_down,
):
    struct = jax.ShapeDtypeStruct
    positions, head_lanes = queries.shape
    heads, size, _ = prior_state.shape
    chips, cores, peers = lax.axis_size("chip"), lax.axis_size("core"), lax.axis_size("tp")
    blocks = chips * cores
    width = out_weight.shape[1]
    share = layer_input.shape[1]
    experts = router.shape[1]
    capacity = 8 * positions // blocks
    slots = experts * capacity
    core, chip, tp = lax.axis_index("core"), lax.axis_index("chip"), lax.axis_index("tp")
    cx = chip * cores + core
    place = jnp.stack([tp, core, chip])
    place, cx, tp, keys = lax.optimization_barrier((place, cx, tp, keys))

    ids = stays(expert_ids.T)
    queries, keys, values, log_decay = stays(queries), stays(keys), stays(values), stays(log_decay)
    vmem = pl.BlockSpec(memory_space=pltpu.VMEM)
    smem = pl.BlockSpec(memory_space=pltpu.SMEM)
    tied = lax.optimization_barrier

    def moved(piece, step):
        return lax.ppermute(piece, "tp", [(i, (i + step) % peers) for i in range(peers)])

    def plus(*pieces):
        return sum(piece.astype(f32) for piece in pieces).astype(bf16)
    hbm = pl.BlockSpec(memory_space=pl.ANY)

    swap = [(0, 1), (1, 0)]
    weights = []
    for weight in (w_gate[0], w_up[0], w_down[0]):
        weights += [weight, lax.ppermute(weight, "core", swap)]

    rows = heads * size // blocks
    parts = call(
        functools.partial(block_state_kernel, experts=experts, capacity=capacity),
        struct((heads, size // rows, 2 * rows, size), bf16), keys, values, log_decay, ids,
    )
    parts, out_weight, prior_state = lax.optimization_barrier((parts, out_weight, prior_state))
    prior = pl.pallas_call(
        load_part_kernel,
        out_shape=pltpu.VMEM((rows, size), f32),
        in_specs=[smem, hbm],
        out_specs=vmem,
        scratch_shapes=[pltpu.SemaphoreType.DMA],
        compiler_params=pltpu.CompilerParams(vmem_limit_bytes=4 << 20),
        cost_estimate=pl.CostEstimate(flops=0, bytes_accessed=1 << 20, transcendentals=0),
    )(cx.reshape(1), stays(prior_state.reshape(heads * size, size)))
    out_weight = pl.pallas_call(
        load_kernel,
        out_shape=pltpu.VMEM((head_lanes, width), bf16),
        in_specs=[hbm],
        out_specs=vmem,
        scratch_shapes=[pltpu.SemaphoreType.DMA((4,))],
        compiler_params=pltpu.CompilerParams(vmem_limit_bytes=4 << 20),
        cost_estimate=pl.CostEstimate(flops=0, bytes_accessed=2 * head_lanes * width, transcendentals=0),
    )(stays(out_weight))
    received = lax.all_to_all(parts.reshape(blocks, 2 * rows, size), ("chip", "core"), 0, 0, tiled=True)
    inner, growth = call(
        inner_kernel,
        (struct((positions, head_lanes), f32), struct((positions, heads), f32)),
        queries, keys, values, log_decay,
    )
    gain_rows = moe_gain.reshape(peers, 1, share)
    small = pltpu.CompilerParams(vmem_limit_bytes=8 << 20)
    scale, layer, chosen = pl.pallas_call(
        functools.partial(prepare_kernel, experts=experts, capacity=capacity),
        out_shape=(pltpu.VMEM((1, share), f32), pltpu.VMEM((positions, share), bf16), pltpu.VMEM((slots, positions), bf16)),
        in_specs=[smem] + [vmem] * 3,
        out_specs=(vmem,) * 3,
        compiler_params=small,
    )(place, stays(gain_rows), stays(layer_input), stays(ids))
    befores, others = call(
        state_scan_kernel, (struct((blocks, rows, size), bf16), pltpu.HBM((blocks, size), f32)),
        received, in_vmem(prior), in_specs=[vmem] * 2,
    )
    state = lax.all_to_all(befores, ("chip", "core"), 0, 0, tiled=True).reshape(heads * size, size)

    partial = call(
        functools.partial(project_kernel, heads=heads), struct((peers, positions, share), bf16),
        queries, stays(inner), stays(growth), state, stays(gate_input), stays(attn_gain.reshape(1, head_lanes)),
        in_vmem(out_weight), in_specs=[vmem] * 7,
    )
    partial, chosen = tied((partial, chosen))
    partial = lax.all_to_all(partial, "tp", 0, 0, tiled=True)
    chosen = in_vmem(chosen)
    outgoing, hidden = pl.pallas_call(
        dispatch_kernel,
        out_shape=(struct((slots, share), bf16), pltpu.VMEM((positions, share), f32)),
        in_specs=[vmem] * 4,
        out_specs=(vmem,) * 2,
        compiler_params=small,
    )(partial, in_vmem(scale), in_vmem(layer), chosen)

    arrived = lax.all_to_all(outgoing.reshape(chips, capacity, share), "chip", 0, 0, tiled=True)
    held = chips * capacity
    half = held // 2
    arrived = arrived.reshape(held, share)
    here = (arrived[:half], arrived[half:])
    here, weights = lax.optimization_barrier((here, weights))

    order = (0, 1, -1, 2, -2, 3, -3, 4)
    parts = order[:2], order[2:4], order[4:6], order[6:]
    far, near = (4, 3, -3), (2, -2, 1, -1, 0)
    units = cores * share
    work = held * width * units
    params = pltpu.CompilerParams(vmem_limit_bytes=LIMIT)
    gain, router = stays(moe_gain.reshape(peers, 1, share)), stays(router.T)
    others = stays(others)
    sides, downs = [stays(weight) for weight in weights[:4]], [stays(weight) for weight in weights[4:]]

    def cost(flops, size):
        return pl.CostEstimate(flops=flops, bytes_accessed=size, transcendentals=0)

    def kept(kernel, shapes, flops, specs, args, scratch=(), **options):
        return pl.pallas_call(
            functools.partial(kernel, **options),
            out_shape=shapes,
            in_specs=specs + [vmem] * (len(args) - len(specs)),
            out_specs=(vmem,) * len(shapes),
            scratch_shapes=scratch,
            compiler_params=params,
            cost_estimate=cost(flops, 4 << 20),
        )(*args)

    sums = (struct((half, 2 * units), f32), struct((half, 128), f32)) * 2
    wide = pltpu.VMEM((width // 4, 2 * units), bf16)
    semaphores = [pltpu.SemaphoreType.DMA((8,)), pltpu.SemaphoreType.DMA((2 * peers,))]
    got = ({0: here[0]}, {0: here[1]})
    for distance in (1, 2, 3):
        moving = [(moved(mine[1 - distance], 1), moved(mine[distance - 1], -1)) for mine in got]
        chunks = [mine[k] for mine in got for k in parts[distance - 2]] if distance > 1 else []
        if distance == 1:
            loaded = kept(
                first_load_kernel,
                (wide, pltpu.VMEM((units, len(far) * share), bf16), pltpu.VMEM(gain.shape, f32),
                 pltpu.VMEM(router.shape, bf16), pltpu.VMEM(others.shape, f32)),
                0, [smem] + [vmem] * 3 + [hbm] * 6, [place, gain, router, others, *sides, *downs], semaphores,
                rows=parts[0], columns=far,
            )
        elif distance == 2:
            *totals, gate_up, down_near = loaded = kept(
                pair_sums_kernel, sums + (wide, pltpu.VMEM((units, len(near) * share), bf16)), work,
                [smem] + [vmem] * 3 + [hbm] * 6, [place, inverse, router, in_vmem(gate_up), *sides, *downs, *chunks], semaphores,
                order=parts[0], rows=parts[1], columns=near, fresh=True,
            )
        else:
            *totals, gate_up = loaded = kept(
                pair_sums_kernel, sums + (wide,), work,
                [smem] + [vmem] * 3 + [hbm] * 6, [place, inverse, router, in_vmem(gate_up), *sides, *downs, *chunks, *totals],
                semaphores, order=parts[1], rows=parts[2], columns=(), fresh=False,
            )
        moving[0], loaded = tied((moving[0], loaded))
        if distance == 1:
            gate_up, down_far, *small = loaded
            inverse, router, others = [in_vmem(x) for x in small]
        elif distance == 2:
            *totals, gate_up, down_near = loaded
        else:
            *totals, gate_up = loaded
        for mine, (up, down_way) in zip(got, moving):
            mine[-distance], mine[distance] = lax.optimization_barrier((up, down_way))
    got[0][4], got[1][4] = moved(got[0][-3], 1), moved(got[1][3], -1)
    *totals, gate_up_last = kept(
        pair_sums_kernel, sums + (wide,), work, [smem] + [vmem] * 3 + [hbm] * 6,
        [place, inverse, router, in_vmem(gate_up), *sides, *downs, *[mine[k] for mine in got for k in parts[2]], *totals],
        semaphores, order=parts[2], rows=parts[3], columns=(), fresh=False,
    )
    gate_up_last, down_far, down_near = in_vmem(gate_up_last), in_vmem(down_far), in_vmem(down_near)
    piece = struct((half, share), bf16)
    ready = [
        kept(
            far_products_kernel, (piece,) * len(far) + (struct((half, units), bf16),), work, [smem],
            [place, inverse, router, gate_up_last, down_far, others, *totals[2 * h:2 * h + 2], *[got[h][k] for k in parts[3]]],
            order=parts[3], h=h, far=len(far), width=width, capacity=capacity,
        )
        for h in range(2)
    ]
    (a4, a3, a3m, active_a), (b4, b3, b3m, active_b) = ready

    a_up, a_down = tied((moved(a4, 1), moved(a3m, -1)))
    b_up, b_down = tied((moved(b3, 1), moved(b4, -1)))
    a2, b2, a2m, b2m, a1, b1, a1m, b1m, a0, b0 = kept(
        near_products_kernel, (piece,) * (2 * len(near)), work, [], [active_a, active_b, down_near], near=len(near))
    a_up, a_down = tied((moved(plus(a_up, a3), 1), moved(plus(a_down, a2m), -1)))
    b_up, b_down = tied((moved(plus(b_up, b2), 1), moved(plus(b_down, b3m), -1)))
    a_up, a_down = tied((moved(plus(a_up, a2), 1), moved(plus(a_down, a1m), -1)))
    b_up, b_down = tied((moved(plus(b_up, b1), 1), moved(plus(b_down, b2m), -1)))
    a_up, b_down = moved(plus(a_up, a1), 1), moved(plus(b_down, b1m), -1)
    summed = jnp.concatenate([plus(a0, a_up, a_down), plus(b0, b_up, b_down)])
    returned = lax.all_to_all(summed.reshape(chips, capacity, share), "chip", 0, 0, tiled=True)
    return call(
        combine_kernel, struct((positions, share), bf16),
        returned.reshape(slots, share), in_vmem(hidden), chosen, in_specs=[vmem] * 3,
    )


def solution(mesh):
    cx, tp = mesh.devices.shape
    fine = Mesh(mesh.devices.reshape(cx // 2, 2, tp), ("chip", "core", "tp"))
    both = ("chip", "core")
    placed = (
        P(both, "tp"), P(both, "tp"), P(both, "tp"), P(both, "tp"), P(both, "tp"),
        P("tp", both), P("tp", None, None), P("tp"), P("tp", None), P(), P(),
        P(both, None), P(both, None, "tp"), P(both, None, "tp"), P(both, "tp", None),
    )
    return jax.shard_map(shards, mesh=fine, in_specs=placed, out_specs=P(both, "tp"), check_vma=False)
```

```python
import functools

import jax
import jax.numpy as jnp
from jax import lax
from jax.experimental import pallas as pl
from jax.experimental.pallas import tpu as pltpu
from jax.sharding import Mesh, PartitionSpec as P

epsilon = 1e-06
exact = lax.Precision.HIGHEST
bf16 = jnp.bfloat16
f32 = jnp.float32
LIMIT = 30 << 20


def mm(a, b, contract_a=1, contract_b=0, precision=None):
    return lax.dot_general(
        a, b, (((contract_a,), (contract_b,)), ((), ())),
        precision=precision, preferred_element_type=f32,
    )


def lower_triangle(n, strict=False):
    rows = lax.broadcasted_iota(jnp.int32, (n, n), 0)
    cols = lax.broadcasted_iota(jnp.int32, (n, n), 1)
    return (rows > cols) if strict else (rows >= cols)


def block_state_kernel(keys, values, log_decay, ids, out, *, experts, capacity):
    heads, positions = log_decay.shape
    size = keys.shape[1] // heads
    per_head = out.shape[1]
    rows = size // per_head
    until = mm(lower_triangle(positions).astype(f32), log_decay[...], 1, 1, exact)
    first, second = slots_of(ids[...], experts, capacity)
    chosen = [jnp.broadcast_to(ids[k:k + 1, :].astype(f32), (8, positions)).astype(bf16) for k in range(2)]
    others = mm(chosen[1], first.astype(bf16), 1, 1) + mm(chosen[0], second.astype(bf16), 1, 1)
    for h in range(heads):
        lanes = slice(h * size, (h + 1) * size)
        total = until[positions - 1:positions, h:h + 1]
        trailing = jnp.exp(total - until[:, h:h + 1])
        weighted = (keys[:, lanes].astype(f32) * trailing).astype(bf16)
        state = mm(weighted, values[:, lanes], 0, 0)
        out[h, :, :rows, :] = state.astype(bf16).reshape(per_head, rows, size)
        high = total.astype(bf16).astype(f32)
        middle = (total - high).astype(bf16).astype(f32)
        low = total - high - middle
        row = lax.broadcasted_iota(jnp.int32, (rows, size), 0)
        terms = jnp.where(row == 0, high, jnp.where(row == 1, middle, jnp.where(row == 2, low, 0.0)))
        terms = jnp.where(row == 3, others[0:1, lanes], terms)
        out[h, :, rows:, :] = jnp.broadcast_to(terms.astype(bf16), (per_head, rows, size))


def load_part_kernel(part, source, target, sem):
    rows = target.shape[0]
    copy = pltpu.make_async_copy(source.at[pl.ds(pl.multiple_of(part[0] * rows, rows), rows)], target, sem)
    copy.start()
    copy.wait()


def state_scan_kernel(received, prior, out, others):
    blocks, rows, _ = out.shape
    state = prior[...]
    for k in range(blocks):
        out[k] = state.astype(bf16)
        terms = received[k, rows:, :].astype(f32)
        total = terms[0:1] + terms[1:2] + terms[2:3]
        state = jnp.exp(total) * state + received[k, :rows, :].astype(f32)
        others[k:k + 1, :] = terms[3:4]


def inner_kernel(queries, keys, values, log_decay, out, growth):
    heads, positions = log_decay.shape
    size = queries.shape[1] // heads
    causal = lower_triangle(positions)
    until = mm(causal.astype(f32), log_decay[...], 1, 1, exact)
    until_row = mm(log_decay[...], causal.astype(f32), 1, 1, exact)
    for h in range(heads):
        lanes = slice(h * size, (h + 1) * size)
        spread = until[:, h:h + 1] - until_row[h:h + 1, :]
        weights = jnp.where(causal, jnp.exp(jnp.where(causal, spread, 0.0)), 0.0)
        scores = mm(queries[:, lanes], keys[:, lanes], 1, 1) * weights
        out[:, lanes] = mm(scores.astype(bf16), values[:, lanes])
    growth[...] = jnp.exp(until)


def project_kernel(queries, inner, growth, state, gate_input, gain, weight, out, *, heads):
    size = queries.shape[1] // heads
    normed = []
    for h in range(heads):
        lanes = slice(h * size, (h + 1) * size)
        carried = mm(queries[:, lanes], state[lanes, :])
        attended = inner[:, lanes] + growth[:, h:h + 1] * carried
        squares = jnp.mean(attended * attended, axis=1, keepdims=True)
        gating = jax.nn.sigmoid(gate_input[:, lanes].astype(f32))
        normed.append((attended * lax.rsqrt(squares + epsilon) * gain[:, lanes] * gating).astype(bf16))
    normed = jnp.concatenate(normed, axis=1)
    peers, _, width = out.shape
    for c in range(0, peers, 2):
        product = mm(normed, weight[:, c * width:(c + 2) * width])
        out[c] = product[:, :width].astype(bf16)
        out[c + 1] = product[:, width:].astype(bf16)


def slots_of(ids, experts, capacity):
    positions = ids.shape[1]
    expert = lax.broadcasted_iota(jnp.int32, (experts, positions), 0)
    choices = [(ids[k:k + 1, :] == expert).astype(f32) for k in range(2)]
    earlier = mm((choices[0] + choices[1]).astype(bf16), lower_triangle(positions, True).astype(bf16), 1, 1)
    slot = lax.broadcasted_iota(jnp.int32, (experts * capacity, positions), 0)
    found = []
    for k, choice in enumerate(choices):
        position = jnp.sum(choice * earlier, axis=0, keepdims=True).astype(jnp.int32)
        found.append((slot == ids[k:k + 1, :] * capacity + position).astype(f32))
    return found


def prepare_kernel(place, gain, layer_input, ids, scale, layer, chosen, *, experts, capacity):
    scale[...] = gain[place[0]]
    layer[...] = layer_input[...]
    first, second = slots_of(ids[...], experts, capacity)
    chosen[...] = (first + second).astype(bf16)


def dispatch_kernel(partial, scale, layer, chosen, outgoing, hidden):
    total = layer[...].astype(f32)
    for k in range(partial.shape[0]):
        total += partial[k].astype(f32)
    hidden[...] = total
    outgoing[...] = mm(chosen[...], (total * scale[...]).astype(bf16)).astype(bf16)


def fetch(pairs, sems):
    copies = [pltpu.make_async_copy(source, target, sems.at[k]) for k, (source, target) in enumerate(pairs)]
    for copy in copies:
        copy.start()
    return copies


def load_kernel(source, target, sems):
    parts = sems.shape[0]
    rows = source.shape[0] // parts
    pairs = [(source.at[pl.ds(k * rows, rows)], target.at[pl.ds(k * rows, rows)]) for k in range(parts)]
    for copy in fetch(pairs, sems):
        copy.wait()


def row_copies(place, weights, gate_up, sems, order, peers):
    depth, share = weights[0].shape
    rows = depth // peers
    copies = []
    for c, distance in enumerate(order):
        start = pl.multiple_of(lax.rem(place[0] + distance + peers, peers) * rows, rows)
        for k, weight in enumerate(weights):
            target = gate_up.at[pl.ds(c * rows, rows), pl.ds(k * share, share)]
            copies.append(pltpu.make_async_copy(weight.at[pl.ds(start, rows)], target, sems.at[c * len(weights) + k]))
    return copies


def column_copies(place, weights, down, sems, order, peers):
    share, depth = weights[0].shape
    width = depth // peers
    copies = []
    for c, distance in enumerate(order):
        start = pl.multiple_of(lax.rem(place[0] + distance + peers, peers) * width, width)
        for k, weight in enumerate(weights):
            target = down.at[pl.ds(k * share, share), pl.ds(c * width, width)]
            copies.append(pltpu.make_async_copy(weight.at[:, pl.ds(start, width)], target, sems.at[c * len(weights) + k]))
    return copies


def gate_up_sums(place, pieces, inverse, router, gate_up, order):
    peers, _, width = inverse.shape
    experts = router.shape[0]
    squares, logits = 0.0, 0.0
    for k, piece in enumerate(pieces):
        group = lax.rem(place[0] + order[k] + peers, peers)
        wide = piece.astype(f32) * inverse[group]
        squares += jnp.sum(wide * wide, axis=1, keepdims=True)
        logits += mm(piece, router[:, pl.ds(pl.multiple_of(group * width, width), width)], 1, 1)
    total = mm(jnp.concatenate(pieces, axis=1), gate_up[...])
    beside = jnp.concatenate([logits, jnp.broadcast_to(squares, (logits.shape[0], 128 - experts))], axis=1)
    return total, beside


def pair_sums_kernel(place, inverse, router, gate_up, *refs, order, rows, columns, fresh):
    weights, downs, chunks = refs[:4], refs[4:6], refs[6:10]
    befores, outs = ((), refs[10:]) if fresh else (refs[10:14], refs[14:])
    peers = inverse.shape[0]
    totals, loaded, sems = outs[:4], outs[4:-2], outs[-2:]
    copies = row_copies(place, weights, loaded[0], sems[0], rows, peers)
    if columns:
        copies += column_copies(place, downs, loaded[1], sems[1], columns, peers)
    for copy in copies:
        copy.start()
    for h in range(2):
        found = gate_up_sums(place, [ref[...] for ref in chunks[2 * h:2 * h + 2]], inverse, router, gate_up, order)
        for k in range(2):
            totals[2 * h + k][...] = found[k] if fresh else befores[2 * h + k][...] + found[k]
    for copy in copies:
        copy.wait()


def first_load_kernel(place, gain, router, others, *refs, rows, columns, capacity):
    weights, downs, (gate_up, down, inverse, router_out, *other, row_sems, column_sems) = refs[:4], refs[4:6], refs[6:]
    sems = row_sems, column_sems
    peers = gain.shape[0]
    copies = row_copies(place, weights, gate_up, sems[0], rows, peers)
    copies += column_copies(place, downs, down, sems[1], columns, peers)
    for copy in copies:
        copy.start()
    inverse[...] = 1.0 / gain[...]
    router_out[...] = router[...]
    for h in range(2):
        found = other_experts(place, others, other[h].shape[0], h, capacity)
        other[h][...] = jnp.broadcast_to(found, other[h].shape)
    for copy in copies:
        copy.wait()


def other_experts(place, others, rows, h, capacity):
    blocks, lanes = others.shape
    row = lax.broadcasted_iota(jnp.int32, (rows, blocks), 0)
    block = lax.broadcasted_iota(jnp.int32, (rows, blocks), 1)
    sender = 2 * (lax.div(row, capacity) + h * (rows // capacity)) + place[1]
    from_sender = mm((sender == block).astype(bf16), others[...].astype(bf16))
    row = lax.broadcasted_iota(jnp.int32, (rows, lanes), 0)
    lane = lax.broadcasted_iota(jnp.int32, (rows, lanes), 1)
    own_lane = lax.rem(place[2], lanes // capacity) * capacity + lax.rem(row, capacity)
    return jnp.sum(jnp.where(lane == own_lane, from_sender, 0.0), axis=1, keepdims=True)


def mixing_of(place, other, logits):
    expert = lax.broadcasted_iota(jnp.int32, logits.shape, 1)
    sign = (expert == place[2]).astype(f32) - (expert == other.astype(jnp.int32)).astype(f32)
    return jax.nn.sigmoid(jnp.sum(sign * logits, axis=1, keepdims=True))


def products(activated, down, start, count, share):
    found = []
    for c in range(start, start + count, 2):
        both = min(2, start + count - c)
        product = mm(activated, down[:, c * share:(c + both) * share])
        found += [product[:, k * share:(k + 1) * share].astype(bf16) for k in range(both)]
    return found


def far_products_kernel(
    place, inverse, router, gate_up, down, other, total, beside, *refs, order, far, width
):
    count = len(order)
    outs, activated = refs[count:-1], refs[-1]
    units = activated.shape[1]
    product, sums = gate_up_sums(place, [ref[...] for ref in refs[:count]], inverse, router, gate_up, order)
    sums += beside[...]
    experts = router.shape[0]
    scale = lax.rsqrt(sums[:, experts:experts + 1] / width + epsilon)
    mixing = mixing_of(place, other[:, 0:1], sums[:, :experts] * scale)
    both = (total[...] + product) * scale
    gated = both[:, :units]
    active = (gated * jax.nn.sigmoid(gated) * both[:, units:] * mixing).astype(bf16)
    activated[...] = active
    for k, piece in enumerate(products(active, down, 0, far, outs[0].shape[1])):
        outs[k][...] = piece


def near_products_kernel(active_a, active_b, down, *outs, near):
    half, width = outs[0].shape
    active = jnp.concatenate([active_a[...], active_b[...]], axis=0)
    for k, piece in enumerate(products(active, down, 0, near, width)):
        outs[2 * k][...] = piece[:half]
        outs[2 * k + 1][...] = piece[half:]


def combine_kernel(returned, hidden, chosen, out):
    out[...] = (hidden[...] + mm(chosen[...], returned[...], 0, 0)).astype(out.dtype)


def call(kernel, shapes, *args, **kwargs):
    return pl.pallas_call(
        kernel,
        out_shape=shapes,
        compiler_params=pltpu.CompilerParams(vmem_limit_bytes=LIMIT),
        **kwargs,
    )(*args)


def stays(x):
    return pltpu.with_memory_space_constraint(x, pltpu.HBM)


def in_vmem(x):
    return pltpu.with_memory_space_constraint(x, pltpu.VMEM)


def whole(shape):
    return pl.BlockSpec(shape, lambda *_: (0,) * len(shape))


def shards(
    layer_input, queries, keys, values, gate_input, log_decay, prior_state, attn_gain,
    out_weight, moe_gain, router, expert_ids, w_gate, w_up, w_down,
):
    struct = jax.ShapeDtypeStruct
    positions, head_lanes = queries.shape
    heads, size, _ = prior_state.shape
    chips, cores, peers = lax.axis_size("chip"), lax.axis_size("core"), lax.axis_size("tp")
    blocks = chips * cores
    width = out_weight.shape[1]
    share = layer_input.shape[1]
    experts = router.shape[1]
    capacity = 8 * positions // blocks
    slots = experts * capacity
    core, chip, tp = lax.axis_index("core"), lax.axis_index("chip"), lax.axis_index("tp")
    cx = chip * cores + core
    place = jnp.stack([tp, core, chip])
    place, cx, tp, keys = lax.optimization_barrier((place, cx, tp, keys))

    ids = stays(expert_ids.T)
    queries, keys, values, log_decay = stays(queries), stays(keys), stays(values), stays(log_decay)
    vmem = pl.BlockSpec(memory_space=pltpu.VMEM)
    smem = pl.BlockSpec(memory_space=pltpu.SMEM)
    tied = lax.optimization_barrier

    def moved(piece, step):
        return lax.ppermute(piece, "tp", [(i, (i + step) % peers) for i in range(peers)])

    def plus(*pieces):
        return sum(piece.astype(f32) for piece in pieces).astype(bf16)
    hbm = pl.BlockSpec(memory_space=pl.ANY)

    swap = [(0, 1), (1, 0)]
    weights = []
    for weight in (w_gate[0], w_up[0], w_down[0]):
        weights += [weight, lax.ppermute(weight, "core", swap)]

    rows = heads * size // blocks
    parts = call(
        functools.partial(block_state_kernel, experts=experts, capacity=capacity),
        struct((heads, size // rows, 2 * rows, size), bf16), keys, values, log_decay, ids,
    )
    parts, out_weight, prior_state = lax.optimization_barrier((parts, out_weight, prior_state))
    prior = pl.pallas_call(
        load_part_kernel,
        out_shape=pltpu.VMEM((rows, size), f32),
        in_specs=[smem, hbm],
        out_specs=vmem,
        scratch_shapes=[pltpu.SemaphoreType.DMA],
        compiler_params=pltpu.CompilerParams(vmem_limit_bytes=4 << 20),
        cost_estimate=pl.CostEstimate(flops=0, bytes_accessed=1 << 20, transcendentals=0),
    )(cx.reshape(1), stays(prior_state.reshape(heads * size, size)))
    out_weight = pl.pallas_call(
        load_kernel,
        out_shape=pltpu.VMEM((head_lanes, width), bf16),
        in_specs=[hbm],
        out_specs=vmem,
        scratch_shapes=[pltpu.SemaphoreType.DMA((4,))],
        compiler_params=pltpu.CompilerParams(vmem_limit_bytes=4 << 20),
        cost_estimate=pl.CostEstimate(flops=0, bytes_accessed=2 * head_lanes * width, transcendentals=0),
    )(stays(out_weight))
    received = lax.all_to_all(parts.reshape(blocks, 2 * rows, size), ("chip", "core"), 0, 0, tiled=True)
    inner, growth = call(
        inner_kernel,
        (struct((positions, head_lanes), f32), struct((positions, heads), f32)),
        queries, keys, values, log_decay,
    )
    gain_rows = moe_gain.reshape(peers, 1, share)
    small = pltpu.CompilerParams(vmem_limit_bytes=8 << 20)
    scale, layer, chosen = pl.pallas_call(
        functools.partial(prepare_kernel, experts=experts, capacity=capacity),
        out_shape=(pltpu.VMEM((1, share), f32), pltpu.VMEM((positions, share), bf16), pltpu.VMEM((slots, positions), bf16)),
        in_specs=[smem] + [vmem] * 3,
        out_specs=(vmem,) * 3,
        compiler_params=small,
    )(place, stays(gain_rows), stays(layer_input), stays(ids))
    befores, others = call(
        state_scan_kernel, (struct((blocks, rows, size), bf16), pltpu.HBM((blocks, size), f32)),
        received, in_vmem(prior), in_specs=[vmem] * 2,
    )
    state = lax.all_to_all(befores, ("chip", "core"), 0, 0, tiled=True).reshape(heads * size, size)

    partial = call(
        functools.partial(project_kernel, heads=heads), struct((peers, positions, share), bf16),
        queries, stays(inner), stays(growth), state, stays(gate_input), stays(attn_gain.reshape(1, head_lanes)),
        in_vmem(out_weight), in_specs=[vmem] * 7,
    )
    partial, chosen = tied((partial, chosen))
    partial = lax.all_to_all(partial, "tp", 0, 0, tiled=True)
    chosen = in_vmem(chosen)
    outgoing, hidden = pl.pallas_call(
        dispatch_kernel,
        out_shape=(struct((slots, share), bf16), pltpu.VMEM((positions, share), f32)),
        in_specs=[vmem] * 4,
        out_specs=(vmem,) * 2,
        compiler_params=small,
    )(partial, in_vmem(scale), in_vmem(layer), chosen)

    arrived = lax.all_to_all(outgoing.reshape(chips, capacity, share), "chip", 0, 0, tiled=True)
    held = chips * capacity
    half = held // 2
    arrived = arrived.reshape(held, share)
    here = (arrived[:half], arrived[half:])
    here, weights = lax.optimization_barrier((here, weights))

    order = (0, 1, -1, 2, -2, 3, -3, 4)
    parts = order[:2], order[2:4], order[4:6], order[6:]
    far, near = (4, 3, -3), (2, -2, 1, -1, 0)
    units = cores * share
    work = held * width * units
    params = pltpu.CompilerParams(vmem_limit_bytes=LIMIT)
    gain, router = stays(moe_gain.reshape(peers, 1, share)), stays(router.T)
    others = stays(others)
    sides, downs = [stays(weight) for weight in weights[:4]], [stays(weight) for weight in weights[4:]]

    def cost(flops, size):
        return pl.CostEstimate(flops=flops, bytes_accessed=size, transcendentals=0)

    def kept(kernel, shapes, flops, specs, args, scratch=(), **options):
        return pl.pallas_call(
            functools.partial(kernel, **options),
            out_shape=shapes,
            in_specs=specs + [vmem] * (len(args) - len(specs)),
            out_specs=(vmem,) * len(shapes),
            scratch_shapes=scratch,
            compiler_params=params,
            cost_estimate=cost(flops, 4 << 20),
        )(*args)

    sums = (struct((half, 2 * units), f32), struct((half, 128), f32)) * 2
    wide = pltpu.VMEM((width // 4, 2 * units), bf16)
    semaphores = [pltpu.SemaphoreType.DMA((8,)), pltpu.SemaphoreType.DMA((2 * peers,))]
    got = ({0: here[0]}, {0: here[1]})
    for distance in (1, 2, 3):
        moving = [(moved(mine[1 - distance], 1), moved(mine[distance - 1], -1)) for mine in got]
        chunks = [mine[k] for mine in got for k in parts[distance - 2]] if distance > 1 else []
        if distance == 1:
            loaded = kept(
                first_load_kernel,
                (wide, pltpu.VMEM((units, len(far) * share), bf16), pltpu.VMEM(gain.shape, f32),
                 pltpu.VMEM(router.shape, bf16)) + (pltpu.VMEM((half, 128), f32),) * 2,
                0, [smem] + [vmem] * 3 + [hbm] * 6, [place, gain, router, others, *sides, *downs], semaphores,
                rows=parts[0], columns=far, capacity=capacity,
            )
        elif distance == 2:
            *totals, gate_up, down_near = loaded = kept(
                pair_sums_kernel, sums + (wide, pltpu.VMEM((units, len(near) * share), bf16)), work,
                [smem] + [vmem] * 3 + [hbm] * 6, [place, inverse, router, in_vmem(gate_up), *sides, *downs, *chunks], semaphores,
                order=parts[0], rows=parts[1], columns=near, fresh=True,
            )
        else:
            *totals, gate_up = loaded = kept(
                pair_sums_kernel, sums + (wide,), work,
                [smem] + [vmem] * 3 + [hbm] * 6, [place, inverse, router, in_vmem(gate_up), *sides, *downs, *chunks, *totals],
                semaphores, order=parts[1], rows=parts[2], columns=(), fresh=False,
            )
        moving[0], loaded = tied((moving[0], loaded))
        if distance == 1:
            gate_up, down_far, *small = loaded
            inverse, router, *other_halves = [in_vmem(x) for x in small]
        elif distance == 2:
            *totals, gate_up, down_near = loaded
        else:
            *totals, gate_up = loaded
        for mine, (up, down_way) in zip(got, moving):
            mine[-distance], mine[distance] = lax.optimization_barrier((up, down_way))
    got[0][4], got[1][4] = moved(got[0][-3], 1), moved(got[1][3], -1)
    *totals, gate_up_last = kept(
        pair_sums_kernel, sums + (wide,), work, [smem] + [vmem] * 3 + [hbm] * 6,
        [place, inverse, router, in_vmem(gate_up), *sides, *downs, *[mine[k] for mine in got for k in parts[2]], *totals],
        semaphores, order=parts[2], rows=parts[3], columns=(), fresh=False,
    )
    gate_up_last, down_far, down_near = in_vmem(gate_up_last), in_vmem(down_far), in_vmem(down_near)
    piece = struct((half, share), bf16)
    ready = [
        kept(
            far_products_kernel, (piece,) * len(far) + (struct((half, units), bf16),), work, [smem],
            [place, inverse, router, gate_up_last, down_far, other_halves[h], *totals[2 * h:2 * h + 2], *[got[h][k] for k in parts[3]]],
            order=parts[3], far=len(far), width=width,
        )
        for h in range(2)
    ]
    (a4, a3, a3m, active_a), (b4, b3, b3m, active_b) = ready

    a_up, a_down = tied((moved(a4, 1), moved(a3m, -1)))
    b_up, b_down = tied((moved(b3, 1), moved(b4, -1)))
    a2, b2, a2m, b2m, a1, b1, a1m, b1m, a0, b0 = kept(
        near_products_kernel, (piece,) * (2 * len(near)), work, [], [active_a, active_b, down_near], near=len(near))
    a_up, a_down = tied((moved(plus(a_up, a3), 1), moved(plus(a_down, a2m), -1)))
    b_up, b_down = tied((moved(plus(b_up, b2), 1), moved(plus(b_down, b3m), -1)))
    a_up, a_down = tied((moved(plus(a_up, a2), 1), moved(plus(a_down, a1m), -1)))
    b_up, b_down = tied((moved(plus(b_up, b1), 1), moved(plus(b_down, b2m), -1)))
    a_up, b_down = moved(plus(a_up, a1), 1), moved(plus(b_down, b1m), -1)
    summed = jnp.concatenate([plus(a0, a_up, a_down), plus(b0, b_up, b_down)])
    returned = lax.all_to_all(summed.reshape(chips, capacity, share), "chip", 0, 0, tiled=True)
    return call(
        combine_kernel, struct((positions, share), bf16),
        returned.reshape(slots, share), in_vmem(hidden), chosen, in_specs=[vmem] * 3,
    )


def solution(mesh):
    cx, tp = mesh.devices.shape
    fine = Mesh(mesh.devices.reshape(cx // 2, 2, tp), ("chip", "core", "tp"))
    both = ("chip", "core")
    placed = (
        P(both, "tp"), P(both, "tp"), P(both, "tp"), P(both, "tp"), P(both, "tp"),
        P("tp", both), P("tp", None, None), P("tp"), P("tp", None), P(), P(),
        P(both, None), P(both, None, "tp"), P(both, None, "tp"), P(both, "tp", None),
    )
    return jax.shard_map(shards, mesh=fine, in_specs=placed, out_specs=P(both, "tp"), check_vma=False)
```
